256 devices in a mesh: dp: 128 (over z, x_hi, y, core), mp: 2 (over x_lo).
Axes of the slice: x: 4 (x_hi: 2, x_lo: 2; x = x_hi * 2 + x_lo), y: 4, z: 8, core: 2. Of those that a mesh axis runs over, the one named last changes fastest.
Arguments:
- image_tokens: bfloat16 [2048, 64, 1536], P('dp'), may hold values from -24 to 24
- text_tokens: bfloat16 [2048, 32, 1536], P('dp'), may hold values from -24 to 24
- image_weight: bfloat16 [1536, 1536], P(None, 'mp'), may hold values from -0.15625 to 0.15625
- text_weight: bfloat16 [1536, 1536], P(None, 'mp'), may hold values from -0.15625 to 0.15625
- logit_scale: float32 [1], replicated, may hold values from 6 to 14
- logit_bias: float32 [1], replicated, may hold values from -8 to -5
- loss_scale: float32 [1], replicated, may hold values from 256 to 4096
- valid_count: int32 [128], P('dp'), may hold values from 3 to 16, as said below
Outputs:
- loss: float32 [], replicated
- image_weight_grad: float32 [1536, 1536], P('dp', 'mp')
- text_weight_grad: float32 [1536, 1536], P('dp', 'mp')
The draws below stay inside these ranges and needn't reach their ends.
Inputs may be any that keep to these rules, and one draw needn't show every extreme that they name: `valid_count`: at least one index of dp has all 16 pairs valid.
All inputs are finite; a program needn't handle non-finite values.
Results may differ from the reference program's by a relative error of at most 0.0014.
Values may be sent and summed in bfloat16 or wider, within the bound.
A program may use at most 128 MiB of HBM per device.

```python
import math
import jax
import jax.numpy as jnp
from jax import lax

D = 1536
SAMP_DEV = 16
IMG_TOK = 64
TXT_TOK = 32
SAMPLES = 2048
N_DP = 128


def draw_valid_count(key, part):
    key = jax.random.fold_in(key, 7)
    positions_dp = jnp.arange(N_DP, dtype=jnp.int32)
    baseline = (SAMP_DEV + 2 * SAMP_DEV * positions_dp // max(N_DP - 1, 1)) // 3
    jitter_draw = jax.random.randint(key, (N_DP,), -(SAMP_DEV // 8), SAMP_DEV // 8 + 1, dtype=jnp.int32)
    counted = jnp.clip(baseline + jitter_draw, 1, SAMP_DEV)
    return jnp.where(positions_dp == N_DP - 1, SAMP_DEV, counted).astype(jnp.int32)


def strengthened(array, key, source, target, parts, factor):
    owner, partner = [(jnp.arange(array.shape[dim]) // (array.shape[dim] // parts)).reshape([-1 if axis == dim else 1 for axis in range(array.ndim)]) for dim in (source, target)]
    chosen = jax.random.permutation(key, parts)[partner]
    strong = (owner == chosen) | (owner == (partner + parts // 2) % parts)
    return jnp.where(strong, factor * array, array)


def block_scale(rng, dims, cuts, least, high):
    def one(dim, blocks):
        steps = jax.random.uniform(jax.random.fold_in(jax.random.fold_in(rng, 6), dim), (blocks,), jnp.float32, least / len(cuts), high / len(cuts))
        return jnp.repeat(jnp.exp(steps), dims[dim] // blocks).reshape((-1,) + (1,) * (len(dims) - dim - 1))

    loudness = one(*cuts[0])
    for cut in cuts[1:]:
        loudness = loudness * one(*cut)
    return loudness


def scatter_about(stream_key, extent, scale, bound, shards=(), kind=jnp.bfloat16):
    gain = block_scale(stream_key, extent, shards, -0.22, 0.18) if shards else 1.0
    drawn = jax.random.normal(stream_key, extent, jnp.float32) * scale * gain
    return jnp.minimum(jnp.maximum(drawn, -bound), bound).astype(kind)


def bell_draw_with(stream_key, extent, width, reach, shards, heavy, held_as=jnp.bfloat16):
    array = width * jax.random.normal(stream_key, extent, jnp.float32)
    if shards:
        array = array * block_scale(stream_key, extent, shards, -0.22, 0.18)
    return jnp.clip(strengthened(array, jax.random.fold_in(stream_key, 3), *heavy), -reach, reach).astype(held_as)


def setup_inputs(seed: int = 0) -> dict:
    key_of = jax.random.split(jax.random.key(seed), 9)
    image_tokens = bell_draw_with(key_of[0], (SAMPLES, IMG_TOK, D), 1.0, 24.0, ((0, 128),), (0, 2, 128, 5.5))
    text_tokens = bell_draw_with(key_of[1], (SAMPLES, TXT_TOK, D), 1.0, 24.0, ((0, 128),), (0, 2, 128, 5.5))
    image_weight = scatter_about(key_of[2], (D, D), D ** -0.5, 0.15625, ((1, 2),))
    text_weight = scatter_about(key_of[3], (D, D), D ** -0.5, 0.15625, ((1, 2),))
    logit_scale = jnp.clip(jax.random.uniform(key_of[4], (1,), jnp.float32, 6.0, 14.0), 6.0, 14.0)
    logit_bias = jnp.clip(jax.random.uniform(key_of[5], (1,), jnp.float32, -8.0, -5.0), -8.0, -5.0)
    loss_scale = jnp.clip(jnp.exp(jax.random.uniform(key_of[6], (1,), jnp.float32, math.log(256.0), math.log(4096.0))), 256.0, 4096.0)
    valid_count = draw_valid_count(jax.random.fold_in(key_of[8], 71), 0)
    return dict(image_tokens=image_tokens, text_tokens=text_tokens, image_weight=image_weight, text_weight=text_weight, logit_scale=logit_scale, logit_bias=logit_bias, loss_scale=loss_scale, valid_count=valid_count)


def gelu_slope(values):
    return jax.jvp(lambda inner: jax.nn.gelu(inner, approximate=True), (values,), (jnp.ones_like(values),))[1]

def tower_pooled(tokens, weight):
    blocks = tokens.reshape(N_DP, SAMP_DEV, tokens.shape[1], D)

    def one_block(block):
        flat_tokens = block.reshape(-1, D)
        preact = jnp.dot(flat_tokens, weight, preferred_element_type=jnp.float32)
        hidden = flat_tokens.astype(jnp.float32) + jax.nn.gelu(preact, approximate=True)
        return lax.optimization_barrier(jnp.mean(hidden.reshape(SAMP_DEV, block.shape[1], D), axis=1))
    return lax.map(one_block, blocks).reshape(-1, D)

def tower_weight_grad(tokens, weight, grad_pooled):
    token_count = tokens.shape[1]
    blocks = tokens.reshape(N_DP, SAMP_DEV, token_count, D)
    grads = grad_pooled.reshape(N_DP, SAMP_DEV, D)

    def one_block(total_grad, paired):
        block, grad_block = paired
        flat_tokens = block.reshape(-1, D)
        preact = jnp.dot(flat_tokens, weight, preferred_element_type=jnp.float32)
        slope = gelu_slope(preact.reshape(SAMP_DEV, token_count, D))
        grad_preact = (grad_block[:, None, :] / token_count * slope).astype(jnp.bfloat16).reshape(-1, D)
        term = lax.dot_general(flat_tokens, grad_preact, (((0,), (0,)), ((), ())), preferred_element_type=jnp.float32)
        return (total_grad + term, None)
    result, _ = lax.scan(one_block, jnp.zeros((D, D), jnp.float32), (blocks, grads))
    return result

def unitize(pooled):
    norm = jnp.sqrt(lax.optimization_barrier(jnp.sum(pooled * pooled, axis=1)) + 1e-06)
    return (pooled / norm[:, None], norm)

def reference(image_tokens, text_tokens, image_weight, text_weight, logit_scale, logit_bias, loss_scale, valid_count):
    logit_mult = logit_scale[0]
    offset_term = logit_bias[0]
    image_unit, image_norm = unitize(tower_pooled(image_tokens, image_weight))
    text_unit, text_norm = unitize(tower_pooled(text_tokens, text_weight))
    image_bf = image_unit.astype(jnp.bfloat16)
    text_bf = text_unit.astype(jnp.bfloat16)
    indices = jnp.arange(SAMP_DEV * N_DP, dtype=jnp.int32)
    usable = indices % SAMP_DEV < valid_count[indices // SAMP_DEV]
    total_count = jnp.sum(valid_count).astype(jnp.float32)
    logits = logit_mult * jnp.dot(image_bf, text_bf.T, preferred_element_type=jnp.float32) + offset_term
    pair_sign = jnp.where(indices[:, None] == indices[None, :], 1.0, -1.0).astype(jnp.float32)
    weighting = usable[:, None] & usable[None, :]
    margin = -pair_sign * logits
    loss = jnp.sum(jnp.where(weighting, jax.nn.softplus(margin), 0.0)) / total_count
    grad_coeff = loss_scale[0] / total_count
    dlogit = (jnp.where(weighting, -pair_sign * jax.nn.sigmoid(margin), 0.0) * grad_coeff).astype(jnp.bfloat16)
    image_grad = logit_mult * jnp.dot(dlogit, text_bf, preferred_element_type=jnp.float32)
    text_grad = logit_mult * jnp.dot(dlogit.T, image_bf, preferred_element_type=jnp.float32)
    image_gp = (image_grad - image_unit * lax.optimization_barrier(jnp.sum(image_unit * image_grad, axis=1))[:, None]) / image_norm[:, None]
    text_gp = (text_grad - text_unit * lax.optimization_barrier(jnp.sum(text_unit * text_grad, axis=1))[:, None]) / text_norm[:, None]
    image_weight_grad = tower_weight_grad(image_tokens, image_weight, image_gp)
    text_weight_grad = tower_weight_grad(text_tokens, text_weight, text_gp)
    return (loss, image_weight_grad, text_weight_grad)
```

```python
import jax
import jax.numpy as jnp
from jax import lax
from jax.experimental import pallas as pl
from jax.experimental.pallas import tpu as pltpu
from jax.sharding import PartitionSpec as P

MESH = pl.DeviceIdType.MESH
F32 = jnp.float32
BF16 = jnp.bfloat16
NZ, NY, NX, NC = 8, 4, 4, 2
D = 1536
H = 768
EXT = 128
ZROWS = D // NZ
OWN = 24


def place():
    dp = lax.axis_index("dp")
    lo = lax.axis_index("mp")
    c = lax.rem(dp, 2)
    y = lax.rem(lax.div(dp, 2), 4)
    xh = lax.rem(lax.div(dp, 8), 2)
    z = lax.div(dp, 16)
    return z, y, xh * 2 + lo, c


def device_at(z, y, x, c):
    return (((z * 2 + lax.div(x, 2)) * 4 + y) * 2 + c, lax.rem(x, 2))


def slot_of(x, c):
    return (lax.div(x, 2) * 2 + c) * 2 + lax.rem(x, 2)


def send_to(src, dst, send_sem, recv_sem, device):
    return pltpu.make_async_remote_copy(
        src_ref=src,
        dst_ref=dst,
        send_sem=send_sem,
        recv_sem=recv_sem,
        device_id=device,
        device_id_type=MESH,
    )


def greet(devices):
    barrier = pltpu.get_barrier_semaphore()
    for device in devices:
        pl.semaphore_signal(barrier, inc=1, device_id=device, device_id_type=MESH)
    pl.semaphore_wait(barrier, len(devices))


GROUP = [(dx, dc) for dx in range(NX) for dc in range(NC) if (dx, dc) != (0, 0)]


def dot_t(a, b):
    return lax.dot_general(a, b, (((1,), (1,)), ((), ())), preferred_element_type=F32)


def pair_kernel(
    pooled_ref,
    count_ref,
    scale_ref,
    bias_ref,
    loss_scale_ref,
    grad_ref,
    loss_ref,
    other,
    counts,
    plane,
    group,
    parts,
    landed,
    unit_own,
    s_other,
    r_other,
    s_count,
    r_count,
    s_group,
    r_group,
    s_y,
    r_y,
    s_up,
    r_up,
    s_down,
    r_down,
    s_part,
    r_part,
):
    z, y, x, c = place()
    lo = lax.rem(x, 2)
    me = slot_of(x, c)
    zu, zd = lax.rem(z + 1, NZ), lax.rem(z + NZ - 1, NZ)
    up, down = device_at(zu, y, x, c), device_at(zd, y, x, c)
    members = {(dx, dc): device_at(z, y, lax.rem(x + dx, NX), lax.rem(c + dc, NC)) for dx, dc in GROUP}
    sources = {(dx, dc): (lax.rem(x + NX - dx, NX), lax.rem(c + dc, NC)) for dx, dc in GROUP}
    y_peers = [device_at(z, lax.rem(y + j, NY), x, c) for j in range(1, NY)]
    partner = device_at(z, y, lax.div(x, 2) * 2 + 1 - lo, c)
    greet([members[key] for key in GROUP] + y_peers + [up, down])

    half_copy = send_to(pooled_ref, other, s_other, r_other, partner)
    half_copy.start()
    counts[me] = count_ref[...]
    count_copies = []
    for n, key in enumerate(GROUP):
        copy = send_to(counts.at[me], counts.at[me], s_count.at[n], r_count.at[n], members[key])
        copy.start()
        count_copies.append(copy)
    mine = pooled_ref[...]
    own_sq = jnp.sum(mine * mine, axis=1, keepdims=True)
    half_copy.wait_recv()
    theirs = other[...]
    norm = jnp.sqrt(own_sq + jnp.sum(theirs * theirs, axis=1, keepdims=True) + 1e-6)
    unit_mine = mine / norm
    unit_theirs = theirs / norm
    unit_own[...] = unit_mine
    first = lo == 0
    low = jnp.where(first, unit_mine, unit_theirs)
    high = jnp.where(first, unit_theirs, unit_mine)
    for n, key in enumerate(GROUP):
        sx, sc = sources[key]
        slot = slot_of(sx, sc)
        send_to(counts.at[slot], counts.at[slot], s_count.at[n], r_count.at[n], members[key]).wait_recv()
    row_total = jnp.sum(counts[...], axis=0)[0:1, :] * 0.5
    own_count = count_ref[0:1, :]
    own_low = jnp.where(first, low[0:16], low[16:32])
    own_high = jnp.where(first, high[0:16], high[16:32])
    sample = lax.rem(lax.broadcasted_iota(jnp.int32, (16, EXT), 0), 8) + 8 * lo
    lane = lax.broadcasted_iota(jnp.int32, (16, EXT), 1)
    usable = jnp.where(sample.astype(F32) < own_count, 1.0, 0.0)
    extra = jnp.where(lane < EXT // 2, usable, jnp.broadcast_to(row_total, (16, EXT)))
    block = jnp.concatenate([own_low.astype(BF16), own_high.astype(BF16), extra.astype(BF16)], axis=1)
    plane[z, y] = block
    group[me] = block

    y_copies = []
    for j in range(1, NY):
        copy = send_to(plane.at[z, y], plane.at[z, y], s_y.at[j - 1], r_y.at[j - 1], y_peers[j - 1])
        copy.start()
        y_copies.append(copy)
    z_copies = []

    def pass_up(step, j, zs, ys):
        copy = send_to(plane.at[zs, ys], plane.at[zs, ys], s_up.at[step, j], r_up.at[step, j], up)
        copy.start()
        z_copies.append(copy)

    def pass_down(step, j, zs, ys):
        copy = send_to(plane.at[zs, ys], plane.at[zs, ys], s_down.at[step, j], r_down.at[step, j], down)
        copy.start()
        z_copies.append(copy)

    pass_up(0, 0, z, y)
    pass_down(0, 0, z, y)
    group_copies = []
    for n, key in enumerate(GROUP):
        copy = send_to(group.at[me], group.at[me], s_group.at[n], r_group.at[n], members[key])
        copy.start()
        group_copies.append(copy)
    for j in range(1, NY):
        ys = lax.rem(y + NY - j, NY)
        send_to(plane.at[z, ys], plane.at[z, ys], s_y.at[j - 1], r_y.at[j - 1], up).wait_recv()
        pass_up(0, j, z, ys)
        pass_down(0, j, z, ys)
    for step in range(4):
        for j in range(NY):
            ys = lax.rem(y + NY - j, NY)
            if step < 3 or j < 2:
                zs = lax.rem(z + NZ - step - 1, NZ)
                send_to(plane.at[zs, ys], plane.at[zs, ys], s_up.at[step, j], r_up.at[step, j], up).wait_recv()
                if step < 2 or (step == 2 and j < 2):
                    pass_up(step + 1, j, zs, ys)
            if step < 3 or j >= 2:
                zs = lax.rem(z + step + 1, NZ)
                send_to(plane.at[zs, ys], plane.at[zs, ys], s_down.at[step, j], r_down.at[step, j], down).wait_recv()
                if step < 2 or (step == 2 and j >= 2):
                    pass_down(step + 1, j, zs, ys)
    for n, key in enumerate(GROUP):
        sx, sc = sources[key]
        slot = slot_of(sx, sc)
        send_to(group.at[slot], group.at[slot], s_group.at[n], r_group.at[n], members[key]).wait_recv()

    rows = group[...].reshape(8 * 16, D + EXT)
    cols = plane[...].reshape(32 * 16, D + EXT)
    row_main, col_main = rows[:, :D], cols[:, :D]
    logit_mult = scale_ref[0]
    logits = logit_mult * dot_t(row_main, col_main) + bias_ref[0]
    pick = lax.broadcasted_iota(jnp.int32, (16, EXT), 0) * (EXT // 2)
    pick = jnp.where(pick == lax.broadcasted_iota(jnp.int32, (16, EXT), 1), 1.0, 0.0).astype(BF16)
    col_extra = dot_t(pick, cols[:, D:])
    total = jnp.sum(col_extra[1:2, :]) * (1.0 / 16.0)
    col_usable = col_extra[0:1, :]
    row_usable = rows[:, D : D + 1].astype(F32)
    shape = (8 * 16, 32 * 16)
    r = lax.broadcasted_iota(jnp.int32, shape, 0)
    q = lax.broadcasted_iota(jnp.int32, shape, 1)
    r_text = lax.rem(lax.div(r, 8), 2)
    q_text = lax.rem(lax.div(q, 8), 2)
    same = (lax.div(r, 16) == me) & (lax.div(q, 16) == z * NY + y) & (lax.rem(r, 8) == lax.rem(q, 8))
    used = (row_usable * col_usable > 0.5) & (r_text != q_text)
    sign = jnp.where(same, 1.0, -1.0)
    margin = -sign * logits
    soft = jnp.maximum(margin, 0.0) + jnp.log1p(jnp.exp(-jnp.abs(margin)))
    loss = jnp.sum(jnp.where(used & (r_text == 0), soft, 0.0), axis=1, keepdims=True)
    loss_ref[...] = jnp.broadcast_to(jnp.sum(loss, axis=0, keepdims=True) / total, (8, 128))
    coeff = loss_scale_ref[0] / total
    dlogit = (jnp.where(used, -sign * jax.nn.sigmoid(margin), 0.0) * coeff).astype(BF16)
    grad = logit_mult * jnp.dot(dlogit, col_main, preferred_element_type=F32)
    radial = jnp.sum(row_main.astype(F32) * grad, axis=1, keepdims=True)
    radial = jnp.broadcast_to(radial, (8 * 16, EXT))
    for pair in range(4):
        for half in range(2):
            band = slice(pair * 32, pair * 32 + 32)
            parts[pair, half, :, :H] = grad[band, half * H : half * H + H]
            parts[pair, half, :, H:] = radial[band]

    part_copies = []
    for n, key in enumerate(GROUP):
        dx, dc = key
        tx, tc = lax.rem(x + dx, NX), lax.rem(c + dc, NC)
        copy = send_to(
            parts.at[lax.div(tx, 2) * 2 + tc, lax.rem(tx, 2)],
            landed.at[me],
            s_part.at[n],
            r_part.at[n],
            members[key],
        )
        copy.start()
        part_copies.append(copy)
    total_grad = parts[lax.div(x, 2) * 2 + c, lo]
    for n, key in enumerate(GROUP):
        sx, sc = sources[key]
        slot = slot_of(sx, sc)
        send_to(landed.at[slot], landed.at[slot], s_part.at[n], r_part.at[n], members[key]).wait_recv()
        total_grad = total_grad + landed[slot]
    grad_ref[...] = (total_grad[:, :H] - unit_own[...] * total_grad[:, H : H + 1]) / norm
    for copy in [half_copy] + count_copies + y_copies + z_copies + group_copies + part_copies:
        copy.wait_send()


def pair_gradients(pooled, count, logit_scale, logit_bias, loss_scale):
    dma = pltpu.SemaphoreType.DMA
    vmem = pl.BlockSpec(memory_space=pltpu.VMEM)
    smem = pl.BlockSpec(memory_space=pltpu.SMEM)
    return pl.pallas_call(
        pair_kernel,
        out_shape=(jax.ShapeDtypeStruct((32, H), F32), jax.ShapeDtypeStruct((8, 128), F32)),
        in_specs=[vmem, vmem, smem, smem, smem],
        out_specs=(vmem, vmem),
        scratch_shapes=[
            pltpu.VMEM((32, H), F32),
            pltpu.VMEM((8, 8, 128), F32),
            pltpu.VMEM((NZ, NY, 16, D + EXT), BF16),
            pltpu.VMEM((8, 16, D + EXT), BF16),
            pltpu.VMEM((4, 2, 32, H + EXT), F32),
            pltpu.VMEM((8, 32, H + EXT), F32),
            pltpu.VMEM((32, H), F32),
            dma, dma,
            dma((7,)), dma((7,)),
            dma((7,)), dma((7,)),
            dma((3,)), dma((3,)),
            dma((4, 4)), dma((4, 4)),
            dma((4, 4)), dma((4, 4)),
            dma((7,)), dma((7,)),
        ],
        compiler_params=pltpu.CompilerParams(
            collective_id=1, has_side_effects=True, vmem_limit_bytes=48 * 1024 * 1024
        ),
    )(pooled, count, logit_scale, logit_bias, loss_scale)


YX = [(dxh, j) for dxh in range(2) for j in range(NY) if (dxh, j) != (0, 0)]


def reduce_kernel(
    image_ref,
    text_ref,
    loss_ref,
    out_ref,
    loss_out_ref,
    terms,
    sibling,
    up_out,
    up_in,
    down_out,
    down_in,
    owned,
    near_in,
    final,
    loss_group,
    loss_y,
    loss_z,
    loss_stage,
    s_load,
    s_sib,
    r_sib,
    s_up,
    r_up,
    s_down,
    r_down,
    s_near,
    r_near,
    s_final,
    r_final,
    s_lg,
    r_lg,
    s_ly,
    r_ly,
    s_lz,
    r_lz,
):
    z, y, x, c = place()
    xh, lo = lax.div(x, 2), lax.rem(x, 2)
    up = device_at(lax.rem(z + 1, NZ), y, x, c)
    down = device_at(lax.rem(z + NZ - 1, NZ), y, x, c)
    twin = device_at(z, y, x, 1 - c)
    members = {(dx, dc): device_at(z, y, lax.rem(x + dx, NX), lax.rem(c + dc, NC)) for dx, dc in GROUP}
    near = {
        (dxh, j): device_at(z, lax.rem(y + j, NY), lax.rem(xh + dxh, 2) * 2 + lo, c) for dxh, j in YX
    }
    z_peers = [device_at(lax.rem(z + k, NZ), y, x, c) for k in range(1, NZ)]

    order = [4, 3, 5, 2, 6, 1, 7, 0]
    loads = []
    for n, k in enumerate(order):
        t = lax.rem(z + k, NZ)
        pair = [
            pltpu.make_async_copy(ref.at[t], terms.at[i, t], s_load.at[i, n])
            for i, ref in enumerate((image_ref, text_ref))
        ]
        for load in pair:
            load.start()
        loads.append(pair)
    loss_group[0] = loss_ref[...]
    greet(
        [members[key] for key in GROUP]
        + [near[key] for key in YX if key != (1, 0)]
        + z_peers
    )
    copies = []

    def start(copy):
        copy.start()
        copies.append(copy)

    for n, key in enumerate(GROUP):
        start(send_to(loss_group.at[0], loss_group.at[n + 1], s_lg.at[n], r_lg.at[n], members[key]))
    for n, k in enumerate(order):
        t = lax.rem(z + k, NZ)
        for load in loads[n]:
            load.wait()
        start(send_to(terms.at[1 - c, t], sibling.at[t], s_sib.at[n], r_sib.at[n], twin))

    def chunk(n):
        t = lax.rem(z + order[n], NZ)
        send_to(sibling.at[t], sibling.at[t], s_sib.at[n], r_sib.at[n], twin).wait_recv()
        return t

    half = H // 2
    t = chunk(0)
    up_out[0, :, :half] = terms[c, t, :, :half] + sibling[t, :, :half]
    start(send_to(up_out.at[0, :, pl.ds(0, half)], up_in.at[0, :, pl.ds(0, half)], s_up.at[0], r_up.at[0], up))
    down_out[0, :, half:] = terms[c, t, :, half:] + sibling[t, :, half:]
    start(send_to(down_out.at[0, :, pl.ds(half, half)], down_in.at[0, :, pl.ds(half, half)], s_down.at[0], r_down.at[0], down))
    for n, key in enumerate(GROUP):
        send_to(loss_group.at[0], loss_group.at[n + 1], s_lg.at[n], r_lg.at[n], members[key]).wait_recv()
    loss_y[0] = jnp.sum(loss_group[...], axis=0)
    for j in range(1, NY):
        start(send_to(loss_y.at[0], loss_y.at[j], s_ly.at[j - 1], r_ly.at[j - 1], near[(0, j)]))
    for step in range(1, 4):
        t = chunk(2 * step - 1)
        up_out[step] = terms[c, t] + sibling[t]
        if step == 1:
            send_to(up_out.at[0, :, pl.ds(0, half)], up_in.at[0, :, pl.ds(0, half)], s_up.at[0], r_up.at[0], up).wait_recv()
            up_out[step, :, :half] += up_in[0, :, :half]
        else:
            send_to(up_out.at[step - 1], up_in.at[step - 1], s_up.at[step - 1], r_up.at[step - 1], up).wait_recv()
            up_out[step] += up_in[step - 1]
        start(send_to(up_out.at[step], up_in.at[step], s_up.at[step], r_up.at[step], up))
        t = chunk(2 * step)
        down_out[step] = terms[c, t] + sibling[t]
        if step == 1:
            send_to(down_out.at[0, :, pl.ds(half, half)], down_in.at[0, :, pl.ds(half, half)], s_down.at[0], r_down.at[0], down).wait_recv()
            down_out[step, :, half:] += down_in[0, :, half:]
        else:
            send_to(down_out.at[step - 1], down_in.at[step - 1], s_down.at[step - 1], r_down.at[step - 1], down).wait_recv()
            down_out[step] += down_in[step - 1]
        start(send_to(down_out.at[step], down_in.at[step], s_down.at[step], r_down.at[step], down))
        if step == 1:
            for j in range(1, NY):
                send_to(loss_y.at[0], loss_y.at[j], s_ly.at[j - 1], r_ly.at[j - 1], near[(0, j)]).wait_recv()
            loss_z[0] = jnp.sum(loss_y[...], axis=0)
            for k in range(1, NZ):
                start(send_to(loss_z.at[0], loss_z.at[k], s_lz.at[k - 1], r_lz.at[k - 1], z_peers[k - 1]))
    t = chunk(7)
    send_to(up_out.at[3], up_in.at[3], s_up.at[3], r_up.at[3], up).wait_recv()
    send_to(down_out.at[3], down_in.at[3], s_down.at[3], r_down.at[3], down).wait_recv()
    total = terms[c, t] + sibling[t] + up_in[3] + down_in[3]
    owned[...] = total.reshape(2, NY, OWN, H)
    for n, (dxh, j) in enumerate(YX):
        start(
            send_to(
                owned.at[lax.rem(xh + dxh, 2), lax.rem(y + j, NY)],
                near_in.at[n],
                s_near.at[n],
                r_near.at[n],
                near[(dxh, j)],
            )
        )
    result = owned[xh, y]
    for n, key in enumerate(YX):
        send_to(near_in.at[n], near_in.at[n], s_near.at[n], r_near.at[n], near[key]).wait_recv()
        result = result + near_in[n]
    final[c] = result
    swap = send_to(final.at[c], final.at[c], s_final, r_final, twin)
    swap.start()
    for k in range(1, NZ):
        send_to(loss_z.at[0], loss_z.at[k], s_lz.at[k - 1], r_lz.at[k - 1], z_peers[k - 1]).wait_recv()
    loss_out_ref[...] = jnp.sum(loss_z[...], axis=0)
    send_to(final.at[1 - c], final.at[1 - c], s_final, r_final, twin).wait_recv()
    out_ref[...] = final[...]
    swap.wait_send()
    for copy in copies:
        copy.wait_send()


def reduce_terms(image_terms, text_terms, loss):
    dma = pltpu.SemaphoreType.DMA
    vmem = pl.BlockSpec(memory_space=pltpu.VMEM)
    anywhere = pl.BlockSpec(memory_space=pl.ANY)
    ring = pltpu.VMEM((4, ZROWS, H), F32)
    tile = (8, 128)
    return pl.pallas_call(
        reduce_kernel,
        out_shape=(jax.ShapeDtypeStruct((2, OWN, H), F32), jax.ShapeDtypeStruct((8, 128), F32)),
        in_specs=[anywhere, anywhere, vmem],
        out_specs=(vmem, vmem),
        scratch_shapes=[
            pltpu.VMEM((2, NZ, ZROWS, H), F32),
            pltpu.VMEM((NZ, ZROWS, H), F32),
            ring, ring, ring, ring,
            pltpu.VMEM((2, NY, OWN, H), F32),
            pltpu.VMEM((7, OWN, H), F32),
            pltpu.VMEM((2, OWN, H), F32),
            pltpu.VMEM((8,) + tile, F32),
            pltpu.VMEM((NY,) + tile, F32),
            pltpu.VMEM((NZ,) + tile, F32),
            pltpu.VMEM(tile, F32),
            dma((2, 8)),
            dma((8,)), dma((8,)),
            dma((4,)), dma((4,)),
            dma((4,)), dma((4,)),
            dma((7,)), dma((7,)),
            dma, dma,
            dma((7,)), dma((7,)),
            dma((3,)), dma((3,)),
            dma((7,)), dma((7,)),
        ],
        compiler_params=pltpu.CompilerParams(
            collective_id=2, has_side_effects=True, vmem_limit_bytes=48 * 1024 * 1024
        ),
    )(image_terms.reshape(NZ, ZROWS, H), text_terms.reshape(NZ, ZROWS, H), loss)


def gelu_slope(values):
    return jax.jvp(
        lambda inner: jax.nn.gelu(inner, approximate=True), (values,), (jnp.ones_like(values),)
    )[1]


def tower_block(tokens, weight, offset):
    flat_tokens = tokens.reshape(-1, tokens.shape[2])
    preact = jnp.dot(flat_tokens, weight, preferred_element_type=F32)
    residual = lax.dynamic_slice_in_dim(flat_tokens, offset, weight.shape[1], 1).astype(F32)
    hidden = residual + jax.nn.gelu(preact, approximate=True)
    pooled = jnp.mean(hidden.reshape(tokens.shape[0], tokens.shape[1], -1), axis=1)
    return (flat_tokens, preact, pooled)


def contract_rows(left_rows, right_rows):
    return lax.dot_general(left_rows, right_rows, (((0,), (0,)), ((), ())), preferred_element_type=F32)


def body(
    image_tokens,
    text_tokens,
    image_weight,
    text_weight,
    logit_scale,
    logit_bias,
    loss_scale,
    valid_count,
):
    core = lax.rem(lax.axis_index("dp"), 2)
    half_start = lax.axis_index("mp") * H
    image_flat, image_preact, image_pooled = tower_block(image_tokens, image_weight, half_start)
    text_flat, text_preact, text_pooled = tower_block(text_tokens, text_weight, half_start)
    pooled = jnp.concatenate([image_pooled[:8], text_pooled[:8], image_pooled[8:], text_pooled[8:]], axis=0)
    count = jnp.broadcast_to(valid_count.astype(F32)[:, None], (8, 128))
    grad_pooled, loss_part = pair_gradients(pooled, count, logit_scale, logit_bias, loss_scale)
    grads = grad_pooled.reshape(2, 2, 8, H)
    image_gp = grads[:, 0].reshape(16, H)
    text_gp = grads[:, 1].reshape(16, H)

    def terms(gp, flat, preact, tokens):
        samples, count = tokens.shape[:2]
        slope = gelu_slope(preact.reshape(samples, count, H))
        gpre = (gp[:, None, :] / count * slope).astype(BF16).reshape(-1, H)
        return contract_rows(flat, gpre)

    image_terms = terms(image_gp, image_flat, image_preact, image_tokens)
    text_terms = terms(text_gp, text_flat, text_preact, text_tokens)
    grads_out, loss = reduce_terms(image_terms, text_terms, loss_part)
    mine = lax.dynamic_slice_in_dim(grads_out, core * 12, 12, 1)
    return (loss[0, 0], mine[0], mine[1])


def solution(mesh):
    placed = (
        P("dp", None, None),
        P("dp", None, None),
        P(None, "mp"),
        P(None, "mp"),
        P(),
        P(),
        P(),
        P("dp"),
    )
    return jax.shard_map(
        body,
        mesh=mesh,
        in_specs=placed,
        out_specs=(P(), P("dp", "mp"), P("dp", "mp")),
        check_vma=False,
    )
```

```python
import jax
import jax.numpy as jnp
from jax import lax
from jax.experimental import pallas as pl
from jax.experimental.pallas import tpu as pltpu
from jax.sharding import PartitionSpec as P

MESH = pl.DeviceIdType.MESH
F32 = jnp.float32
BF16 = jnp.bfloat16
NZ, NY, NX, NC = 8, 4, 4, 2
D = 1536
H = 768
EXT = 128
ZROWS = D // NZ
OWN = 24


def place():
    dp = lax.axis_index("dp")
    lo = lax.axis_index("mp")
    c = lax.rem(dp, 2)
    y = lax.rem(lax.div(dp, 2), 4)
    xh = lax.rem(lax.div(dp, 8), 2)
    z = lax.div(dp, 16)
    return z, y, xh * 2 + lo, c


def device_at(z, y, x, c):
    return (((z * 2 + lax.div(x, 2)) * 4 + y) * 2 + c, lax.rem(x, 2))


def slot_of(x, c):
    return (lax.div(x, 2) * 2 + c) * 2 + lax.rem(x, 2)


def send_to(src, dst, send_sem, recv_sem, device):
    return pltpu.make_async_remote_copy(
        src_ref=src,
        dst_ref=dst,
        send_sem=send_sem,
        recv_sem=recv_sem,
        device_id=device,
        device_id_type=MESH,
    )


def greet(devices):
    barrier = pltpu.get_barrier_semaphore()
    for device in devices:
        pl.semaphore_signal(barrier, inc=1, device_id=device, device_id_type=MESH)
    pl.semaphore_wait(barrier, len(devices))


GROUP = [(dx, dc) for dx in range(NX) for dc in range(NC) if (dx, dc) != (0, 0)]


def dot_t(a, b):
    return lax.dot_general(a, b, (((1,), (1,)), ((), ())), preferred_element_type=F32)


CODE = 256.0
TOP = 14.98
LEAST = 2.0**-100


def code_of(peak):
    return jnp.ceil(jnp.log2(jnp.maximum(peak, LEAST)) * CODE)


def whole(values):
    return jnp.round(values).astype(jnp.int32)


def encode(values, pad):
    code = code_of(jnp.max(jnp.abs(values), axis=0, keepdims=True))
    digits = whole(values * jnp.exp2(TOP - code / CODE))
    codes = jnp.broadcast_to(code.astype(jnp.int32), (pad, values.shape[1]))
    return jnp.concatenate([digits, codes], axis=0).astype(jnp.int16)


def decode(packed, pad):
    wide = packed.astype(jnp.int32).astype(F32)
    rows = packed.shape[0] - pad
    return wide[:rows] * jnp.exp2(wide[rows : rows + 1] / CODE - TOP)


def slope_of(x):
    k = 0.7978845608028654
    x2 = x * x
    t = jnp.tanh(k * x * (1.0 + 0.044715 * x2))
    return 0.5 * (1.0 + t) + 0.5 * x * (1.0 - t * t) * (k * (1.0 + 3.0 * 0.044715 * x2))


YX = [(dxh, j) for dxh in range(2) for j in range(NY) if (dxh, j) != (0, 0)]
PAIRS = [(0, 1), (2, 0), (2, 1)]
ORDER = [4, 3, 5, 2, 6, 1, 7, 0]
SUBS = 2
SUB = H // SUBS


def kernel(
    pooled_ref,
    count_ref,
    scale_ref,
    bias_ref,
    loss_scale_ref,
    image_ref,
    text_ref,
    image_pre_ref,
    text_pre_ref,
    out_ref,
    loss_out_ref,
    half_out,
    half_in,
    counts,
    plane,
    group,
    parts,
    landed,
    unit_own,
    image_tok,
    text_tok,
    image_t,
    text_t,
    image_pre,
    text_pre,
    image_gpre,
    text_gpre,
    terms,
    sibling,
    up_out,
    up_in,
    down_out,
    down_in,
    near_out,
    near_in,
    final,
    loss_group,
    loss_y,
    loss_z,
    s_load,
    s_other,
    r_other,
    s_count,
    r_count,
    s_group,
    r_group,
    s_y,
    r_y,
    s_up,
    r_up,
    s_down,
    r_down,
    s_part,
    r_part,
    s_sib,
    r_sib,
    s_rup,
    r_rup,
    s_rdown,
    r_rdown,
    s_near,
    r_near,
    s_final,
    r_final,
    s_lg,
    r_lg,
    s_ly,
    r_ly,
    s_lz,
    r_lz,
):
    z, y, x, c = place()
    xh, lo = lax.div(x, 2), lax.rem(x, 2)
    me = slot_of(x, c)
    up = device_at(lax.rem(z + 1, NZ), y, x, c)
    down = device_at(lax.rem(z + NZ - 1, NZ), y, x, c)
    members = {(dx, dc): device_at(z, y, lax.rem(x + dx, NX), lax.rem(c + dc, NC)) for dx, dc in GROUP}
    sources = {(dx, dc): (lax.rem(x + NX - dx, NX), lax.rem(c + dc, NC)) for dx, dc in GROUP}
    near = {(dxh, j): device_at(z, lax.rem(y + j, NY), lax.rem(xh + dxh, 2) * 2 + lo, c) for dxh, j in YX}
    y_peers = [near[(0, j)] for j in range(1, NY)]
    z_peers = [device_at(lax.rem(z + k, NZ), y, x, c) for k in range(1, NZ)]
    partner = device_at(z, y, xh * 2 + 1 - lo, c)
    twin = members[(0, 1)]
    copies = []

    def start(*args):
        copy = send_to(*args)
        copy.start()
        copies.append(copy)

    loads = [
        pltpu.make_async_copy(src, dst, s_load.at[n])
        for n, (src, dst) in enumerate(
            [(image_ref, image_tok), (text_ref, text_tok), (image_pre_ref, image_pre), (text_pre_ref, text_pre)]
        )
    ]
    for load in loads:
        load.start()
    greet([members[key] for key in GROUP] + [near[key] for key in YX if key != (1, 0)] + z_peers)

    mine = pooled_ref[...]
    first = lo == 0
    own_sq = jnp.sum(mine * mine, axis=1, keepdims=True)
    half_out[:, :H] = jnp.where(first, mine[16:32], mine[0:16])
    half_out[:, H:] = jnp.broadcast_to(jnp.where(first, own_sq[0:16], own_sq[16:32]), (16, EXT))
    start(half_out, half_in, s_other, r_other, partner)
    pair_slot = xh * 2 + c
    counts[pair_slot] = count_ref[...]
    for n, key in enumerate(PAIRS):
        start(counts.at[pair_slot], counts.at[pair_slot], s_count.at[n], r_count.at[n], members[key])
    own_rows = jnp.where(first, mine[0:16], mine[16:32])
    own_rows_sq = jnp.where(first, own_sq[0:16], own_sq[16:32])
    rest_sq = jnp.where(first, own_sq[16:32], own_sq[0:16])
    send_to(half_out, half_in, s_other, r_other, partner).wait_recv()
    theirs = half_in[:, :H]
    norm_own = jnp.sqrt(own_rows_sq + jnp.sum(theirs * theirs, axis=1, keepdims=True) + 1e-6)
    norm_rest = jnp.sqrt(rest_sq + half_in[:, H : H + 1] + 1e-6)
    norm = jnp.concatenate(
        [jnp.where(first, norm_own, norm_rest), jnp.where(first, norm_rest, norm_own)], axis=0
    )
    unit_own[...] = mine / norm
    unit_mine = own_rows / norm_own
    unit_theirs = theirs / norm_own
    low = jnp.where(first, unit_mine, unit_theirs)
    high = jnp.where(first, unit_theirs, unit_mine)
    for n, (dx, dc) in enumerate(PAIRS):
        slot = lax.rem(xh + dx // 2, 2) * 2 + lax.rem(c + dc, NC)
        send_to(counts.at[slot], counts.at[slot], s_count.at[n], r_count.at[n], members[(dx, dc)]).wait_recv()
    row_total = jnp.sum(counts[...], axis=0)[0:1, :]
    own_count = count_ref[0:1, :]
    sample = lax.rem(lax.broadcasted_iota(jnp.int32, (16, EXT), 0), 8) + 8 * lo
    lane = lax.broadcasted_iota(jnp.int32, (16, EXT), 1)
    usable = jnp.where(sample.astype(F32) < own_count, 1.0, 0.0)
    extra = jnp.where(lane < EXT // 2, usable, jnp.broadcast_to(row_total, (16, EXT)))
    block = jnp.concatenate([low.astype(BF16), high.astype(BF16), extra.astype(BF16)], axis=1)
    plane[z, y] = block
    group[me] = block

    def pass_up(step, j, zs, ys):
        start(plane.at[zs, ys], plane.at[zs, ys], s_up.at[step, j], r_up.at[step, j], up)

    def pass_down(step, j, zs, ys):
        start(plane.at[zs, ys], plane.at[zs, ys], s_down.at[step, j], r_down.at[step, j], down)

    for j in range(1, NY):
        start(plane.at[z, y], plane.at[z, y], s_y.at[j - 1], r_y.at[j - 1], y_peers[j - 1])
    pass_up(0, 0, z, y)
    pass_down(0, 0, z, y)
    for n, key in enumerate(GROUP):
        start(group.at[me], group.at[me], s_group.at[n], r_group.at[n], members[key])

    def turn(tok, out, p):
        def work():
            flipped = tok[:, 384 * p : 384 * p + 384].T
            out[2 * p : 2 * p + 2] = flipped.reshape(2, ZROWS, tok.shape[0])

        return work

    def bend(pre, first_row, rows):
        def work():
            @pl.loop(0, rows // 16)
            def _(i):
                at = pl.ds(pl.multiple_of(first_row + i * 16, 16), 16)
                pre[at, :] = slope_of(pre[at, :])

        return work

    for load in loads:
        load.wait()
    pieces = [turn(image_tok, image_t, p) for p in range(4)] + [turn(text_tok, text_t, p) for p in range(4)]
    pieces += [bend(image_pre, 128 * p, 128) for p in range(8)] + [bend(text_pre, 128 * p, 128) for p in range(4)]
    done = [0]

    def idle(amount=1):
        for piece in pieces[done[0] : done[0] + amount]:
            piece()
        done[0] += amount

    for j in range(1, NY):
        ys = lax.rem(y + NY - j, NY)
        send_to(plane.at[z, ys], plane.at[z, ys], s_y.at[j - 1], r_y.at[j - 1], up).wait_recv()
        pass_up(0, j, z, ys)
        pass_down(0, j, z, ys)
    idle()
    for step in range(4):
        for j in range(NY):
            ys = lax.rem(y + NY - j, NY)
            if step < 3 or j < 2:
                zs = lax.rem(z + NZ - step - 1, NZ)
                send_to(plane.at[zs, ys], plane.at[zs, ys], s_up.at[step, j], r_up.at[step, j], up).wait_recv()
                if step < 2 or (step == 2 and j < 2):
                    pass_up(step + 1, j, zs, ys)
            if step < 3 or j >= 2:
                zs = lax.rem(z + step + 1, NZ)
                send_to(plane.at[zs, ys], plane.at[zs, ys], s_down.at[step, j], r_down.at[step, j], down).wait_recv()
                if step < 2 or (step == 2 and j >= 2):
                    pass_down(step + 1, j, zs, ys)
            idle(2 if step < 1 else 1)
    idle(len(pieces) - done[0])
    for n, key in enumerate(GROUP):
        slot = slot_of(*sources[key])
        send_to(group.at[slot], group.at[slot], s_group.at[n], r_group.at[n], members[key]).wait_recv()

    rows = group[...].reshape(8 * 16, D + EXT)
    cols = plane[...].reshape(32 * 16, D + EXT)
    row_main, col_main = rows[:, :D], cols[:, :D]
    logit_mult = scale_ref[0]
    logits = logit_mult * dot_t(row_main, col_main) + bias_ref[0]
    pick = lax.broadcasted_iota(jnp.int32, (16, EXT), 0) * (EXT // 2)
    pick = jnp.where(pick == lax.broadcasted_iota(jnp.int32, (16, EXT), 1), 1.0, 0.0).astype(BF16)
    col_extra = dot_t(pick, cols[:, D:])
    total = jnp.sum(col_extra[1:2, :]) * (1.0 / 16.0)
    col_usable = col_extra[0:1, :]
    row_usable = rows[:, D : D + 1].astype(F32)
    shape = (8 * 16, 32 * 16)
    r = lax.broadcasted_iota(jnp.int32, shape, 0)
    q = lax.broadcasted_iota(jnp.int32, shape, 1)
    r_text = lax.rem(lax.div(r, 8), 2)
    q_text = lax.rem(lax.div(q, 8), 2)
    same = (lax.div(r, 16) == me) & (lax.div(q, 16) == z * NY + y) & (lax.rem(r, 8) == lax.rem(q, 8))
    used = (row_usable * col_usable > 0.5) & (r_text != q_text)
    sign = jnp.where(same, 1.0, -1.0)
    margin = -sign * logits
    coeff = loss_scale_ref[0] / total
    dlogit = (jnp.where(used, -sign * jax.nn.sigmoid(margin), 0.0) * coeff).astype(BF16)
    grad = logit_mult * jnp.dot(dlogit, col_main, preferred_element_type=F32)
    radial = jnp.sum(row_main.astype(F32) * grad, axis=1, keepdims=True)
    code = code_of(jnp.max(jnp.abs(grad), axis=1, keepdims=True))
    factor = jnp.exp2(TOP - code / CODE)
    digits = whole(grad * factor).astype(jnp.int16)
    radial = whole(radial * factor * (1.0 / 40.0))
    side = lax.broadcasted_iota(jnp.int32, (8 * 16, EXT), 1) < EXT // 2
    side = jnp.where(side, code.astype(jnp.int32), radial).astype(jnp.int16)
    for pair in range(4):
        for half in range(2):
            band = slice(pair * 32, pair * 32 + 32)
            parts[pair, half, :, :H] = digits[band, half * H : half * H + H]
            parts[pair, half, :, H:] = side[band]

    for n, (dx, dc) in enumerate(GROUP):
        tx, tc = lax.rem(x + dx, NX), lax.rem(c + dc, NC)
        src = parts.at[lax.div(tx, 2) * 2 + tc, lax.rem(tx, 2)]
        start(src, landed.at[me], s_part.at[n], r_part.at[n], members[(dx, dc)])

    soft = jnp.maximum(margin, 0.0) + jnp.log1p(jnp.exp(-jnp.abs(margin)))
    loss = jnp.sum(jnp.where(used & (r_text == 0), soft, 0.0), axis=1, keepdims=True)
    loss_group[0] = jnp.broadcast_to(jnp.sum(loss, axis=0, keepdims=True) / total, (8, 128))
    for n, key in enumerate(GROUP):
        start(loss_group.at[0], loss_group.at[n + 1], s_lg.at[n], r_lg.at[n], members[key])

    def opened(packed):
        wide = packed.astype(jnp.int32).astype(F32)
        back = jnp.exp2(wide[:, H : H + 1] / CODE - TOP)
        return wide[:, :H] * back, wide[:, H + EXT // 2 : H + EXT // 2 + 1] * (back * 40.0)

    sum_grad, sum_radial = opened(parts[pair_slot, lo])
    for n, key in enumerate(GROUP):
        slot = slot_of(*sources[key])
        send_to(landed.at[slot], landed.at[slot], s_part.at[n], r_part.at[n], members[key]).wait_recv()
        more_grad, more_radial = opened(landed[slot])
        sum_grad = sum_grad + more_grad
        sum_radial = sum_radial + more_radial
    gp = (sum_grad - unit_own[...] * sum_radial) / norm
    for i in range(16):
        row = (i // 8) * 16 + i % 8
        at = slice(64 * i, 64 * i + 64)
        image_gpre[at, :] = (gp[row : row + 1] / 64.0 * image_pre[at, :]).astype(BF16)
        at = slice(32 * i, 32 * i + 32)
        text_gpre[at, :] = (gp[row + 8 : row + 9] / 32.0 * text_pre[at, :]).astype(BF16)

    def compute(n):
        t = lax.rem(z + ORDER[n], NZ)
        terms[0, t] = jnp.dot(image_t[t], image_gpre[...], preferred_element_type=F32)
        terms[1, t] = jnp.dot(text_t[t], text_gpre[...], preferred_element_type=F32)
        start(terms.at[1 - c, t], sibling.at[t], s_sib.at[n], r_sib.at[n], twin)

    def chunk(n):
        t = lax.rem(z + ORDER[n], NZ)
        send_to(sibling.at[t], sibling.at[t], s_sib.at[n], r_sib.at[n], twin).wait_recv()
        return t

    def ring(step, n, out, inn, send_sem, recv_sem, way, split):
        t = chunk(n) if n is not None else lax.rem(z + ORDER[0], NZ)
        for h in range(SUBS):
            if step == 0 and h != split:
                continue
            at = slice(h * SUB, h * SUB + SUB)
            value = terms[c, t, :, at] + sibling[t, :, at]
            if step > 1 or (step == 1 and h == split):
                send_to(out.at[step - 1, h], inn.at[step - 1, h], send_sem.at[step - 1, h], recv_sem.at[step - 1, h], way).wait_recv()
                value = value + decode(inn[step - 1, h], 16)
            out[step, h] = encode(value, 16)
            start(out.at[step, h], inn.at[step, h], send_sem.at[step, h], recv_sem.at[step, h], way)

    def ring_up(step, n):
        ring(step, n, up_out, up_in, s_rup, r_rup, up, 0)

    def ring_down(step, n):
        ring(step, n, down_out, down_in, s_rdown, r_rdown, down, 1)

    compute(0)
    compute(1)
    ring_up(0, 0)
    ring_down(0, None)
    compute(2)
    compute(3)
    for n, key in enumerate(GROUP):
        send_to(loss_group.at[0], loss_group.at[n + 1], s_lg.at[n], r_lg.at[n], members[key]).wait_recv()
    loss_y[0] = jnp.sum(loss_group[...], axis=0)
    for j in range(1, NY):
        start(loss_y.at[0], loss_y.at[j], s_ly.at[j - 1], r_ly.at[j - 1], y_peers[j - 1])
    ring_up(1, 1)
    ring_down(1, 2)
    compute(4)
    compute(5)
    for j in range(1, NY):
        send_to(loss_y.at[0], loss_y.at[j], s_ly.at[j - 1], r_ly.at[j - 1], y_peers[j - 1]).wait_recv()
    loss_z[0] = jnp.sum(loss_y[...], axis=0)
    for k in range(1, NZ):
        start(loss_z.at[0], loss_z.at[k], s_lz.at[k - 1], r_lz.at[k - 1], z_peers[k - 1])
    ring_up(2, 3)
    ring_down(2, 4)
    compute(6)
    compute(7)
    ring_up(3, 5)
    ring_down(3, 6)
    for k in range(1, NZ):
        send_to(loss_z.at[0], loss_z.at[k], s_lz.at[k - 1], r_lz.at[k - 1], z_peers[k - 1]).wait_recv()
    loss_out_ref[...] = jnp.sum(loss_z[...], axis=0)
    t = chunk(7)
    own = []
    for h in range(SUBS):
        at = slice(h * SUB, h * SUB + SUB)
        value = terms[c, t, :, at] + sibling[t, :, at]
        send_to(up_out.at[3, h], up_in.at[3, h], s_rup.at[3, h], r_rup.at[3, h], up).wait_recv()
        value = value + decode(up_in[3, h], 16)
        send_to(down_out.at[3, h], down_in.at[3, h], s_rdown.at[3, h], r_rdown.at[3, h], down).wait_recv()
        own.append(value + decode(down_in[3, h], 16))
    own = jnp.concatenate(own, axis=1).reshape(2 * NY, OWN, H)
    for i in range(2 * NY):
        near_out[i] = encode(own[i], 8)
    for n, (dxh, j) in enumerate(YX):
        src = near_out.at[lax.rem(xh + dxh, 2) * NY + lax.rem(y + j, NY)]
        start(src, near_in.at[n], s_near.at[n], r_near.at[n], near[(dxh, j)])
    result = decode(near_out[xh * NY + y], 8)
    for n, key in enumerate(YX):
        send_to(near_in.at[n], near_in.at[n], s_near.at[n], r_near.at[n], near[key]).wait_recv()
        result = result + decode(near_in[n], 8)
    final[c] = result
    start(final.at[c], final.at[c], s_final, r_final, twin)
    send_to(final.at[1 - c], final.at[1 - c], s_final, r_final, twin).wait_recv()
    out_ref[...] = final[...]
    for copy in copies:
        copy.wait_send()


def run_kernel(pooled, count, logit_scale, logit_bias, loss_scale, image, text, image_pre, text_pre):
    dma = pltpu.SemaphoreType.DMA
    vmem = pl.BlockSpec(memory_space=pltpu.VMEM)
    smem = pl.BlockSpec(memory_space=pltpu.SMEM)
    anywhere = pl.BlockSpec(memory_space=pl.ANY)
    image_rows, text_rows = image.shape[0], text.shape[0]
    ring = pltpu.VMEM((4, SUBS, ZROWS + 16, SUB), jnp.int16)
    tile = (8, 128)
    return pl.pallas_call(
        kernel,
        out_shape=(jax.ShapeDtypeStruct((2, OWN, H), F32), jax.ShapeDtypeStruct(tile, F32)),
        in_specs=[vmem, vmem, smem, smem, smem, anywhere, anywhere, anywhere, anywhere],
        out_specs=(vmem, vmem),
        scratch_shapes=[
            pltpu.VMEM((16, H + EXT), F32),
            pltpu.VMEM((16, H + EXT), F32),
            pltpu.VMEM((4,) + tile, F32),
            pltpu.VMEM((NZ, NY, 16, D + EXT), BF16),
            pltpu.VMEM((8, 16, D + EXT), BF16),
            pltpu.VMEM((4, 2, 32, H + EXT), jnp.int16),
            pltpu.VMEM((8, 32, H + EXT), jnp.int16),
            pltpu.VMEM((32, H), F32),
            pltpu.VMEM((image_rows, D), BF16),
            pltpu.VMEM((text_rows, D), BF16),
            pltpu.VMEM((NZ, ZROWS, image_rows), BF16),
            pltpu.VMEM((NZ, ZROWS, text_rows), BF16),
            pltpu.VMEM((image_rows, H), F32),
            pltpu.VMEM((text_rows, H), F32),
            pltpu.VMEM((image_rows, H), BF16),
            pltpu.VMEM((text_rows, H), BF16),
            pltpu.VMEM((2, NZ, ZROWS, H), F32),
            pltpu.VMEM((NZ, ZROWS, H), F32),
            ring,
            ring,
            ring,
            ring,
            pltpu.VMEM((2 * NY, 32, H), jnp.int16),
            pltpu.VMEM((7, 32, H), jnp.int16),
            pltpu.VMEM((2, OWN, H), F32),
            pltpu.VMEM((8,) + tile, F32),
            pltpu.VMEM((NY,) + tile, F32),
            pltpu.VMEM((NZ,) + tile, F32),
            dma((4,)),
        ]
        + [dma] * 2
        + [dma((3,))] * 2
        + [dma((7,))] * 2
        + [dma((3,))] * 2
        + [dma((4, 4))] * 4
        + [dma((7,))] * 2
        + [dma((8,))] * 2
        + [dma((4, SUBS))] * 4
        + [dma((7,))] * 2
        + [dma] * 2
        + [dma((7,))] * 2
        + [dma((3,))] * 2
        + [dma((7,))] * 2,
        compiler_params=pltpu.CompilerParams(
            collective_id=1, has_side_effects=True, vmem_limit_bytes=58 * 1024 * 1024
        ),
    )(pooled, count, logit_scale, logit_bias, loss_scale, image, text, image_pre, text_pre)


def tower_block(tokens, weight, offset):
    flat_tokens = tokens.reshape(-1, tokens.shape[2])
    preact = jnp.dot(flat_tokens, weight, preferred_element_type=F32)
    residual = lax.dynamic_slice_in_dim(flat_tokens, offset, weight.shape[1], 1).astype(F32)
    hidden = residual + jax.nn.gelu(preact, approximate=True)
    pooled = jnp.mean(hidden.reshape(tokens.shape[0], tokens.shape[1], -1), axis=1)
    return (flat_tokens, preact, pooled)


def body(
    image_tokens,
    text_tokens,
    image_weight,
    text_weight,
    logit_scale,
    logit_bias,
    loss_scale,
    valid_count,
):
    core = lax.rem(lax.axis_index("dp"), 2)
    half_start = lax.axis_index("mp") * H
    image_flat, image_preact, image_pooled = tower_block(image_tokens, image_weight, half_start)
    text_flat, text_preact, text_pooled = tower_block(text_tokens, text_weight, half_start)
    pooled = jnp.concatenate([image_pooled[:8], text_pooled[:8], image_pooled[8:], text_pooled[8:]], axis=0)
    count = jnp.broadcast_to(valid_count.astype(F32)[:, None], (8, 128))
    grads_out, loss = run_kernel(
        pooled, count, logit_scale, logit_bias, loss_scale, image_flat, text_flat, image_preact, text_preact
    )
    mine = lax.dynamic_slice_in_dim(grads_out, core * 12, 12, 1)
    return (loss[0, 0], mine[0], mine[1])


def solution(mesh):
    placed = (
        P("dp", None, None),
        P("dp", None, None),
        P(None, "mp"),
        P(None, "mp"),
        P(),
        P(),
        P(),
        P("dp"),
    )
    return jax.shard_map(
        body,
        mesh=mesh,
        in_specs=placed,
        out_specs=(P(), P("dp", "mp"), P("dp", "mp")),
        check_vma=False,
    )
```

```python
import jax
import jax.numpy as jnp
from jax import lax
from jax.experimental import pallas as pl
from jax.experimental.pallas import tpu as pltpu
from jax.sharding import PartitionSpec as P

MESH = pl.DeviceIdType.MESH
F32 = jnp.float32
BF16 = jnp.bfloat16
NZ, NY, NX, NC = 8, 4, 4, 2
D = 1536
H = 768
EXT = 128
ZROWS = D // NZ
OWN = 24


def place():
    dp = lax.axis_index("dp")
    lo = lax.axis_index("mp")
    c = lax.rem(dp, 2)
    y = lax.rem(lax.div(dp, 2), 4)
    xh = lax.rem(lax.div(dp, 8), 2)
    z = lax.div(dp, 16)
    return z, y, xh * 2 + lo, c


def device_at(z, y, x, c):
    return (((z * 2 + lax.div(x, 2)) * 4 + y) * 2 + c, lax.rem(x, 2))


def slot_of(x, c):
    return (lax.div(x, 2) * 2 + c) * 2 + lax.rem(x, 2)


def send_to(src, dst, send_sem, recv_sem, device):
    return pltpu.make_async_remote_copy(
        src_ref=src,
        dst_ref=dst,
        send_sem=send_sem,
        recv_sem=recv_sem,
        device_id=device,
        device_id_type=MESH,
    )


def greet(devices):
    barrier = pltpu.get_barrier_semaphore()
    for device in devices:
        pl.semaphore_signal(barrier, inc=1, device_id=device, device_id_type=MESH)
    pl.semaphore_wait(barrier, len(devices))


GROUP = [(dx, dc) for dx in range(NX) for dc in range(NC) if (dx, dc) != (0, 0)]


def dot_t(a, b):
    return lax.dot_general(a, b, (((1,), (1,)), ((), ())), preferred_element_type=F32)


CODE = 256.0
TOP = 14.98
LEAST = 2.0**-100


def code_of(peak):
    return jnp.ceil(jnp.log2(jnp.maximum(peak, LEAST)) * CODE)


def whole(values):
    return jnp.round(values).astype(jnp.int32)


def encode(values, pad):
    code = code_of(jnp.max(jnp.abs(values), axis=0, keepdims=True))
    digits = whole(values * jnp.exp2(TOP - code / CODE))
    codes = jnp.broadcast_to(code.astype(jnp.int32), (pad, values.shape[1]))
    return jnp.concatenate([digits, codes], axis=0).astype(jnp.int16)


def decode(packed, pad):
    wide = packed.astype(jnp.int32).astype(F32)
    rows = packed.shape[0] - pad
    return wide[:rows] * jnp.exp2(wide[rows : rows + 1] / CODE - TOP)


def gelu(x):
    k = 0.7978845608028654
    return 0.5 * x * (1.0 + jnp.tanh(k * x * (1.0 + 0.044715 * (x * x))))


def slope_of(x):
    k = 0.7978845608028654
    x2 = x * x
    t = jnp.tanh(k * x * (1.0 + 0.044715 * x2))
    return 0.5 * (1.0 + t) + 0.5 * x * (1.0 - t * t) * (k * (1.0 + 3.0 * 0.044715 * x2))


YX = [(dxh, j) for dxh in range(2) for j in range(NY) if (dxh, j) != (0, 0)]
PAIRS = [(0, 1), (2, 0), (2, 1)]
ORDER = [4, 3, 5, 2, 6, 1, 7, 0]
SUBS = 2
SUB = 256
FAR = SUBS * SUB
REST = H - FAR


def kernel(
    count_ref,
    scale_ref,
    bias_ref,
    loss_scale_ref,
    image_ref,
    text_ref,
    image_weight_ref,
    text_weight_ref,
    image_out_ref,
    text_out_ref,
    loss_out_ref,
    image_weight,
    text_weight,
    pooled,
    half_out,
    half_in,
    counts,
    plane,
    group,
    parts,
    landed,
    unit_own,
    image_tok,
    text_tok,
    image_t,
    text_t,
    image_pre,
    text_pre,
    image_gpre,
    text_gpre,
    terms,
    sibling,
    up_out,
    up_in,
    down_out,
    down_in,
    near_out,
    near_in,
    wide_out,
    wide_in,
    line_out,
    line_in,
    rest_own,
    final,
    loss_group,
    loss_y,
    loss_z,
    s_load,
    s_other,
    r_other,
    s_count,
    r_count,
    s_group,
    r_group,
    s_y,
    r_y,
    s_up,
    r_up,
    s_down,
    r_down,
    s_part,
    r_part,
    s_sib,
    r_sib,
    s_rup,
    r_rup,
    s_rdown,
    r_rdown,
    s_near,
    r_near,
    s_wide,
    r_wide,
    s_line,
    r_line,
    s_final,
    r_final,
    s_lg,
    r_lg,
    s_ly,
    r_ly,
    s_lz,
    r_lz,
):
    z, y, x, c = place()
    xh, lo = lax.div(x, 2), lax.rem(x, 2)
    me = slot_of(x, c)
    up = device_at(lax.rem(z + 1, NZ), y, x, c)
    down = device_at(lax.rem(z + NZ - 1, NZ), y, x, c)
    members = {(dx, dc): device_at(z, y, lax.rem(x + dx, NX), lax.rem(c + dc, NC)) for dx, dc in GROUP}
    sources = {(dx, dc): (lax.rem(x + NX - dx, NX), lax.rem(c + dc, NC)) for dx, dc in GROUP}
    near = {(dxh, j): device_at(z, lax.rem(y + j, NY), lax.rem(xh + dxh, 2) * 2 + lo, c) for dxh, j in YX}
    y_peers = [near[(0, j)] for j in range(1, NY)]
    z_peers = [device_at(lax.rem(z + k, NZ), y, x, c) for k in range(1, NZ)]
    partner = device_at(z, y, xh * 2 + 1 - lo, c)
    twin = members[(0, 1)]
    copies = []

    def start(*args):
        copy = send_to(*args)
        copy.start()
        copies.append(copy)

    loads = {}

    def fetch(name, src, dst):
        loads[name] = pltpu.make_async_copy(src, dst, s_load.at[len(loads)])
        loads[name].start()

    fetch("tw", text_weight_ref, text_weight)
    for p in range(2):
        at = pl.ds(256 * p, 256)
        fetch("t%d" % p, text_ref.at[at], text_tok.at[at])
    fetch("iw", image_weight_ref, image_weight)
    for p in range(4):
        at = pl.ds(256 * p, 256)
        fetch("i%d" % p, image_ref.at[at], image_tok.at[at])
    peers = [members[key] for key in GROUP] + [near[key] for key in YX if key != (1, 0)] + z_peers
    barrier = pltpu.get_barrier_semaphore()
    for peer in peers:
        pl.semaphore_signal(barrier, inc=1, device_id=peer, device_id_type=MESH)

    columns = pl.ds(pl.multiple_of(lo * H, H), H)

    def forward(tok, weight, pre, p):
        at = slice(256 * p, 256 * p + 256)
        pre[at, :] = jnp.dot(tok[at, :], weight[...], preferred_element_type=F32)

    def pool(tok, pre, p, tokens, offset):
        for i in range(256 // tokens):
            at = slice(256 * p + tokens * i, 256 * p + tokens * i + tokens)
            hidden = tok[at, columns].astype(F32) + gelu(pre[at, :])
            sample = 256 // tokens * p + i
            row = (sample // 8) * 16 + offset + sample % 8
            pooled[row : row + 1, :] = jnp.sum(hidden, axis=0, keepdims=True) * (1.0 / tokens)

    first = lo == 0
    pair_slot = xh * 2 + c

    def swap(w):
        low, high = pooled[8 * w : 8 * w + 8, :], pooled[16 + 8 * w : 24 + 8 * w, :]
        ours = jnp.where(first, low, high)
        squares = jnp.sum(ours * ours, axis=1, keepdims=True)
        half_out[w, :, :H] = jnp.where(first, high, low)
        half_out[w, :, H:] = jnp.broadcast_to(squares, (8, EXT))
        start(half_out.at[w], half_in.at[w], s_other.at[w], r_other.at[w], partner)

    for name in ("tw", "t0"):
        loads[name].wait()
    forward(text_tok, text_weight, text_pre, 0)
    loads["t1"].wait()
    forward(text_tok, text_weight, text_pre, 1)
    pool(text_tok, text_pre, 0, 32, 8)
    for name in ("iw", "i0"):
        loads[name].wait()
    forward(image_tok, image_weight, image_pre, 0)
    pool(text_tok, text_pre, 1, 32, 8)
    pl.semaphore_wait(barrier, len(peers))
    swap(1)
    counts[pair_slot] = count_ref[...]
    for n, key in enumerate(PAIRS):
        start(counts.at[pair_slot], counts.at[pair_slot], s_count.at[n], r_count.at[n], members[key])
    for p in range(1, 4):
        loads["i%d" % p].wait()
        forward(image_tok, image_weight, image_pre, p)
        pool(image_tok, image_pre, p - 1, 64, 0)
    pool(image_tok, image_pre, 3, 64, 0)
    swap(0)
    mine = pooled[...]
    own_sq = jnp.sum(mine * mine, axis=1, keepdims=True)
    own_rows = jnp.where(first, mine[0:16], mine[16:32])
    own_rows_sq = jnp.where(first, own_sq[0:16], own_sq[16:32])
    rest_sq = jnp.where(first, own_sq[16:32], own_sq[0:16])
    for w in range(2):
        send_to(half_out.at[w], half_in.at[w], s_other.at[w], r_other.at[w], partner).wait_recv()
    arrived = half_in[...].reshape(16, H + EXT)
    theirs = arrived[:, :H]
    norm_own = jnp.sqrt(own_rows_sq + jnp.sum(theirs * theirs, axis=1, keepdims=True) + 1e-6)
    norm_rest = jnp.sqrt(rest_sq + arrived[:, H : H + 1] + 1e-6)
    norm = jnp.concatenate(
        [jnp.where(first, norm_own, norm_rest), jnp.where(first, norm_rest, norm_own)], axis=0
    )
    unit_own[...] = mine / norm
    unit_mine = own_rows / norm_own
    unit_theirs = theirs / norm_own
    low = jnp.where(first, unit_mine, unit_theirs)
    high = jnp.where(first, unit_theirs, unit_mine)
    for n, (dx, dc) in enumerate(PAIRS):
        slot = lax.rem(xh + dx // 2, 2) * 2 + lax.rem(c + dc, NC)
        send_to(counts.at[slot], counts.at[slot], s_count.at[n], r_count.at[n], members[(dx, dc)]).wait_recv()
    row_total = jnp.sum(counts[...], axis=0)[0:1, :]
    own_count = count_ref[0:1, :]
    sample = lax.rem(lax.broadcasted_iota(jnp.int32, (16, EXT), 0), 8) + 8 * lo
    lane = lax.broadcasted_iota(jnp.int32, (16, EXT), 1)
    usable = jnp.where(sample.astype(F32) < own_count, 1.0, 0.0)
    extra = jnp.where(lane < EXT // 2, usable, jnp.broadcast_to(row_total, (16, EXT)))
    block = jnp.concatenate([low.astype(BF16), high.astype(BF16), extra.astype(BF16)], axis=1)
    plane[z, y] = block
    group[me] = block

    def pass_up(step, j, zs, ys):
        start(plane.at[zs, ys], plane.at[zs, ys], s_up.at[step, j], r_up.at[step, j], up)

    def pass_down(step, j, zs, ys):
        start(plane.at[zs, ys], plane.at[zs, ys], s_down.at[step, j], r_down.at[step, j], down)

    for j in range(1, NY):
        start(plane.at[z, y], plane.at[z, y], s_y.at[j - 1], r_y.at[j - 1], y_peers[j - 1])
    pass_up(0, 0, z, y)
    pass_down(0, 0, z, y)
    for n, key in enumerate(GROUP):
        start(group.at[me], group.at[me], s_group.at[n], r_group.at[n], members[key])

    def turn(tok, out, p):
        def work():
            flipped = tok[:, 384 * p : 384 * p + 384].T
            out[2 * p : 2 * p + 2] = flipped.reshape(2, ZROWS, tok.shape[0])

        return work

    def bend(pre, first_row, rows):
        def work():
            @pl.loop(0, rows // 16)
            def _(i):
                at = pl.ds(pl.multiple_of(first_row + i * 16, 16), 16)
                pre[at, :] = slope_of(pre[at, :])

        return work

    pieces = [turn(image_tok, image_t, p) for p in range(4)] + [turn(text_tok, text_t, p) for p in range(4)]
    pieces += [bend(image_pre, 128 * p, 128) for p in range(8)] + [bend(text_pre, 128 * p, 128) for p in range(4)]
    done = [0]

    def idle(amount=1):
        for piece in pieces[done[0] : done[0] + amount]:
            piece()
        done[0] += amount

    for j in range(1, NY):
        ys = lax.rem(y + NY - j, NY)
        send_to(plane.at[z, ys], plane.at[z, ys], s_y.at[j - 1], r_y.at[j - 1], up).wait_recv()
        pass_up(0, j, z, ys)
        pass_down(0, j, z, ys)
    idle()
    for step in range(4):
        for j in range(NY):
            ys = lax.rem(y + NY - j, NY)
            if step < 3 or j < 2:
                zs = lax.rem(z + NZ - step - 1, NZ)
                send_to(plane.at[zs, ys], plane.at[zs, ys], s_up.at[step, j], r_up.at[step, j], up).wait_recv()
                if step < 2 or (step == 2 and j < 2):
                    pass_up(step + 1, j, zs, ys)
            if step < 3 or j >= 2:
                zs = lax.rem(z + step + 1, NZ)
                send_to(plane.at[zs, ys], plane.at[zs, ys], s_down.at[step, j], r_down.at[step, j], down).wait_recv()
                if step < 2 or (step == 2 and j >= 2):
                    pass_down(step + 1, j, zs, ys)
            idle(2 if step < 1 else 1)
    idle(len(pieces) - done[0])
    for n, key in enumerate(GROUP):
        slot = slot_of(*sources[key])
        send_to(group.at[slot], group.at[slot], s_group.at[n], r_group.at[n], members[key]).wait_recv()

    rows = group[...].reshape(8 * 16, D + EXT)
    cols = plane[...].reshape(32 * 16, D + EXT)
    row_main, col_main = rows[:, :D], cols[:, :D]
    logit_mult = scale_ref[0]
    logits = logit_mult * dot_t(row_main, col_main) + bias_ref[0]
    pick = lax.broadcasted_iota(jnp.int32, (16, EXT), 0) * (EXT // 2)
    pick = jnp.where(pick == lax.broadcasted_iota(jnp.int32, (16, EXT), 1), 1.0, 0.0).astype(BF16)
    col_extra = dot_t(pick, cols[:, D:])
    total = jnp.sum(col_extra[1:2, :]) * (1.0 / 16.0)
    col_usable = col_extra[0:1, :]
    row_usable = rows[:, D : D + 1].astype(F32)
    shape = (8 * 16, 32 * 16)
    r = lax.broadcasted_iota(jnp.int32, shape, 0)
    q = lax.broadcasted_iota(jnp.int32, shape, 1)
    r_text = lax.rem(lax.div(r, 8), 2)
    q_text = lax.rem(lax.div(q, 8), 2)
    same = (lax.div(r, 16) == me) & (lax.div(q, 16) == z * NY + y) & (lax.rem(r, 8) == lax.rem(q, 8))
    used = (row_usable * col_usable > 0.5) & (r_text != q_text)
    sign = jnp.where(same, 1.0, -1.0)
    margin = -sign * logits
    coeff = loss_scale_ref[0] / total
    dlogit = (jnp.where(used, -sign * jax.nn.sigmoid(margin), 0.0) * coeff).astype(BF16)
    grad = logit_mult * jnp.dot(dlogit, col_main, preferred_element_type=F32)
    radial = jnp.sum(row_main.astype(F32) * grad, axis=1, keepdims=True)
    code = code_of(jnp.max(jnp.abs(grad), axis=1, keepdims=True))
    factor = jnp.exp2(TOP - code / CODE)
    digits = whole(grad * factor).astype(jnp.int16)
    radial = whole(radial * factor * (1.0 / 40.0))
    side = lax.broadcasted_iota(jnp.int32, (8 * 16, EXT), 1) < EXT // 2
    side = jnp.where(side, code.astype(jnp.int32), radial).astype(jnp.int16)
    for pair in range(4):
        for half in range(2):
            band = slice(pair * 32, pair * 32 + 32)
            parts[pair, half, :, :H] = digits[band, half * H : half * H + H]
            parts[pair, half, :, H:] = side[band]

    for n, (dx, dc) in enumerate(GROUP):
        tx, tc = lax.rem(x + dx, NX), lax.rem(c + dc, NC)
        src = parts.at[lax.div(tx, 2) * 2 + tc, lax.rem(tx, 2)]
        start(src, landed.at[me], s_part.at[n], r_part.at[n], members[(dx, dc)])

    soft = jnp.maximum(margin, 0.0) + jnp.log1p(jnp.exp(-jnp.abs(margin)))
    loss = jnp.sum(jnp.where(used & (r_text == 0), soft, 0.0), axis=1, keepdims=True)
    loss_group[0] = jnp.broadcast_to(jnp.sum(loss, axis=0, keepdims=True) / total, (8, 128))
    for n, key in enumerate(GROUP):
        start(loss_group.at[0], loss_group.at[n + 1], s_lg.at[n], r_lg.at[n], members[key])

    def opened(packed):
        wide = packed.astype(jnp.int32).astype(F32)
        back = jnp.exp2(wide[:, H : H + 1] / CODE - TOP)
        return wide[:, :H] * back, wide[:, H + EXT // 2 : H + EXT // 2 + 1] * (back * 40.0)

    sum_grad, sum_radial = opened(parts[pair_slot, lo])
    for n, key in enumerate(GROUP):
        slot = slot_of(*sources[key])
        send_to(landed.at[slot], landed.at[slot], s_part.at[n], r_part.at[n], members[key]).wait_recv()
        more_grad, more_radial = opened(landed[slot])
        sum_grad = sum_grad + more_grad
        sum_radial = sum_radial + more_radial
    gp = (sum_grad - unit_own[...] * sum_radial) / norm
    for i in range(16):
        row = (i // 8) * 16 + i % 8
        at = slice(64 * i, 64 * i + 64)
        image_gpre[at, :] = (gp[row : row + 1] / 64.0 * image_pre[at, :]).astype(BF16)
        at = slice(32 * i, 32 * i + 32)
        text_gpre[at, :] = (gp[row + 8 : row + 9] / 32.0 * text_pre[at, :]).astype(BF16)

    def compute(n):
        t = lax.rem(z + ORDER[n], NZ)
        terms[0, t] = jnp.dot(image_t[t], image_gpre[...], preferred_element_type=F32)
        terms[1, t] = jnp.dot(text_t[t], text_gpre[...], preferred_element_type=F32)
        start(terms.at[1 - c, t], sibling.at[t], s_sib.at[n], r_sib.at[n], twin)

    def chunk(n):
        t = lax.rem(z + ORDER[n], NZ)
        send_to(sibling.at[t], sibling.at[t], s_sib.at[n], r_sib.at[n], twin).wait_recv()
        return t

    def ring(step, n, out, inn, send_sem, recv_sem, way, split):
        t = lax.rem(z + ORDER[n], NZ)
        for h in range(SUBS):
            if step == 0 and h != split:
                continue
            at = slice(h * SUB, h * SUB + SUB)
            value = terms[c, t, :, at] + sibling[t, :, at]
            if step > 1 or (step == 1 and h == split):
                send_to(out.at[step - 1, h], inn.at[step - 1, h], send_sem.at[step - 1, h], recv_sem.at[step - 1, h], way).wait_recv()
                value = value + decode(inn[step - 1, h], 16)
            out[step, h] = encode(value, 16)
            start(out.at[step, h], inn.at[step, h], send_sem.at[step, h], recv_sem.at[step, h], way)

    def ring_up(step, n):
        ring(step, n, up_out, up_in, s_rup, r_rup, up, 0)

    def ring_down(step, n):
        ring(step, n, down_out, down_in, s_rdown, r_rdown, down, 1)

    def spread(q):
        values = []
        for n in range(4 * q, 4 * q + 4):
            t = lax.rem(z + ORDER[n], NZ)
            values.append((terms[c, t, :, FAR:] + sibling[t, :, FAR:]).reshape(2 * NY, OWN, REST))
        for i in range(2 * NY):
            wide_out[q, i] = encode(jnp.concatenate([value[i] for value in values], axis=0), 16)
        for n, (dxh, j) in enumerate(YX):
            src = wide_out.at[q, lax.rem(xh + dxh, 2) * NY + lax.rem(y + j, NY)]
            start(src, wide_in.at[q, n], s_wide.at[q, n], r_wide.at[q, n], near[(dxh, j)])

    def collect(q):
        value = decode(wide_out[q, xh * NY + y], 16)
        for n, key in enumerate(YX):
            send_to(wide_in.at[q, n], wide_in.at[q, n], s_wide.at[q, n], r_wide.at[q, n], near[key]).wait_recv()
            value = value + decode(wide_in[q, n], 16)
        for i in range(4):
            k = ORDER[4 * q + i]
            part = value[OWN * i : OWN * i + OWN]
            if k == 0:
                rest_own[...] = part
            else:
                line_out[k - 1] = encode(part, 8)
                start(line_out.at[k - 1], line_in.at[k - 1], s_line.at[k - 1], r_line.at[k - 1], z_peers[k - 1])

    compute(0)
    compute(1)
    chunk(0)
    ring_up(0, 0)
    ring_down(0, 0)
    compute(2)
    compute(3)
    for n, key in enumerate(GROUP):
        send_to(loss_group.at[0], loss_group.at[n + 1], s_lg.at[n], r_lg.at[n], members[key]).wait_recv()
    loss_y[0] = jnp.sum(loss_group[...], axis=0)
    for j in range(1, NY):
        start(loss_y.at[0], loss_y.at[j], s_ly.at[j - 1], r_ly.at[j - 1], y_peers[j - 1])
    chunk(1)
    ring_up(1, 1)
    chunk(2)
    ring_down(1, 2)
    chunk(3)
    spread(0)
    compute(4)
    compute(5)
    for j in range(1, NY):
        send_to(loss_y.at[0], loss_y.at[j], s_ly.at[j - 1], r_ly.at[j - 1], y_peers[j - 1]).wait_recv()
    loss_z[0] = jnp.sum(loss_y[...], axis=0)
    for k in range(1, NZ):
        start(loss_z.at[0], loss_z.at[k], s_lz.at[k - 1], r_lz.at[k - 1], z_peers[k - 1])
    chunk(4)
    ring_up(2, 3)
    ring_down(2, 4)
    compute(6)
    compute(7)
    for n in (5, 6, 7):
        chunk(n)
    spread(1)
    ring_up(3, 5)
    ring_down(3, 6)
    collect(0)
    collect(1)
    for k in range(1, NZ):
        send_to(loss_z.at[0], loss_z.at[k], s_lz.at[k - 1], r_lz.at[k - 1], z_peers[k - 1]).wait_recv()
    loss_out_ref[...] = jnp.sum(loss_z[...], axis=0)
    for copy in copies:
        copy.wait_send()
    del copies[:]
    t = lax.rem(z + ORDER[7], NZ)
    for h in range(SUBS):
        at = slice(h * SUB, h * SUB + SUB)
        value = terms[c, t, :, at] + sibling[t, :, at]
        send_to(up_out.at[3, h], up_in.at[3, h], s_rup.at[3, h], r_rup.at[3, h], up).wait_recv()
        value = value + decode(up_in[3, h], 16)
        send_to(down_out.at[3, h], down_in.at[3, h], s_rdown.at[3, h], r_rdown.at[3, h], down).wait_recv()
        value = (value + decode(down_in[3, h], 16)).reshape(2 * NY, OWN, SUB)
        for i in range(2 * NY):
            near_out[i, :, at] = encode(value[i], 8)
    for n, (dxh, j) in enumerate(YX):
        src = near_out.at[lax.rem(xh + dxh, 2) * NY + lax.rem(y + j, NY)]
        start(src, near_in.at[n], s_near.at[n], r_near.at[n], near[(dxh, j)])
    rest = rest_own[...]
    for k in range(1, NZ):
        send_to(line_in.at[k - 1], line_in.at[k - 1], s_line.at[k - 1], r_line.at[k - 1], z_peers[k - 1]).wait_recv()
        rest = rest + decode(line_in[k - 1], 8)
    final[c, :, FAR:] = rest
    result = decode(near_out[xh * NY + y], 8)
    for n, key in enumerate(YX):
        send_to(near_in.at[n], near_in.at[n], s_near.at[n], r_near.at[n], near[key]).wait_recv()
        result = result + decode(near_in[n], 8)
    final[c, :, :FAR] = result
    start(final.at[c], final.at[c], s_final, r_final, twin)
    send_to(final.at[1 - c], final.at[1 - c], s_final, r_final, twin).wait_recv()
    even = c == 0
    image_out_ref[...] = jnp.where(even, final[0, 0:12, :], final[0, 12:24, :])
    text_out_ref[...] = jnp.where(even, final[1, 0:12, :], final[1, 12:24, :])
    for copy in copies:
        copy.wait_send()


def run_kernel(count, logit_scale, logit_bias, loss_scale, image, text, image_weight, text_weight):
    dma = pltpu.SemaphoreType.DMA
    vmem = pl.BlockSpec(memory_space=pltpu.VMEM)
    smem = pl.BlockSpec(memory_space=pltpu.SMEM)
    anywhere = pl.BlockSpec(memory_space=pl.ANY)
    image_rows, text_rows = image.shape[0], text.shape[0]
    ring = pltpu.VMEM((4, SUBS, ZROWS + 16, SUB), jnp.int16)
    tile = (8, 128)
    return pl.pallas_call(
        kernel,
        out_shape=(
            jax.ShapeDtypeStruct((12, H), F32),
            jax.ShapeDtypeStruct((12, H), F32),
            jax.ShapeDtypeStruct(tile, F32),
        ),
        in_specs=[vmem, smem, smem, smem, anywhere, anywhere, anywhere, anywhere],
        out_specs=(vmem, vmem, vmem),
        scratch_shapes=[
            pltpu.VMEM((D, H), BF16),
            pltpu.VMEM((D, H), BF16),
            pltpu.VMEM((32, H), F32),
            pltpu.VMEM((2, 8, H + EXT), F32),
            pltpu.VMEM((2, 8, H + EXT), F32),
            pltpu.VMEM((4,) + tile, F32),
            pltpu.VMEM((NZ, NY, 16, D + EXT), BF16),
            pltpu.VMEM((8, 16, D + EXT), BF16),
            pltpu.VMEM((4, 2, 32, H + EXT), jnp.int16),
            pltpu.VMEM((8, 32, H + EXT), jnp.int16),
            pltpu.VMEM((32, H), F32),
            pltpu.VMEM((image_rows, D), BF16),
            pltpu.VMEM((text_rows, D), BF16),
            pltpu.VMEM((NZ, ZROWS, image_rows), BF16),
            pltpu.VMEM((NZ, ZROWS, text_rows), BF16),
            pltpu.VMEM((image_rows, H), F32),
            pltpu.VMEM((text_rows, H), F32),
            pltpu.VMEM((image_rows, H), BF16),
            pltpu.VMEM((text_rows, H), BF16),
            pltpu.VMEM((2, NZ, ZROWS, H), F32),
            pltpu.VMEM((NZ, ZROWS, H), F32),
            ring,
            ring,
            ring,
            ring,
            pltpu.VMEM((2 * NY, 32, FAR), jnp.int16),
            pltpu.VMEM((7, 32, FAR), jnp.int16),
            pltpu.VMEM((2, 2 * NY, 112, REST), jnp.int16),
            pltpu.VMEM((2, 7, 112, REST), jnp.int16),
            pltpu.VMEM((7, 32, REST), jnp.int16),
            pltpu.VMEM((7, 32, REST), jnp.int16),
            pltpu.VMEM((OWN, REST), F32),
            pltpu.VMEM((2, OWN, H), F32),
            pltpu.VMEM((8,) + tile, F32),
            pltpu.VMEM((NY,) + tile, F32),
            pltpu.VMEM((NZ,) + tile, F32),
            dma((8,)),
        ]
        + [dma((2,))] * 2
        + [dma((3,))] * 2
        + [dma((7,))] * 2
        + [dma((3,))] * 2
        + [dma((4, 4))] * 4
        + [dma((7,))] * 2
        + [dma((8,))] * 2
        + [dma((4, SUBS))] * 4
        + [dma((7,))] * 2
        + [dma((2, 7))] * 2
        + [dma((7,))] * 2
        + [dma] * 2
        + [dma((7,))] * 2
        + [dma((3,))] * 2
        + [dma((7,))] * 2,
        compiler_params=pltpu.CompilerParams(
            collective_id=1, has_side_effects=True, vmem_limit_bytes=58 * 1024 * 1024
        ),
    )(count, logit_scale, logit_bias, loss_scale, image, text, image_weight, text_weight)


def body(
    image_tokens,
    text_tokens,
    image_weight,
    text_weight,
    logit_scale,
    logit_bias,
    loss_scale,
    valid_count,
):
    count = jnp.broadcast_to(valid_count.astype(F32)[:, None], (8, 128))
    image_grad, text_grad, loss = run_kernel(
        count,
        logit_scale,
        logit_bias,
        loss_scale,
        image_tokens.reshape(-1, D),
        text_tokens.reshape(-1, D),
        image_weight,
        text_weight,
    )
    return (loss[0, 0], image_grad, text_grad)


def solution(mesh):
    placed = (
        P("dp", None, None),
        P("dp", None, None),
        P(None, "mp"),
        P(None, "mp"),
        P(),
        P(),
        P(),
        P("dp"),
    )
    return jax.shard_map(
        body,
        mesh=mesh,
        in_specs=placed,
        out_specs=(P(), P("dp", "mp"), P("dp", "mp")),
        check_vma=False,
    )
```

```python
import jax
import jax.numpy as jnp
from jax import lax
from jax.experimental import pallas as pl
from jax.experimental.pallas import tpu as pltpu
from jax.sharding import PartitionSpec as P

MESH = pl.DeviceIdType.MESH
F32 = jnp.float32
BF16 = jnp.bfloat16
NZ, NY, NX, NC = 8, 4, 4, 2
D = 1536
H = 768
EXT = 128
ZROWS = D // NZ
OWN = 24


def place():
    dp = lax.axis_index("dp")
    lo = lax.axis_index("mp")
    c = lax.rem(dp, 2)
    y = lax.rem(lax.div(dp, 2), 4)
    xh = lax.rem(lax.div(dp, 8), 2)
    z = lax.div(dp, 16)
    return z, y, xh * 2 + lo, c


def device_at(z, y, x, c):
    return (((z * 2 + lax.div(x, 2)) * 4 + y) * 2 + c, lax.rem(x, 2))


def slot_of(x, c):
    return (lax.div(x, 2) * 2 + c) * 2 + lax.rem(x, 2)


def send_to(src, dst, send_sem, recv_sem, device):
    return pltpu.make_async_remote_copy(
        src_ref=src,
        dst_ref=dst,
        send_sem=send_sem,
        recv_sem=recv_sem,
        device_id=device,
        device_id_type=MESH,
    )


def greet(devices):
    barrier = pltpu.get_barrier_semaphore()
    for device in devices:
        pl.semaphore_signal(barrier, inc=1, device_id=device, device_id_type=MESH)
    pl.semaphore_wait(barrier, len(devices))


GROUP = [(dx, dc) for dx in range(NX) for dc in range(NC) if (dx, dc) != (0, 0)]


def dot_t(a, b):
    return lax.dot_general(a, b, (((1,), (1,)), ((), ())), preferred_element_type=F32)


CODE = 256.0
TOP = 14.98
LEAST = 2.0**-100


def code_of(peak):
    return jnp.ceil(jnp.log2(jnp.maximum(peak, LEAST)) * CODE)


def whole(values):
    return jnp.round(values).astype(jnp.int32)


def encode(values, pad):
    code = code_of(jnp.max(jnp.abs(values), axis=0, keepdims=True))
    digits = whole(values * jnp.exp2(TOP - code / CODE))
    codes = jnp.broadcast_to(code.astype(jnp.int32), (pad, values.shape[1]))
    return jnp.concatenate([digits, codes], axis=0).astype(jnp.int16)


def decode(packed, pad):
    wide = packed.astype(jnp.int32).astype(F32)
    rows = packed.shape[0] - pad
    return wide[:rows] * jnp.exp2(wide[rows : rows + 1] / CODE - TOP)


def gelu(x):
    k = 0.7978845608028654
    return 0.5 * x * (1.0 + jnp.tanh(k * x * (1.0 + 0.044715 * (x * x))))


def slope_of(x):
    k = 0.7978845608028654
    x2 = x * x
    t = jnp.tanh(k * x * (1.0 + 0.044715 * x2))
    return 0.5 * (1.0 + t) + 0.5 * x * (1.0 - t * t) * (k * (1.0 + 3.0 * 0.044715 * x2))


YX = [(dxh, j) for dxh in range(2) for j in range(NY) if (dxh, j) != (0, 0)]
PAIRS = [(0, 1), (2, 0), (2, 1)]
ORDER = [4, 3, 5, 2, 6, 1, 7, 0]
SUBS = 3
UPS = 2
SUB = 128
FAR = SUBS * SUB
REST = H - FAR


def kernel(
    count_ref,
    scale_ref,
    bias_ref,
    loss_scale_ref,
    image_ref,
    text_ref,
    image_weight_ref,
    text_weight_ref,
    image_out_ref,
    text_out_ref,
    loss_out_ref,
    image_weight,
    text_weight,
    pooled,
    half_out,
    half_in,
    counts,
    plane,
    upper,
    group,
    parts,
    landed,
    unit_own,
    image_tok,
    text_tok,
    image_t,
    text_t,
    image_pre,
    text_pre,
    image_gpre,
    text_gpre,
    terms,
    sib_out,
    sib_in,
    up_out,
    up_in,
    down_out,
    down_in,
    near_out,
    near_in,
    wide_out,
    wide_in,
    line_out,
    line_in,
    rest_own,
    final,
    loss_group,
    loss_y,
    loss_z,
    s_load,
    s_other,
    r_other,
    s_count,
    r_count,
    s_group,
    r_group,
    s_y,
    r_y,
    s_up,
    r_up,
    s_down,
    r_down,
    s_uz,
    r_uz,
    s_uy,
    r_uy,
    s_part,
    r_part,
    s_sib,
    r_sib,
    s_rup,
    r_rup,
    s_rdown,
    r_rdown,
    s_near,
    r_near,
    s_wide,
    r_wide,
    s_line,
    r_line,
    s_final,
    r_final,
    s_lg,
    r_lg,
    s_ly,
    r_ly,
    s_lz,
    r_lz,
):
    z, y, x, c = place()
    xh, lo = lax.div(x, 2), lax.rem(x, 2)
    me = slot_of(x, c)
    up = device_at(lax.rem(z + 1, NZ), y, x, c)
    down = device_at(lax.rem(z + NZ - 1, NZ), y, x, c)
    members = {(dx, dc): device_at(z, y, lax.rem(x + dx, NX), lax.rem(c + dc, NC)) for dx, dc in GROUP}
    sources = {(dx, dc): (lax.rem(x + NX - dx, NX), lax.rem(c + dc, NC)) for dx, dc in GROUP}
    near = {(dxh, j): device_at(z, lax.rem(y + j, NY), lax.rem(xh + dxh, 2) * 2 + lo, c) for dxh, j in YX}
    y_peers = [near[(0, j)] for j in range(1, NY)]
    z_peers = [device_at(lax.rem(z + k, NZ), y, x, c) for k in range(1, NZ)]
    partner = device_at(z, y, xh * 2 + 1 - lo, c)
    twin = members[(0, 1)]
    copies = []

    def start(*args):
        copy = send_to(*args)
        copy.start()
        copies.append(copy)

    loads = {}

    def fetch(name, src, dst):
        loads[name] = pltpu.make_async_copy(src, dst, s_load.at[len(loads)])
        loads[name].start()

    fetch("tw", text_weight_ref, text_weight)
    for p in range(2):
        at = pl.ds(256 * p, 256)
        fetch("t%d" % p, text_ref.at[at], text_tok.at[at])
    fetch("iw", image_weight_ref, image_weight)
    for p in range(4):
        at = pl.ds(256 * p, 256)
        fetch("i%d" % p, image_ref.at[at], image_tok.at[at])
    peers = [members[key] for key in GROUP] + [near[key] for key in YX if key != (1, 0)] + z_peers
    barrier = pltpu.get_barrier_semaphore()
    for peer in peers:
        pl.semaphore_signal(barrier, inc=1, device_id=peer, device_id_type=MESH)

    columns = pl.ds(pl.multiple_of(lo * H, H), H)

    def forward(tok, weight, pre, p):
        at = slice(256 * p, 256 * p + 256)
        pre[at, :] = jnp.dot(tok[at, :], weight[...], preferred_element_type=F32)

    def pool(tok, pre, p, tokens, offset):
        for i in range(256 // tokens):
            at = slice(256 * p + tokens * i, 256 * p + tokens * i + tokens)
            hidden = tok[at, columns].astype(F32) + gelu(pre[at, :])
            sample = 256 // tokens * p + i
            row = (sample // 8) * 16 + offset + sample % 8
            pooled[row : row + 1, :] = jnp.sum(hidden, axis=0, keepdims=True) * (1.0 / tokens)

    first = lo == 0
    pair_slot = xh * 2 + c

    def swap(w):
        low, high = pooled[8 * w : 8 * w + 8, :], pooled[16 + 8 * w : 24 + 8 * w, :]
        ours = jnp.where(first, low, high)
        squares = jnp.sum(ours * ours, axis=1, keepdims=True)
        half_out[w, :, :H] = jnp.where(first, high, low)
        half_out[w, :, H:] = jnp.broadcast_to(squares, (8, EXT))
        start(half_out.at[w], half_in.at[w], s_other.at[w], r_other.at[w], partner)

    for name in ("tw", "t0"):
        loads[name].wait()
    forward(text_tok, text_weight, text_pre, 0)
    loads["t1"].wait()
    forward(text_tok, text_weight, text_pre, 1)
    pool(text_tok, text_pre, 0, 32, 8)
    for name in ("iw", "i0"):
        loads[name].wait()
    forward(image_tok, image_weight, image_pre, 0)
    pool(text_tok, text_pre, 1, 32, 8)
    pl.semaphore_wait(barrier, len(peers))
    swap(1)
    own_count = jnp.full((8, 128), count_ref[0], jnp.int32).astype(F32)
    counts[pair_slot] = own_count
    for n, key in enumerate(PAIRS):
        start(counts.at[pair_slot], counts.at[pair_slot], s_count.at[n], r_count.at[n], members[key])
    for p in range(1, 4):
        loads["i%d" % p].wait()
        forward(image_tok, image_weight, image_pre, p)
        pool(image_tok, image_pre, p - 1, 64, 0)
    pool(image_tok, image_pre, 3, 64, 0)
    swap(0)
    mine = pooled[...]
    own_sq = jnp.sum(mine * mine, axis=1, keepdims=True)
    own_rows = jnp.where(first, mine[0:16], mine[16:32])
    own_rows_sq = jnp.where(first, own_sq[0:16], own_sq[16:32])
    rest_sq = jnp.where(first, own_sq[16:32], own_sq[0:16])
    for w in range(2):
        send_to(half_out.at[w], half_in.at[w], s_other.at[w], r_other.at[w], partner).wait_recv()
    arrived = half_in[...].reshape(16, H + EXT)
    theirs = arrived[:, :H]
    norm_own = jnp.sqrt(own_rows_sq + jnp.sum(theirs * theirs, axis=1, keepdims=True) + 1e-6)
    norm_rest = jnp.sqrt(rest_sq + arrived[:, H : H + 1] + 1e-6)
    norm = jnp.concatenate(
        [jnp.where(first, norm_own, norm_rest), jnp.where(first, norm_rest, norm_own)], axis=0
    )
    unit_own[...] = mine / norm
    unit_mine = own_rows / norm_own
    unit_theirs = theirs / norm_own
    low = jnp.where(first, unit_mine, unit_theirs)
    high = jnp.where(first, unit_theirs, unit_mine)
    for n, (dx, dc) in enumerate(PAIRS):
        slot = lax.rem(xh + dx // 2, 2) * 2 + lax.rem(c + dc, NC)
        send_to(counts.at[slot], counts.at[slot], s_count.at[n], r_count.at[n], members[(dx, dc)]).wait_recv()
    row_total = jnp.sum(counts[...], axis=0)[0:1, :]
    own_count = own_count[0:1, :]
    sample = lax.rem(lax.broadcasted_iota(jnp.int32, (16, EXT), 0), 8) + 8 * lo
    lane = lax.broadcasted_iota(jnp.int32, (16, EXT), 1)
    usable = jnp.where(sample.astype(F32) < own_count, 1.0, 0.0)
    extra = jnp.where(lane < EXT // 2, usable, jnp.broadcast_to(row_total, (16, EXT)))
    block = jnp.concatenate([low.astype(BF16), high.astype(BF16), extra.astype(BF16)], axis=1)
    plane[z, y] = block[:, :H]
    upper[z, y] = block[:, H:]
    group[me] = block

    def pass_up(step, j, zs, ys):
        start(plane.at[zs, ys], plane.at[zs, ys], s_up.at[step, j], r_up.at[step, j], up)

    def pass_down(step, j, zs, ys):
        start(plane.at[zs, ys], plane.at[zs, ys], s_down.at[step, j], r_down.at[step, j], down)

    def pass_y(k):
        zs = lax.rem(z + k, NZ)
        for j in range(1, NY):
            start(upper.at[zs, y], upper.at[zs, y], s_uy.at[k, j - 1], r_uy.at[k, j - 1], y_peers[j - 1])

    def land_z(k):
        zs = lax.rem(z + k, NZ)
        send_to(upper.at[zs, y], upper.at[zs, y], s_uz.at[NZ - k - 1], r_uz.at[NZ - k - 1], up).wait_recv()
        pass_y(k)

    for j in range(1, NY):
        start(plane.at[z, y], plane.at[z, y], s_y.at[j - 1], r_y.at[j - 1], y_peers[j - 1])
    pass_up(0, 0, z, y)
    pass_down(0, 0, z, y)
    for k in (1, 7, 2, 6, 3, 5, 4):
        start(upper.at[z, y], upper.at[z, y], s_uz.at[k - 1], r_uz.at[k - 1], z_peers[k - 1])
    pass_y(0)
    for n, key in enumerate(GROUP):
        start(group.at[me], group.at[me], s_group.at[n], r_group.at[n], members[key])

    def turn(tok, out, p):
        def work():
            flipped = tok[:, 384 * p : 384 * p + 384].T
            out[2 * p : 2 * p + 2] = flipped.reshape(2, ZROWS, tok.shape[0])

        return work

    def bend(pre, first_row, rows):
        def work():
            @pl.loop(0, rows // 16)
            def _(i):
                at = pl.ds(pl.multiple_of(first_row + i * 16, 16), 16)
                pre[at, :] = slope_of(pre[at, :])

        return work

    pieces = [turn(image_tok, image_t, p) for p in range(4)] + [turn(text_tok, text_t, p) for p in range(4)]
    pieces += [bend(image_pre, 128 * p, 128) for p in range(8)] + [bend(text_pre, 128 * p, 128) for p in range(4)]
    done = [0]

    def idle(amount=1):
        for piece in pieces[done[0] : done[0] + amount]:
            piece()
        done[0] += amount

    for j in range(1, NY):
        ys = lax.rem(y + NY - j, NY)
        send_to(plane.at[z, ys], plane.at[z, ys], s_y.at[j - 1], r_y.at[j - 1], up).wait_recv()
        pass_up(0, j, z, ys)
        pass_down(0, j, z, ys)
    idle()
    for step in range(4):
        for j in range(NY):
            ys = lax.rem(y + NY - j, NY)
            if step < 3 or j < 2:
                zs = lax.rem(z + NZ - step - 1, NZ)
                send_to(plane.at[zs, ys], plane.at[zs, ys], s_up.at[step, j], r_up.at[step, j], up).wait_recv()
                if step < 2 or (step == 2 and j < 2):
                    pass_up(step + 1, j, zs, ys)
            if step < 3 or j >= 2:
                zs = lax.rem(z + step + 1, NZ)
                send_to(plane.at[zs, ys], plane.at[zs, ys], s_down.at[step, j], r_down.at[step, j], down).wait_recv()
                if step < 2 or (step == 2 and j >= 2):
                    pass_down(step + 1, j, zs, ys)
            if step == 0 and j == 0:
                land_z(1)
                land_z(7)
            if step == 0 and j == 2:
                land_z(2)
                land_z(6)
            if step == 1 and j == 0:
                land_z(3)
                land_z(5)
                land_z(4)
            idle(2 if step < 1 else 1)
    idle(len(pieces) - done[0])
    for n, key in enumerate(GROUP):
        slot = slot_of(*sources[key])
        send_to(group.at[slot], group.at[slot], s_group.at[n], r_group.at[n], members[key]).wait_recv()

    for k in range(NZ):
        for j in range(1, NY):
            zs, ys = lax.rem(z + k, NZ), lax.rem(y + NY - j, NY)
            send_to(upper.at[zs, ys], upper.at[zs, ys], s_uy.at[k, j - 1], r_uy.at[k, j - 1], up).wait_recv()

    rows = group[...].reshape(8 * 16, D + EXT)
    low_cols = plane[...].reshape(32 * 16, H)
    high_cols = upper[...].reshape(32 * 16, H + EXT)
    row_main, high_main = rows[:, :D], high_cols[:, :H]
    logit_mult = scale_ref[0]
    products = dot_t(row_main[:, :H], low_cols) + dot_t(row_main[:, H:], high_main)
    logits = logit_mult * products + bias_ref[0]
    pick = lax.broadcasted_iota(jnp.int32, (16, EXT), 0) * (EXT // 2)
    pick = jnp.where(pick == lax.broadcasted_iota(jnp.int32, (16, EXT), 1), 1.0, 0.0).astype(BF16)
    col_extra = dot_t(pick, high_cols[:, H:])
    total = jnp.sum(col_extra[1:2, :]) * (1.0 / 16.0)
    col_usable = col_extra[0:1, :]
    row_usable = rows[:, D : D + 1].astype(F32)
    shape = (8 * 16, 32 * 16)
    r = lax.broadcasted_iota(jnp.int32, shape, 0)
    q = lax.broadcasted_iota(jnp.int32, shape, 1)
    r_text = lax.rem(lax.div(r, 8), 2)
    q_text = lax.rem(lax.div(q, 8), 2)
    same = (lax.div(r, 16) == me) & (lax.div(q, 16) == z * NY + y) & (lax.rem(r, 8) == lax.rem(q, 8))
    used = (row_usable * col_usable > 0.5) & (r_text != q_text)
    sign = jnp.where(same, 1.0, -1.0)
    margin = -sign * logits
    coeff = loss_scale_ref[0] / total
    dlogit = (jnp.where(used, -sign * jax.nn.sigmoid(margin), 0.0) * coeff).astype(BF16)
    grad = logit_mult * jnp.concatenate(
        [jnp.dot(dlogit, cols, preferred_element_type=F32) for cols in (low_cols, high_main)], axis=1
    )
    radial = jnp.sum(row_main.astype(F32) * grad, axis=1, keepdims=True)
    code = code_of(jnp.max(jnp.abs(grad), axis=1, keepdims=True))
    factor = jnp.exp2(TOP - code / CODE)
    digits = whole(grad * factor).astype(jnp.int16)
    radial = whole(radial * factor * (1.0 / 40.0))
    side = lax.broadcasted_iota(jnp.int32, (8 * 16, EXT), 1) < EXT // 2
    side = jnp.where(side, code.astype(jnp.int32), radial).astype(jnp.int16)
    for pair in range(4):
        for half in range(2):
            band = slice(pair * 32, pair * 32 + 32)
            parts[pair, half, :, :H] = digits[band, half * H : half * H + H]
            parts[pair, half, :, H:] = side[band]

    for n, (dx, dc) in enumerate(GROUP):
        tx, tc = lax.rem(x + dx, NX), lax.rem(c + dc, NC)
        src = parts.at[lax.div(tx, 2) * 2 + tc, lax.rem(tx, 2)]
        start(src, landed.at[me], s_part.at[n], r_part.at[n], members[(dx, dc)])

    soft = jnp.maximum(margin, 0.0) + jnp.log1p(jnp.exp(-jnp.abs(margin)))
    loss = jnp.sum(jnp.where(used & (r_text == 0), soft, 0.0), axis=1, keepdims=True)
    loss_group[0] = jnp.broadcast_to(jnp.sum(loss, axis=0, keepdims=True) / total, (8, 128))
    for n, key in enumerate(GROUP):
        start(loss_group.at[0], loss_group.at[n + 1], s_lg.at[n], r_lg.at[n], members[key])

    def opened(packed):
        wide = packed.astype(jnp.int32).astype(F32)
        back = jnp.exp2(wide[:, H : H + 1] / CODE - TOP)
        return wide[:, :H] * back, wide[:, H + EXT // 2 : H + EXT // 2 + 1] * (back * 40.0)

    sum_grad, sum_radial = opened(parts[pair_slot, lo])
    for n, key in enumerate(GROUP):
        slot = slot_of(*sources[key])
        send_to(landed.at[slot], landed.at[slot], s_part.at[n], r_part.at[n], members[key]).wait_recv()
        more_grad, more_radial = opened(landed[slot])
        sum_grad = sum_grad + more_grad
        sum_radial = sum_radial + more_radial
    gp = (sum_grad - unit_own[...] * sum_radial) / norm
    for i in range(16):
        row = (i // 8) * 16 + i % 8
        at = slice(64 * i, 64 * i + 64)
        image_gpre[at, :] = (gp[row : row + 1] / 64.0 * image_pre[at, :]).astype(BF16)
        at = slice(32 * i, 32 * i + 32)
        text_gpre[at, :] = (gp[row + 8 : row + 9] / 32.0 * text_pre[at, :]).astype(BF16)

    def compute(n):
        t = lax.rem(z + ORDER[n], NZ)
        image = jnp.dot(image_t[t], image_gpre[...], preferred_element_type=F32)
        text = jnp.dot(text_t[t], text_gpre[...], preferred_element_type=F32)
        terms[n] = jnp.where(c == 0, image, text)
        sib_out[n] = encode(jnp.where(c == 0, text, image), 16)
        start(sib_out.at[n], sib_in.at[n], s_sib.at[n], r_sib.at[n], twin)

    def chunk(n):
        send_to(sib_out.at[n], sib_in.at[n], s_sib.at[n], r_sib.at[n], twin).wait_recv()
        terms[n] += decode(sib_in[n], 16)

    def ring(step, n, h, out, inn, send_sem, recv_sem, way, early):
        value = terms[n, :, h * SUB : h * SUB + SUB]
        if step > 1 or (step == 1 and early):
            send_to(out.at[step - 1, h], inn.at[step - 1, h], send_sem.at[step - 1, h], recv_sem.at[step - 1, h], way).wait_recv()
            value = value + decode(inn[step - 1, h], 16)
        out[step, h] = encode(value, 16)
        start(out.at[step, h], inn.at[step, h], send_sem.at[step, h], recv_sem.at[step, h], way)

    def ring_step(step, n_up, n_down):
        ups, downs = list(range(UPS)), list(range(UPS, SUBS))
        if step > 0:
            ups, downs = downs + ups, ups + downs
        for i in range(SUBS):
            if i < len(ups):
                ring(step, n_up, ups[i], up_out, up_in, s_rup, r_rup, up, ups[i] < UPS)
            if i < len(downs):
                ring(step, n_down, downs[i], down_out, down_in, s_rdown, r_rdown, down, downs[i] >= UPS)

    def spread(q):
        values = []
        for n in range(4 * q, 4 * q + 4):
            values.append(terms[n, :, FAR:].reshape(2 * NY, OWN, REST))
        for i in range(2 * NY):
            wide_out[q, i] = encode(jnp.concatenate([value[i] for value in values], axis=0), 16)
        for n, (dxh, j) in enumerate(YX):
            src = wide_out.at[q, lax.rem(xh + dxh, 2) * NY + lax.rem(y + j, NY)]
            start(src, wide_in.at[q, n], s_wide.at[q, n], r_wide.at[q, n], near[(dxh, j)])

    def collect(q):
        value = decode(wide_out[q, xh * NY + y], 16)
        for n, key in enumerate(YX):
            send_to(wide_in.at[q, n], wide_in.at[q, n], s_wide.at[q, n], r_wide.at[q, n], near[key]).wait_recv()
            value = value + decode(wide_in[q, n], 16)
        for i in range(4):
            k = ORDER[4 * q + i]
            part = value[OWN * i : OWN * i + OWN]
            if k == 0:
                rest_own[...] = part
            else:
                line_out[k - 1] = encode(part, 8)
                start(line_out.at[k - 1], line_in.at[k - 1], s_line.at[k - 1], r_line.at[k - 1], z_peers[k - 1])

    compute(0)
    compute(1)
    chunk(0)
    ring_step(0, 0, 0)
    compute(2)
    compute(3)
    for n in (1, 2, 3):
        chunk(n)
    spread(0)
    compute(4)
    compute(5)
    ring_step(1, 1, 2)
    compute(6)
    compute(7)
    for n in (4, 5, 6, 7):
        chunk(n)
    spread(1)
    for n, key in enumerate(GROUP):
        send_to(loss_group.at[0], loss_group.at[n + 1], s_lg.at[n], r_lg.at[n], members[key]).wait_recv()
    loss_y[0] = jnp.sum(loss_group[...], axis=0)
    for j in range(1, NY):
        start(loss_y.at[0], loss_y.at[j], s_ly.at[j - 1], r_ly.at[j - 1], y_peers[j - 1])
    ring_step(2, 3, 4)
    collect(0)
    for j in range(1, NY):
        send_to(loss_y.at[0], loss_y.at[j], s_ly.at[j - 1], r_ly.at[j - 1], y_peers[j - 1]).wait_recv()
    loss_z[0] = jnp.sum(loss_y[...], axis=0)
    for k in range(1, NZ):
        start(loss_z.at[0], loss_z.at[k], s_lz.at[k - 1], r_lz.at[k - 1], z_peers[k - 1])
    ring_step(3, 5, 6)
    collect(1)
    for copy in copies:
        copy.wait_send()
    del copies[:]
    for h in range(SUBS):
        at = slice(h * SUB, h * SUB + SUB)
        value = terms[7, :, at]
        send_to(up_out.at[3, h], up_in.at[3, h], s_rup.at[3, h], r_rup.at[3, h], up).wait_recv()
        value = value + decode(up_in[3, h], 16)
        send_to(down_out.at[3, h], down_in.at[3, h], s_rdown.at[3, h], r_rdown.at[3, h], down).wait_recv()
        value = (value + decode(down_in[3, h], 16)).reshape(2 * NY, OWN, SUB)
        for i in range(2 * NY):
            near_out[i, :, at] = encode(value[i], 8)
    for n, (dxh, j) in enumerate(YX):
        src = near_out.at[lax.rem(xh + dxh, 2) * NY + lax.rem(y + j, NY)]
        start(src, near_in.at[n], s_near.at[n], r_near.at[n], near[(dxh, j)])
    rest = rest_own[...]
    for k in range(1, NZ):
        send_to(line_in.at[k - 1], line_in.at[k - 1], s_line.at[k - 1], r_line.at[k - 1], z_peers[k - 1]).wait_recv()
        rest = rest + decode(line_in[k - 1], 8)
    final[c, :, FAR:] = rest
    result = decode(near_out[xh * NY + y], 8)
    for n, key in enumerate(YX):
        send_to(near_in.at[n], near_in.at[n], s_near.at[n], r_near.at[n], near[key]).wait_recv()
        result = result + decode(near_in[n], 8)
    for k in range(1, NZ):
        send_to(loss_z.at[0], loss_z.at[k], s_lz.at[k - 1], r_lz.at[k - 1], z_peers[k - 1]).wait_recv()
    loss_out_ref[...] = jnp.sum(loss_z[...], axis=0)
    final[c, :, :FAR] = result
    start(final.at[c], final.at[c], s_final, r_final, twin)
    send_to(final.at[1 - c], final.at[1 - c], s_final, r_final, twin).wait_recv()
    even = c == 0
    image_out_ref[...] = jnp.where(even, final[0, 0:12, :], final[0, 12:24, :])
    text_out_ref[...] = jnp.where(even, final[1, 0:12, :], final[1, 12:24, :])
    for copy in copies:
        copy.wait_send()


def run_kernel(count, logit_scale, logit_bias, loss_scale, image, text, image_weight, text_weight):
    dma = pltpu.SemaphoreType.DMA
    vmem = pl.BlockSpec(memory_space=pltpu.VMEM)
    smem = pl.BlockSpec(memory_space=pltpu.SMEM)
    anywhere = pl.BlockSpec(memory_space=pltpu.HBM)
    image_rows, text_rows = image.shape[0], text.shape[0]
    ring = pltpu.VMEM((4, SUBS, ZROWS + 16, SUB), jnp.int16)
    tile = (8, 128)
    return pl.pallas_call(
        kernel,
        out_shape=(
            jax.ShapeDtypeStruct((12, H), F32),
            jax.ShapeDtypeStruct((12, H), F32),
            jax.ShapeDtypeStruct(tile, F32),
        ),
        in_specs=[smem, smem, smem, smem, anywhere, anywhere, anywhere, anywhere],
        out_specs=(vmem, vmem, vmem),
        scratch_shapes=[
            pltpu.VMEM((D, H), BF16),
            pltpu.VMEM((D, H), BF16),
            pltpu.VMEM((32, H), F32),
            pltpu.VMEM((2, 8, H + EXT), F32),
            pltpu.VMEM((2, 8, H + EXT), F32),
            pltpu.VMEM((4,) + tile, F32),
            pltpu.VMEM((NZ, NY, 16, H), BF16),
            pltpu.VMEM((NZ, NY, 16, H + EXT), BF16),
            pltpu.VMEM((8, 16, D + EXT), BF16),
            pltpu.VMEM((4, 2, 32, H + EXT), jnp.int16),
            pltpu.VMEM((8, 32, H + EXT), jnp.int16),
            pltpu.VMEM((32, H), F32),
            pltpu.VMEM((image_rows, D), BF16),
            pltpu.VMEM((text_rows, D), BF16),
            pltpu.VMEM((NZ, ZROWS, image_rows), BF16),
            pltpu.VMEM((NZ, ZROWS, text_rows), BF16),
            pltpu.VMEM((image_rows, H), F32),
            pltpu.VMEM((text_rows, H), F32),
            pltpu.VMEM((image_rows, H), BF16),
            pltpu.VMEM((text_rows, H), BF16),
            pltpu.VMEM((NZ, ZROWS, H), F32),
            pltpu.VMEM((NZ, ZROWS + 16, H), jnp.int16),
            pltpu.VMEM((NZ, ZROWS + 16, H), jnp.int16),
            ring,
            ring,
            ring,
            ring,
            pltpu.VMEM((2 * NY, 32, FAR), jnp.int16),
            pltpu.VMEM((7, 32, FAR), jnp.int16),
            pltpu.VMEM((2, 2 * NY, 112, REST), jnp.int16),
            pltpu.VMEM((2, 7, 112, REST), jnp.int16),
            pltpu.VMEM((7, 32, REST), jnp.int16),
            pltpu.VMEM((7, 32, REST), jnp.int16),
            pltpu.VMEM((OWN, REST), F32),
            pltpu.VMEM((2, OWN, H), F32),
            pltpu.VMEM((8,) + tile, F32),
            pltpu.VMEM((NY,) + tile, F32),
            pltpu.VMEM((NZ,) + tile, F32),
            dma((8,)),
        ]
        + [dma((2,))] * 2
        + [dma((3,))] * 2
        + [dma((7,))] * 2
        + [dma((3,))] * 2
        + [dma((4, 4))] * 4
        + [dma((7,))] * 2
        + [dma((NZ, 3))] * 2
        + [dma((7,))] * 2
        + [dma((8,))] * 2
        + [dma((4, SUBS))] * 4
        + [dma((7,))] * 2
        + [dma((2, 7))] * 2
        + [dma((7,))] * 2
        + [dma] * 2
        + [dma((7,))] * 2
        + [dma((3,))] * 2
        + [dma((7,))] * 2,
        compiler_params=pltpu.CompilerParams(
            collective_id=1, has_side_effects=True, vmem_limit_bytes=53 * 1024 * 1024
        ),
    )(count, logit_scale, logit_bias, loss_scale, image, text, image_weight, text_weight)


def body(
    image_tokens,
    text_tokens,
    image_weight,
    text_weight,
    logit_scale,
    logit_bias,
    loss_scale,
    valid_count,
):
    image_grad, text_grad, loss = run_kernel(
        valid_count,
        logit_scale,
        logit_bias,
        loss_scale,
        image_tokens.reshape(-1, D),
        text_tokens.reshape(-1, D),
        image_weight,
        text_weight,
    )
    return (loss[0, 0], image_grad, text_grad)


def solution(mesh):
    placed = (
        P("dp", None, None),
        P("dp", None, None),
        P(None, "mp"),
        P(None, "mp"),
        P(),
        P(),
        P(),
        P("dp"),
    )
    return jax.shard_map(
        body,
        mesh=mesh,
        in_specs=placed,
        out_specs=(P(), P("dp", "mp"), P("dp", "mp")),
        check_vma=False,
    )
```

```python
import jax
import jax.numpy as jnp
from jax import lax
from jax.experimental import pallas as pl
from jax.experimental.pallas import tpu as pltpu
from jax.sharding import PartitionSpec as P

MESH = pl.DeviceIdType.MESH
F32 = jnp.float32
BF16 = jnp.bfloat16
NZ, NY, NX, NC = 8, 4, 4, 2
D = 1536
H = 768
EXT = 128
ZROWS = D // NZ
OWN = 24


def place():
    dp = lax.axis_index("dp")
    lo = lax.axis_index("mp")
    c = lax.rem(dp, 2)
    y = lax.rem(lax.div(dp, 2), 4)
    xh = lax.rem(lax.div(dp, 8), 2)
    z = lax.div(dp, 16)
    return z, y, xh * 2 + lo, c


def device_at(z, y, x, c):
    return (((z * 2 + lax.div(x, 2)) * 4 + y) * 2 + c, lax.rem(x, 2))


def slot_of(x, c):
    return (lax.div(x, 2) * 2 + c) * 2 + lax.rem(x, 2)


def send_to(src, dst, send_sem, recv_sem, device):
    return pltpu.make_async_remote_copy(
        src_ref=src,
        dst_ref=dst,
        send_sem=send_sem,
        recv_sem=recv_sem,
        device_id=device,
        device_id_type=MESH,
    )


def greet(devices):
    barrier = pltpu.get_barrier_semaphore()
    for device in devices:
        pl.semaphore_signal(barrier, inc=1, device_id=device, device_id_type=MESH)
    pl.semaphore_wait(barrier, len(devices))


GROUP = [(dx, dc) for dx in range(NX) for dc in range(NC) if (dx, dc) != (0, 0)]


def dot_t(a, b):
    return lax.dot_general(a, b, (((1,), (1,)), ((), ())), preferred_element_type=F32)


CODE = 256.0
TOP = 14.98
LEAST = 2.0**-100


def code_of(peak):
    return jnp.ceil(jnp.log2(jnp.maximum(peak, LEAST)) * CODE)


def whole(values):
    return jnp.round(values).astype(jnp.int32)


def encode(values, pad):
    code = code_of(jnp.max(jnp.abs(values), axis=0, keepdims=True))
    digits = whole(values * jnp.exp2(TOP - code / CODE))
    codes = jnp.broadcast_to(code.astype(jnp.int32), (pad, values.shape[1]))
    return jnp.concatenate([digits, codes], axis=0).astype(jnp.int16)


def decode(packed, pad):
    wide = packed.astype(jnp.int32).astype(F32)
    rows = packed.shape[0] - pad
    return wide[:rows] * jnp.exp2(wide[rows : rows + 1] / CODE - TOP)


def gelu(x):
    k = 0.7978845608028654
    return 0.5 * x * (1.0 + jnp.tanh(k * x * (1.0 + 0.044715 * (x * x))))


def slope_of(x):
    k = 0.7978845608028654
    x2 = x * x
    t = jnp.tanh(k * x * (1.0 + 0.044715 * x2))
    return 0.5 * (1.0 + t) + 0.5 * x * (1.0 - t * t) * (k * (1.0 + 3.0 * 0.044715 * x2))


YX = [(dxh, j) for dxh in range(2) for j in range(NY) if (dxh, j) != (0, 0)]
PAIRS = [(0, 1), (2, 0), (2, 1)]
LOW = 640
LINE = [0, 1, 3, 2]
ORDER = [4, 3, 5, 2, 6, 1, 7, 0]
SUBS = 4
UPS = 2
SUB = 128
FAR = SUBS * SUB
REST = H - FAR


def kernel(
    count_hbm,
    scale_hbm,
    bias_hbm,
    loss_scale_hbm,
    image_ref,
    text_ref,
    image_weight_ref,
    text_weight_ref,
    image_out_ref,
    text_out_ref,
    loss_out_ref,
    count_ref,
    scale_ref,
    bias_ref,
    loss_scale_ref,
    image_weight,
    text_weight,
    pooled,
    half_out,
    half_in,
    counts,
    plane,
    upper,
    group,
    parts,
    landed,
    unit_own,
    image_tok,
    text_tok,
    image_t,
    text_t,
    image_pre,
    text_pre,
    image_gpre,
    text_gpre,
    terms,
    sib_out,
    sib_in,
    up_out,
    up_in,
    down_out,
    down_in,
    near_out,
    near_in,
    wide_out,
    wide_in,
    line_out,
    line_in,
    rest_own,
    final,
    loss_group,
    loss_y,
    loss_z,
    s_load,
    s_other,
    r_other,
    s_count,
    r_count,
    s_group,
    r_group,
    s_y,
    r_y,
    s_up,
    r_up,
    s_down,
    r_down,
    s_uz,
    r_uz,
    s_uy,
    r_uy,
    s_part,
    r_part,
    s_sib,
    r_sib,
    s_rup,
    r_rup,
    s_rdown,
    r_rdown,
    s_near,
    r_near,
    s_wide,
    r_wide,
    s_line,
    r_line,
    s_final,
    r_final,
    s_lg,
    r_lg,
    s_ly,
    r_ly,
    s_lz,
    r_lz,
):
    z, y, x, c = place()
    xh, lo = lax.div(x, 2), lax.rem(x, 2)
    me = slot_of(x, c)
    up = device_at(lax.rem(z + 1, NZ), y, x, c)
    down = device_at(lax.rem(z + NZ - 1, NZ), y, x, c)
    members = {(dx, dc): device_at(z, y, lax.rem(x + dx, NX), lax.rem(c + dc, NC)) for dx, dc in GROUP}
    sources = {(dx, dc): (lax.rem(x + NX - dx, NX), lax.rem(c + dc, NC)) for dx, dc in GROUP}
    near = {(dxh, j): device_at(z, lax.rem(y + j, NY), lax.rem(xh + dxh, 2) * 2 + lo, c) for dxh, j in YX}
    y_peers = [near[(0, j)] for j in range(1, NY)]
    z_peers = [device_at(lax.rem(z + k, NZ), y, x, c) for k in range(1, NZ)]
    partner = device_at(z, y, xh * 2 + 1 - lo, c)
    twin = members[(0, 1)]
    copies = []

    def start(*args):
        copy = send_to(*args)
        copy.start()
        copies.append(copy)

    loads = {}

    def fetch(name, src, dst):
        loads[name] = pltpu.make_async_copy(src, dst, s_load.at[len(loads)])
        loads[name].start()

    fetch("count", count_hbm, count_ref)
    fetch("scale", scale_hbm, scale_ref)
    fetch("bias", bias_hbm, bias_ref)
    fetch("loss", loss_scale_hbm, loss_scale_ref)
    fetch("tw", text_weight_ref, text_weight)
    for p in range(2):
        at = pl.ds(256 * p, 256)
        fetch("t%d" % p, text_ref.at[at], text_tok.at[at])
    fetch("iw", image_weight_ref, image_weight)
    for p in range(4):
        at = pl.ds(256 * p, 256)
        fetch("i%d" % p, image_ref.at[at], image_tok.at[at])
    peers = [members[key] for key in GROUP] + [near[key] for key in YX if key != (1, 0)] + z_peers
    barrier = pltpu.get_barrier_semaphore()
    for peer in peers:
        pl.semaphore_signal(barrier, inc=1, device_id=peer, device_id_type=MESH)

    columns = pl.ds(pl.multiple_of(lo * H, H), H)

    def forward(tok, weight, pre, p):
        at = slice(256 * p, 256 * p + 256)
        pre[at, :] = jnp.dot(tok[at, :], weight[...], preferred_element_type=F32)

    def pool(tok, pre, p, tokens, offset):
        for i in range(256 // tokens):
            at = slice(256 * p + tokens * i, 256 * p + tokens * i + tokens)
            hidden = tok[at, columns].astype(F32) + gelu(pre[at, :])
            sample = 256 // tokens * p + i
            row = (sample // 8) * 16 + offset + sample % 8
            pooled[row : row + 1, :] = jnp.sum(hidden, axis=0, keepdims=True) * (1.0 / tokens)

    first = lo == 0
    pair_slot = xh * 2 + c

    def swap(w):
        low, high = pooled[8 * w : 8 * w + 8, :], pooled[16 + 8 * w : 24 + 8 * w, :]
        ours = jnp.where(first, low, high)
        squares = jnp.sum(ours * ours, axis=1, keepdims=True)
        half_out[w, :, :H] = jnp.where(first, high, low)
        half_out[w, :, H:] = jnp.broadcast_to(squares, (8, EXT))
        start(half_out.at[w], half_in.at[w], s_other.at[w], r_other.at[w], partner)

    for name in ("tw", "t0"):
        loads[name].wait()
    forward(text_tok, text_weight, text_pre, 0)
    loads["t1"].wait()
    forward(text_tok, text_weight, text_pre, 1)
    pool(text_tok, text_pre, 0, 32, 8)
    for name in ("iw", "i0"):
        loads[name].wait()
    forward(image_tok, image_weight, image_pre, 0)
    pool(text_tok, text_pre, 1, 32, 8)
    pl.semaphore_wait(barrier, len(peers))
    swap(1)
    for name in ("count", "scale", "bias", "loss"):
        loads[name].wait()
    own_count = jnp.full((8, 128), count_ref[0], jnp.int32).astype(F32)
    counts[pair_slot] = own_count
    for n, key in enumerate(PAIRS):
        start(counts.at[pair_slot], counts.at[pair_slot], s_count.at[n], r_count.at[n], members[key])
    for p in range(1, 4):
        loads["i%d" % p].wait()
        forward(image_tok, image_weight, image_pre, p)
        pool(image_tok, image_pre, p - 1, 64, 0)
    pool(image_tok, image_pre, 3, 64, 0)
    swap(0)
    mine = pooled[...]
    own_sq = jnp.sum(mine * mine, axis=1, keepdims=True)
    own_rows = jnp.where(first, mine[0:16], mine[16:32])
    own_rows_sq = jnp.where(first, own_sq[0:16], own_sq[16:32])
    rest_sq = jnp.where(first, own_sq[16:32], own_sq[0:16])
    for w in range(2):
        send_to(half_out.at[w], half_in.at[w], s_other.at[w], r_other.at[w], partner).wait_recv()
    arrived = half_in[...].reshape(16, H + EXT)
    theirs = arrived[:, :H]
    norm_own = jnp.sqrt(own_rows_sq + jnp.sum(theirs * theirs, axis=1, keepdims=True) + 1e-6)
    norm_rest = jnp.sqrt(rest_sq + arrived[:, H : H + 1] + 1e-6)
    norm = jnp.concatenate(
        [jnp.where(first, norm_own, norm_rest), jnp.where(first, norm_rest, norm_own)], axis=0
    )
    unit_own[...] = mine / norm
    unit_mine = own_rows / norm_own
    unit_theirs = theirs / norm_own
    low = jnp.where(first, unit_mine, unit_theirs)
    high = jnp.where(first, unit_theirs, unit_mine)
    for n, (dx, dc) in enumerate(PAIRS):
        slot = lax.rem(xh + dx // 2, 2) * 2 + lax.rem(c + dc, NC)
        send_to(counts.at[slot], counts.at[slot], s_count.at[n], r_count.at[n], members[(dx, dc)]).wait_recv()
    row_total = jnp.sum(counts[...], axis=0)[0:1, :]
    own_count = own_count[0:1, :]
    sample = lax.rem(lax.broadcasted_iota(jnp.int32, (16, EXT), 0), 8) + 8 * lo
    lane = lax.broadcasted_iota(jnp.int32, (16, EXT), 1)
    usable = jnp.where(sample.astype(F32) < own_count, 1.0, 0.0)
    extra = jnp.where(lane < EXT // 2, usable, jnp.broadcast_to(row_total, (16, EXT)))
    block = jnp.concatenate([low.astype(BF16), high.astype(BF16), extra.astype(BF16)], axis=1)
    plane[z, y] = block[:, :LOW]
    upper[z, y] = block[:, LOW:]
    group[me] = block

    def pass_up(far, j, zs, ys, hops):
        start(plane.at[zs, ys], plane.at[zs, ys], s_up.at[far, j], r_up.at[far, j], z_peers[hops - 1])

    def pass_down(far, j, zs, ys, hops):
        start(plane.at[zs, ys], plane.at[zs, ys], s_down.at[far, j], r_down.at[far, j], z_peers[NZ - hops - 1])

    def send_line(j, ys):
        for hops in (2, 1):
            pass_up(hops - 1, j, z, ys, hops)
            pass_down(hops - 1, j, z, ys, hops)

    def land_up(far, j):
        zs, ys = lax.rem(z + NZ - far - 1, NZ), lax.rem(y + NY - j, NY)
        send_to(plane.at[zs, ys], plane.at[zs, ys], s_up.at[far, j], r_up.at[far, j], up).wait_recv()
        if far == 1:
            if j < 2:
                pass_up(3, j, zs, ys, 2)
            pass_up(2, j, zs, ys, 1)

    def land_down(far, j):
        zs, ys = lax.rem(z + far + 1, NZ), lax.rem(y + NY - j, NY)
        send_to(plane.at[zs, ys], plane.at[zs, ys], s_down.at[far, j], r_down.at[far, j], down).wait_recv()
        if far == 1:
            if j >= 2:
                pass_down(3, j, zs, ys, 2)
            pass_down(2, j, zs, ys, 1)

    def pass_y(k):
        zs = lax.rem(z + k, NZ)
        for j in range(1, NY):
            start(upper.at[zs, y], upper.at[zs, y], s_uy.at[k, j - 1], r_uy.at[k, j - 1], y_peers[j - 1])

    def send_z(k, n, way):
        zs = lax.rem(z + k, NZ)
        start(upper.at[zs, y], upper.at[zs, y], s_uz.at[n], r_uz.at[n], way)

    def land_z(k):
        zs = lax.rem(z + k, NZ)
        send_to(upper.at[zs, y], upper.at[zs, y], s_uz.at[NZ - k - 1], r_uz.at[NZ - k - 1], up).wait_recv()
        if k < 3:
            send_z(k, NZ - k - 2, down)
        if k > 5:
            send_z(k, NZ - k, up)
        pass_y(k)

    for j in range(1, NY):
        start(plane.at[z, y], plane.at[z, y], s_y.at[j - 1], r_y.at[j - 1], y_peers[j - 1])
    send_line(0, y)
    send_z(0, 0, up)
    send_z(0, 6, down)
    send_z(0, 3, z_peers[3])
    pass_y(0)
    for n, key in enumerate(GROUP):
        start(group.at[me], group.at[me], s_group.at[n], r_group.at[n], members[key])

    def turn(tok, out, p):
        def work():
            flipped = tok[:, 384 * p : 384 * p + 384].T
            out[2 * p : 2 * p + 2] = flipped.reshape(2, ZROWS, tok.shape[0])

        return work

    def bend(pre, first_row, rows):
        def work():
            @pl.loop(0, rows // 16)
            def _(i):
                at = pl.ds(pl.multiple_of(first_row + i * 16, 16), 16)
                pre[at, :] = slope_of(pre[at, :])

        return work

    pieces = [turn(image_tok, image_t, p) for p in range(4)] + [turn(text_tok, text_t, p) for p in range(4)]
    pieces += [bend(image_pre, 128 * p, 128) for p in range(8)] + [bend(text_pre, 128 * p, 128) for p in range(4)]
    done = [0]

    def idle(amount=1):
        for piece in pieces[done[0] : done[0] + amount]:
            piece()
        done[0] += amount

    for j in LINE[1:]:
        ys = lax.rem(y + NY - j, NY)
        send_to(plane.at[z, ys], plane.at[z, ys], s_y.at[j - 1], r_y.at[j - 1], up).wait_recv()
        send_line(j, ys)
    land_z(1)
    land_z(7)
    idle()
    for i, j in enumerate(LINE):
        land_up(1, j)
        land_down(1, j)
        idle()
        if i == 0:
            land_z(2)
            land_z(6)
        idle()
        if i == 2:
            land_z(3)
            land_z(5)
            land_z(4)
        idle()
    for far in (0, 2, 3):
        for j in LINE:
            if far < 3 or j < 2:
                land_up(far, j)
            if far < 3 or j >= 2:
                land_down(far, j)
            idle()
    idle(len(pieces) - done[0])
    for n, key in enumerate(GROUP):
        slot = slot_of(*sources[key])
        send_to(group.at[slot], group.at[slot], s_group.at[n], r_group.at[n], members[key]).wait_recv()

    for k in range(NZ):
        for j in range(1, NY):
            zs, ys = lax.rem(z + k, NZ), lax.rem(y + NY - j, NY)
            send_to(upper.at[zs, ys], upper.at[zs, ys], s_uy.at[k, j - 1], r_uy.at[k, j - 1], up).wait_recv()

    rows = group[...].reshape(8 * 16, D + EXT)
    low_cols = plane[...].reshape(32 * 16, LOW)
    high_cols = upper[...].reshape(32 * 16, D - LOW + EXT)
    row_main, high_main = rows[:, :D], high_cols[:, : D - LOW]
    logit_mult = scale_ref[0]
    products = dot_t(row_main[:, :LOW], low_cols) + dot_t(row_main[:, LOW:], high_main)
    logits = logit_mult * products + bias_ref[0]
    pick = lax.broadcasted_iota(jnp.int32, (16, EXT), 0) * (EXT // 2)
    pick = jnp.where(pick == lax.broadcasted_iota(jnp.int32, (16, EXT), 1), 1.0, 0.0).astype(BF16)
    col_extra = dot_t(pick, high_cols[:, D - LOW :])
    total = jnp.sum(col_extra[1:2, :]) * (1.0 / 16.0)
    col_usable = col_extra[0:1, :]
    row_usable = rows[:, D : D + 1].astype(F32)
    shape = (8 * 16, 32 * 16)
    r = lax.broadcasted_iota(jnp.int32, shape, 0)
    q = lax.broadcasted_iota(jnp.int32, shape, 1)
    r_text = lax.rem(lax.div(r, 8), 2)
    q_text = lax.rem(lax.div(q, 8), 2)
    same = (lax.div(r, 16) == me) & (lax.div(q, 16) == z * NY + y) & (lax.rem(r, 8) == lax.rem(q, 8))
    used = (row_usable * col_usable > 0.5) & (r_text != q_text)
    sign = jnp.where(same, 1.0, -1.0)
    margin = -sign * logits
    coeff = loss_scale_ref[0] / total
    dlogit = (jnp.where(used, -sign * jax.nn.sigmoid(margin), 0.0) * coeff).astype(BF16)
    grad = logit_mult * jnp.concatenate(
        [jnp.dot(dlogit, cols, preferred_element_type=F32) for cols in (low_cols, high_main)], axis=1
    )
    radial = jnp.sum(row_main.astype(F32) * grad, axis=1, keepdims=True)
    code = code_of(jnp.max(jnp.abs(grad), axis=1, keepdims=True))
    factor = jnp.exp2(TOP - code / CODE)
    digits = whole(grad * factor).astype(jnp.int16)
    radial = whole(radial * factor * (1.0 / 40.0))
    side = lax.broadcasted_iota(jnp.int32, (8 * 16, EXT), 1) < EXT // 2
    side = jnp.where(side, code.astype(jnp.int32), radial).astype(jnp.int16)
    for pair in range(4):
        for half in range(2):
            band = slice(pair * 32, pair * 32 + 32)
            parts[pair, half, :, :H] = digits[band, half * H : half * H + H]
            parts[pair, half, :, H:] = side[band]

    for n, (dx, dc) in enumerate(GROUP):
        tx, tc = lax.rem(x + dx, NX), lax.rem(c + dc, NC)
        src = parts.at[lax.div(tx, 2) * 2 + tc, lax.rem(tx, 2)]
        start(src, landed.at[me], s_part.at[n], r_part.at[n], members[(dx, dc)])

    soft = jnp.maximum(margin, 0.0) + jnp.log1p(jnp.exp(-jnp.abs(margin)))
    loss = jnp.sum(jnp.where(used & (r_text == 0), soft, 0.0), axis=1, keepdims=True)
    loss_group[0] = jnp.broadcast_to(jnp.sum(loss, axis=0, keepdims=True) / total, (8, 128))
    for n, key in enumerate(GROUP):
        start(loss_group.at[0], loss_group.at[n + 1], s_lg.at[n], r_lg.at[n], members[key])

    def opened(packed):
        wide = packed.astype(jnp.int32).astype(F32)
        back = jnp.exp2(wide[:, H : H + 1] / CODE - TOP)
        return wide[:, :H] * back, wide[:, H + EXT // 2 : H + EXT // 2 + 1] * (back * 40.0)

    sum_grad, sum_radial = opened(parts[pair_slot, lo])
    for n, key in enumerate(GROUP):
        slot = slot_of(*sources[key])
        send_to(landed.at[slot], landed.at[slot], s_part.at[n], r_part.at[n], members[key]).wait_recv()
        more_grad, more_radial = opened(landed[slot])
        sum_grad = sum_grad + more_grad
        sum_radial = sum_radial + more_radial
    gp = (sum_grad - unit_own[...] * sum_radial) / norm
    for i in range(16):
        row = (i // 8) * 16 + i % 8
        at = slice(64 * i, 64 * i + 64)
        image_gpre[at, :] = (gp[row : row + 1] / 64.0 * image_pre[at, :]).astype(BF16)
        at = slice(32 * i, 32 * i + 32)
        text_gpre[at, :] = (gp[row + 8 : row + 9] / 32.0 * text_pre[at, :]).astype(BF16)

    def compute(n):
        t = lax.rem(z + ORDER[n], NZ)
        image = jnp.dot(image_t[t], image_gpre[...], preferred_element_type=F32)
        text = jnp.dot(text_t[t], text_gpre[...], preferred_element_type=F32)
        terms[n] = jnp.where(c == 0, image, text)
        sib_out[n] = encode(jnp.where(c == 0, text, image), 16)
        start(sib_out.at[n], sib_in.at[n], s_sib.at[n], r_sib.at[n], twin)

    def chunk(n):
        send_to(sib_out.at[n], sib_in.at[n], s_sib.at[n], r_sib.at[n], twin).wait_recv()
        terms[n] += decode(sib_in[n], 16)

    def ring(step, n, h, out, inn, send_sem, recv_sem, way, early):
        value = terms[n, :, h * SUB : h * SUB + SUB]
        if step > 1 or (step == 1 and early):
            send_to(out.at[step - 1, h], inn.at[step - 1, h], send_sem.at[step - 1, h], recv_sem.at[step - 1, h], way).wait_recv()
            value = value + decode(inn[step - 1, h], 16)
        out[step, h] = encode(value, 16)
        start(out.at[step, h], inn.at[step, h], send_sem.at[step, h], recv_sem.at[step, h], way)

    def ring_step(step, n_up, n_down):
        ups, downs = list(range(UPS)), list(range(UPS, SUBS))
        if step > 0:
            ups, downs = downs + ups, ups + downs
        for i in range(SUBS):
            if i < len(ups):
                ring(step, n_up, ups[i], up_out, up_in, s_rup, r_rup, up, ups[i] < UPS)
            if i < len(downs):
                ring(step, n_down, downs[i], down_out, down_in, s_rdown, r_rdown, down, downs[i] >= UPS)

    def spread(q):
        values = []
        for n in range(4 * q, 4 * q + 4):
            values.append(terms[n, :, FAR:].reshape(2 * NY, OWN, REST))
        for i in range(2 * NY):
            wide_out[q, i] = encode(jnp.concatenate([value[i] for value in values], axis=0), 16)
        for n, (dxh, j) in enumerate(YX):
            src = wide_out.at[q, lax.rem(xh + dxh, 2) * NY + lax.rem(y + j, NY)]
            start(src, wide_in.at[q, n], s_wide.at[q, n], r_wide.at[q, n], near[(dxh, j)])

    def collect(q):
        value = decode(wide_out[q, xh * NY + y], 16)
        for n, key in enumerate(YX):
            send_to(wide_in.at[q, n], wide_in.at[q, n], s_wide.at[q, n], r_wide.at[q, n], near[key]).wait_recv()
            value = value + decode(wide_in[q, n], 16)
        for i in range(4):
            k = ORDER[4 * q + i]
            part = value[OWN * i : OWN * i + OWN]
            if k == 0:
                rest_own[...] = part
            else:
                line_out[k - 1] = encode(part, 8)
                start(line_out.at[k - 1], line_in.at[k - 1], s_line.at[k - 1], r_line.at[k - 1], z_peers[k - 1])

    compute(0)
    compute(1)
    chunk(0)
    ring_step(0, 0, 0)
    compute(2)
    compute(3)
    for n in (1, 2, 3):
        chunk(n)
    spread(0)
    compute(4)
    compute(5)
    ring_step(1, 1, 2)
    compute(6)
    compute(7)
    for n in (4, 5, 6, 7):
        chunk(n)
    spread(1)
    for n, key in enumerate(GROUP):
        send_to(loss_group.at[0], loss_group.at[n + 1], s_lg.at[n], r_lg.at[n], members[key]).wait_recv()
    loss_y[0] = jnp.sum(loss_group[...], axis=0)
    for j in range(1, NY):
        start(loss_y.at[0], loss_y.at[j], s_ly.at[j - 1], r_ly.at[j - 1], y_peers[j - 1])
    ring_step(2, 3, 4)
    collect(0)
    for j in range(1, NY):
        send_to(loss_y.at[0], loss_y.at[j], s_ly.at[j - 1], r_ly.at[j - 1], y_peers[j - 1]).wait_recv()
    loss_z[0] = jnp.sum(loss_y[...], axis=0)
    for k in range(1, NZ):
        start(loss_z.at[0], loss_z.at[k], s_lz.at[k - 1], r_lz.at[k - 1], z_peers[k - 1])
    ring_step(3, 5, 6)
    collect(1)
    for copy in copies:
        copy.wait_send()
    del copies[:]
    for h in range(SUBS):
        at = slice(h * SUB, h * SUB + SUB)
        value = terms[7, :, at]
        send_to(up_out.at[3, h], up_in.at[3, h], s_rup.at[3, h], r_rup.at[3, h], up).wait_recv()
        value = value + decode(up_in[3, h], 16)
        send_to(down_out.at[3, h], down_in.at[3, h], s_rdown.at[3, h], r_rdown.at[3, h], down).wait_recv()
        value = (value + decode(down_in[3, h], 16)).reshape(2 * NY, OWN, SUB)
        for i in range(2 * NY):
            near_out[i, :, at] = encode(value[i], 8)
    for n, (dxh, j) in enumerate(YX):
        src = near_out.at[lax.rem(xh + dxh, 2) * NY + lax.rem(y + j, NY)]
        start(src, near_in.at[n], s_near.at[n], r_near.at[n], near[(dxh, j)])
    rest = rest_own[...]
    for k in range(1, NZ):
        send_to(line_in.at[k - 1], line_in.at[k - 1], s_line.at[k - 1], r_line.at[k - 1], z_peers[k - 1]).wait_recv()
        rest = rest + decode(line_in[k - 1], 8)
    final[c, :, FAR:] = rest
    result = decode(near_out[xh * NY + y], 8)
    for n, key in enumerate(YX):
        send_to(near_in.at[n], near_in.at[n], s_near.at[n], r_near.at[n], near[key]).wait_recv()
        result = result + decode(near_in[n], 8)
    for k in range(1, NZ):
        send_to(loss_z.at[0], loss_z.at[k], s_lz.at[k - 1], r_lz.at[k - 1], z_peers[k - 1]).wait_recv()
    loss_out_ref[...] = jnp.sum(loss_z[...], axis=0)
    final[c, :, :FAR] = result
    start(final.at[c], final.at[c], s_final, r_final, twin)
    send_to(final.at[1 - c], final.at[1 - c], s_final, r_final, twin).wait_recv()
    even = c == 0
    image_out_ref[...] = jnp.where(even, final[0, 0:12, :], final[0, 12:24, :])
    text_out_ref[...] = jnp.where(even, final[1, 0:12, :], final[1, 12:24, :])
    for copy in copies:
        copy.wait_send()


def run_kernel(count, logit_scale, logit_bias, loss_scale, image, text, image_weight, text_weight):
    dma = pltpu.SemaphoreType.DMA
    vmem = pl.BlockSpec(memory_space=pltpu.VMEM)
    anywhere = pl.BlockSpec(memory_space=pltpu.HBM)
    image_rows, text_rows = image.shape[0], text.shape[0]
    ring = pltpu.VMEM((4, SUBS, ZROWS + 16, SUB), jnp.int16)
    tile = (8, 128)
    return pl.pallas_call(
        kernel,
        out_shape=(
            jax.ShapeDtypeStruct((12, H), F32),
            jax.ShapeDtypeStruct((12, H), F32),
            jax.ShapeDtypeStruct(tile, F32),
        ),
        in_specs=[anywhere, anywhere, anywhere, anywhere, anywhere, anywhere, anywhere, anywhere],
        out_specs=(vmem, vmem, vmem),
        scratch_shapes=[
            pltpu.SMEM((1,), jnp.int32),
            pltpu.SMEM((1,), F32),
            pltpu.SMEM((1,), F32),
            pltpu.SMEM((1,), F32),
            pltpu.VMEM((D, H), BF16),
            pltpu.VMEM((D, H), BF16),
            pltpu.VMEM((32, H), F32),
            pltpu.VMEM((2, 8, H + EXT), F32),
            pltpu.VMEM((2, 8, H + EXT), F32),
            pltpu.VMEM((4,) + tile, F32),
            pltpu.VMEM((NZ, NY, 16, LOW), BF16),
            pltpu.VMEM((NZ, NY, 16, D - LOW + EXT), BF16),
            pltpu.VMEM((8, 16, D + EXT), BF16),
            pltpu.VMEM((4, 2, 32, H + EXT), jnp.int16),
            pltpu.VMEM((8, 32, H + EXT), jnp.int16),
            pltpu.VMEM((32, H), F32),
            pltpu.VMEM((image_rows, D), BF16),
            pltpu.VMEM((text_rows, D), BF16),
            pltpu.VMEM((NZ, ZROWS, image_rows), BF16),
            pltpu.VMEM((NZ, ZROWS, text_rows), BF16),
            pltpu.VMEM((image_rows, H), F32),
            pltpu.VMEM((text_rows, H), F32),
            pltpu.VMEM((image_rows, H), BF16),
            pltpu.VMEM((text_rows, H), BF16),
            pltpu.VMEM((NZ, ZROWS, H), F32),
            pltpu.VMEM((NZ, ZROWS + 16, H), jnp.int16),
            pltpu.VMEM((NZ, ZROWS + 16, H), jnp.int16),
            ring,
            ring,
            ring,
            ring,
            pltpu.VMEM((2 * NY, 32, FAR), jnp.int16),
            pltpu.VMEM((7, 32, FAR), jnp.int16),
            pltpu.VMEM((2, 2 * NY, 112, REST), jnp.int16),
            pltpu.VMEM((2, 7, 112, REST), jnp.int16),
            pltpu.VMEM((7, 32, REST), jnp.int16),
            pltpu.VMEM((7, 32, REST), jnp.int16),
            pltpu.VMEM((OWN, REST), F32),
            pltpu.VMEM((2, OWN, H), F32),
            pltpu.VMEM((8,) + tile, F32),
            pltpu.VMEM((NY,) + tile, F32),
            pltpu.VMEM((NZ,) + tile, F32),
            dma((12,)),
        ]
        + [dma((2,))] * 2
        + [dma((3,))] * 2
        + [dma((7,))] * 2
        + [dma((3,))] * 2
        + [dma((4, 4))] * 4
        + [dma((7,))] * 2
        + [dma((NZ, 3))] * 2
        + [dma((7,))] * 2
        + [dma((8,))] * 2
        + [dma((4, SUBS))] * 4
        + [dma((7,))] * 2
        + [dma((2, 7))] * 2
        + [dma((7,))] * 2
        + [dma] * 2
        + [dma((7,))] * 2
        + [dma((3,))] * 2
        + [dma((7,))] * 2,
        compiler_params=pltpu.CompilerParams(
            collective_id=1, has_side_effects=True, vmem_limit_bytes=53 * 1024 * 1024
        ),
    )(count, logit_scale, logit_bias, loss_scale, image, text, image_weight, text_weight)


def body(
    image_tokens,
    text_tokens,
    image_weight,
    text_weight,
    logit_scale,
    logit_bias,
    loss_scale,
    valid_count,
):
    image_grad, text_grad, loss = run_kernel(
        valid_count,
        logit_scale,
        logit_bias,
        loss_scale,
        image_tokens.reshape(-1, D),
        text_tokens.reshape(-1, D),
        image_weight,
        text_weight,
    )
    return (loss[0, 0], image_grad, text_grad)


def solution(mesh):
    placed = (
        P("dp", None, None),
        P("dp", None, None),
        P(None, "mp"),
        P(None, "mp"),
        P(),
        P(),
        P(),
        P("dp"),
    )
    return jax.shard_map(
        body,
        mesh=mesh,
        in_specs=placed,
        out_specs=(P(), P("dp", "mp"), P("dp", "mp")),
        check_vma=False,
    )
```

```python
import jax
import jax.numpy as jnp
from jax import lax
from jax.experimental import pallas as pl
from jax.experimental.pallas import tpu as pltpu
from jax.sharding import PartitionSpec as P

MESH = pl.DeviceIdType.MESH
F32 = jnp.float32
BF16 = jnp.bfloat16
NZ, NY, NX, NC = 8, 4, 4, 2
D = 1536
H = 768
EXT = 128
ZROWS = D // NZ
OWN = 24


def place():
    dp = lax.axis_index("dp")
    lo = lax.axis_index("mp")
    c = lax.rem(dp, 2)
    y = lax.rem(lax.div(dp, 2), 4)
    xh = lax.rem(lax.div(dp, 8), 2)
    z = lax.div(dp, 16)
    return z, y, xh * 2 + lo, c


def device_at(z, y, x, c):
    return (((z * 2 + lax.div(x, 2)) * 4 + y) * 2 + c, lax.rem(x, 2))


def slot_of(x, c):
    return (lax.div(x, 2) * 2 + c) * 2 + lax.rem(x, 2)


def send_to(src, dst, send_sem, recv_sem, device):
    return pltpu.make_async_remote_copy(
        src_ref=src,
        dst_ref=dst,
        send_sem=send_sem,
        recv_sem=recv_sem,
        device_id=device,
        device_id_type=MESH,
    )


def greet(devices):
    barrier = pltpu.get_barrier_semaphore()
    for device in devices:
        pl.semaphore_signal(barrier, inc=1, device_id=device, device_id_type=MESH)
    pl.semaphore_wait(barrier, len(devices))


GROUP = [(dx, dc) for dx in range(NX) for dc in range(NC) if (dx, dc) != (0, 0)]


def dot_t(a, b):
    return lax.dot_general(a, b, (((1,), (1,)), ((), ())), preferred_element_type=F32)


CODE = 256.0
TOP = 14.98
LEAST = 2.0**-100


def code_of(peak):
    return jnp.ceil(jnp.log2(jnp.maximum(peak, LEAST)) * CODE)


def whole(values):
    return jnp.round(values).astype(jnp.int32)


def encode(values, pad):
    code = code_of(jnp.max(jnp.abs(values), axis=0, keepdims=True))
    digits = whole(values * jnp.exp2(TOP - code / CODE))
    codes = jnp.broadcast_to(code.astype(jnp.int32), (pad, values.shape[1]))
    return jnp.concatenate([digits, codes], axis=0).astype(jnp.int16)


def decode(packed, pad):
    wide = packed.astype(jnp.int32).astype(F32)
    rows = packed.shape[0] - pad
    return wide[:rows] * jnp.exp2(wide[rows : rows + 1] / CODE - TOP)


def gelu(x):
    k = 0.7978845608028654
    return 0.5 * x * (1.0 + jnp.tanh(k * x * (1.0 + 0.044715 * (x * x))))


def slope_of(x):
    k = 0.7978845608028654
    x2 = x * x
    t = jnp.tanh(k * x * (1.0 + 0.044715 * x2))
    return 0.5 * (1.0 + t) + 0.5 * x * (1.0 - t * t) * (k * (1.0 + 3.0 * 0.044715 * x2))


YX = [(dxh, j) for dxh in range(2) for j in range(NY) if (dxh, j) != (0, 0)]
PAIRS = [(0, 1), (2, 0), (2, 1)]
LOW = 512
LINE = [0, 1, 3, 2]
ORDER = [4, 3, 5, 2, 6, 1, 7, 0]
SUBS = 4
UPS = 2
SUB = 128
FAR = SUBS * SUB
REST = H - FAR


def kernel(
    scalars_ref,
    image_ref,
    text_ref,
    image_weight_ref,
    text_weight_ref,
    image_out_ref,
    text_out_ref,
    loss_out_ref,
    image_weight,
    text_weight,
    pooled,
    half_out,
    half_in,
    counts,
    plane,
    upper,
    group,
    parts,
    landed,
    unit_own,
    image_tok,
    text_tok,
    image_t,
    text_t,
    image_pre,
    text_pre,
    image_gpre,
    text_gpre,
    terms,
    sib_out,
    sib_in,
    up_out,
    up_in,
    down_out,
    down_in,
    near_out,
    near_in,
    wide_out,
    wide_in,
    line_out,
    line_in,
    rest_own,
    final,
    loss_group,
    loss_y,
    loss_z,
    s_load,
    s_other,
    r_other,
    s_count,
    r_count,
    s_group,
    r_group,
    s_y,
    r_y,
    s_up,
    r_up,
    s_down,
    r_down,
    s_uz,
    r_uz,
    s_uy,
    r_uy,
    s_part,
    r_part,
    s_sib,
    r_sib,
    s_rup,
    r_rup,
    s_rdown,
    r_rdown,
    s_near,
    r_near,
    s_wide,
    r_wide,
    s_line,
    r_line,
    s_final,
    r_final,
    s_lg,
    r_lg,
    s_ly,
    r_ly,
    s_lz,
    r_lz,
):
    z, y, x, c = place()
    xh, lo = lax.div(x, 2), lax.rem(x, 2)
    me = slot_of(x, c)
    up = device_at(lax.rem(z + 1, NZ), y, x, c)
    down = device_at(lax.rem(z + NZ - 1, NZ), y, x, c)
    members = {(dx, dc): device_at(z, y, lax.rem(x + dx, NX), lax.rem(c + dc, NC)) for dx, dc in GROUP}
    sources = {(dx, dc): (lax.rem(x + NX - dx, NX), lax.rem(c + dc, NC)) for dx, dc in GROUP}
    near = {(dxh, j): device_at(z, lax.rem(y + j, NY), lax.rem(xh + dxh, 2) * 2 + lo, c) for dxh, j in YX}
    y_peers = [near[(0, j)] for j in range(1, NY)]
    z_peers = [device_at(lax.rem(z + k, NZ), y, x, c) for k in range(1, NZ)]
    partner = device_at(z, y, xh * 2 + 1 - lo, c)
    twin = members[(0, 1)]
    copies = []

    def flush(sent):
        for copy in sent:
            copy.wait_send()

    def start(*args):
        copy = send_to(*args)
        copy.start()
        copies.append(copy)

    loads = {}

    def fetch(name, src, dst):
        loads[name] = pltpu.make_async_copy(src, dst, s_load.at[len(loads)])
        loads[name].start()

    fetch("tw", text_weight_ref, text_weight)
    for p in range(2):
        at = pl.ds(256 * p, 256)
        fetch("t%d" % p, text_ref.at[at], text_tok.at[at])
    fetch("iw", image_weight_ref, image_weight)
    for p in range(4):
        at = pl.ds(256 * p, 256)
        fetch("i%d" % p, image_ref.at[at], image_tok.at[at])
    peers = [members[key] for key in GROUP] + [near[key] for key in YX if key != (1, 0)] + z_peers
    barrier = pltpu.get_barrier_semaphore()
    for peer in peers:
        pl.semaphore_signal(barrier, inc=1, device_id=peer, device_id_type=MESH)

    columns = pl.ds(pl.multiple_of(lo * H, H), H)

    def forward(tok, weight, pre, p):
        at = slice(256 * p, 256 * p + 256)
        pre[at, :] = jnp.dot(tok[at, :], weight[...], preferred_element_type=F32)

    def pool(tok, pre, p, tokens, offset):
        for i in range(256 // tokens):
            at = slice(256 * p + tokens * i, 256 * p + tokens * i + tokens)
            hidden = tok[at, columns].astype(F32) + gelu(pre[at, :])
            sample = 256 // tokens * p + i
            row = (sample // 8) * 16 + offset + sample % 8
            pooled[row : row + 1, :] = jnp.sum(hidden, axis=0, keepdims=True) * (1.0 / tokens)

    first = lo == 0
    pair_slot = xh * 2 + c

    def swap(w):
        low, high = pooled[8 * w : 8 * w + 8, :], pooled[16 + 8 * w : 24 + 8 * w, :]
        ours = jnp.where(first, low, high)
        squares = jnp.sum(ours * ours, axis=1, keepdims=True)
        half_out[w, :, :H] = jnp.where(first, high, low)
        half_out[w, :, H:] = jnp.broadcast_to(squares, (8, EXT))
        start(half_out.at[w], half_in.at[w], s_other.at[w], r_other.at[w], partner)

    for name in ("tw", "t0"):
        loads[name].wait()
    forward(text_tok, text_weight, text_pre, 0)
    loads["t1"].wait()
    forward(text_tok, text_weight, text_pre, 1)
    pool(text_tok, text_pre, 0, 32, 8)
    for name in ("iw", "i0"):
        loads[name].wait()
    forward(image_tok, image_weight, image_pre, 0)
    pool(text_tok, text_pre, 1, 32, 8)
    pl.semaphore_wait(barrier, len(peers))
    swap(1)
    own_count = jnp.broadcast_to(scalars_ref[0:1, :], (8, 128))
    counts[pair_slot] = own_count
    for n, key in enumerate(PAIRS):
        start(counts.at[pair_slot], counts.at[pair_slot], s_count.at[n], r_count.at[n], members[key])
    for p in range(1, 4):
        loads["i%d" % p].wait()
        forward(image_tok, image_weight, image_pre, p)
        pool(image_tok, image_pre, p - 1, 64, 0)
    pool(image_tok, image_pre, 3, 64, 0)
    swap(0)
    mine = pooled[...]
    own_sq = jnp.sum(mine * mine, axis=1, keepdims=True)
    own_rows = jnp.where(first, mine[0:16], mine[16:32])
    own_rows_sq = jnp.where(first, own_sq[0:16], own_sq[16:32])
    rest_sq = jnp.where(first, own_sq[16:32], own_sq[0:16])
    for w in range(2):
        send_to(half_out.at[w], half_in.at[w], s_other.at[w], r_other.at[w], partner).wait_recv()
    arrived = half_in[...].reshape(16, H + EXT)
    theirs = arrived[:, :H]
    norm_own = jnp.sqrt(own_rows_sq + jnp.sum(theirs * theirs, axis=1, keepdims=True) + 1e-6)
    norm_rest = jnp.sqrt(rest_sq + arrived[:, H : H + 1] + 1e-6)
    norm = jnp.concatenate(
        [jnp.where(first, norm_own, norm_rest), jnp.where(first, norm_rest, norm_own)], axis=0
    )
    unit_own[...] = mine / norm
    unit_mine = own_rows / norm_own
    unit_theirs = theirs / norm_own
    low = jnp.where(first, unit_mine, unit_theirs)
    high = jnp.where(first, unit_theirs, unit_mine)
    for n, (dx, dc) in enumerate(PAIRS):
        slot = lax.rem(xh + dx // 2, 2) * 2 + lax.rem(c + dc, NC)
        send_to(counts.at[slot], counts.at[slot], s_count.at[n], r_count.at[n], members[(dx, dc)]).wait_recv()
    row_total = jnp.sum(counts[...], axis=0)[0:1, :]
    own_count = own_count[0:1, :]
    sample = lax.rem(lax.broadcasted_iota(jnp.int32, (16, EXT), 0), 8) + 8 * lo
    lane = lax.broadcasted_iota(jnp.int32, (16, EXT), 1)
    usable = jnp.where(sample.astype(F32) < own_count, 1.0, 0.0)
    extra = jnp.where(lane < EXT // 2, usable, jnp.broadcast_to(row_total, (16, EXT)))
    block = jnp.concatenate([low.astype(BF16), high.astype(BF16), extra.astype(BF16)], axis=1)
    plane[z, y] = block[:, :LOW]
    upper[z, y] = block[:, LOW:]
    group[me] = block

    def pass_up(far, j, zs, ys, hops):
        start(plane.at[zs, ys], plane.at[zs, ys], s_up.at[far, j], r_up.at[far, j], z_peers[hops - 1])

    def pass_down(far, j, zs, ys, hops):
        start(plane.at[zs, ys], plane.at[zs, ys], s_down.at[far, j], r_down.at[far, j], z_peers[NZ - hops - 1])

    def send_line(j, ys):
        for hops in (2, 1):
            pass_up(hops - 1, j, z, ys, hops)
            pass_down(hops - 1, j, z, ys, hops)

    def land_up(far, j):
        zs, ys = lax.rem(z + NZ - far - 1, NZ), lax.rem(y + NY - j, NY)
        send_to(plane.at[zs, ys], plane.at[zs, ys], s_up.at[far, j], r_up.at[far, j], up).wait_recv()
        if far == 1:
            if j < 2:
                pass_up(3, j, zs, ys, 2)
            pass_up(2, j, zs, ys, 1)

    def land_down(far, j):
        zs, ys = lax.rem(z + far + 1, NZ), lax.rem(y + NY - j, NY)
        send_to(plane.at[zs, ys], plane.at[zs, ys], s_down.at[far, j], r_down.at[far, j], down).wait_recv()
        if far == 1:
            if j >= 2:
                pass_down(3, j, zs, ys, 2)
            pass_down(2, j, zs, ys, 1)

    def pass_y(k):
        zs = lax.rem(z + k, NZ)
        for j in range(1, NY):
            start(upper.at[zs, y], upper.at[zs, y], s_uy.at[k, j - 1], r_uy.at[k, j - 1], y_peers[j - 1])

    def send_z(k, n, way):
        zs = lax.rem(z + k, NZ)
        start(upper.at[zs, y], upper.at[zs, y], s_uz.at[n], r_uz.at[n], way)

    def land_z(k):
        zs = lax.rem(z + k, NZ)
        send_to(upper.at[zs, y], upper.at[zs, y], s_uz.at[NZ - k - 1], r_uz.at[NZ - k - 1], up).wait_recv()
        if k < 3:
            send_z(k, NZ - k - 2, down)
        if k > 5:
            send_z(k, NZ - k, up)
        pass_y(k)

    for j in range(1, NY):
        start(plane.at[z, y], plane.at[z, y], s_y.at[j - 1], r_y.at[j - 1], y_peers[j - 1])
    send_line(0, y)
    send_z(0, 0, up)
    send_z(0, 6, down)
    send_z(0, 3, z_peers[3])
    pass_y(0)
    for n, key in enumerate(GROUP):
        start(group.at[me], group.at[me], s_group.at[n], r_group.at[n], members[key])

    def turn(tok, out, p):
        def work():
            flipped = tok[:, 384 * p : 384 * p + 384].T
            out[2 * p : 2 * p + 2] = flipped.reshape(2, ZROWS, tok.shape[0])

        return work

    def bend(pre, first_row, rows):
        def work():
            @pl.loop(0, rows // 16)
            def _(i):
                at = pl.ds(pl.multiple_of(first_row + i * 16, 16), 16)
                pre[at, :] = slope_of(pre[at, :])

        return work

    pieces = [turn(image_tok, image_t, p) for p in range(4)] + [turn(text_tok, text_t, p) for p in range(4)]
    pieces += [bend(image_pre, 128 * p, 128) for p in range(8)] + [bend(text_pre, 128 * p, 128) for p in range(4)]
    done = [0]

    def idle(amount=1):
        for piece in pieces[done[0] : done[0] + amount]:
            piece()
        done[0] += amount

    for j in LINE[1:]:
        ys = lax.rem(y + NY - j, NY)
        send_to(plane.at[z, ys], plane.at[z, ys], s_y.at[j - 1], r_y.at[j - 1], up).wait_recv()
        send_line(j, ys)
    land_z(1)
    land_z(7)
    idle()
    for i, j in enumerate(LINE):
        land_up(1, j)
        land_down(1, j)
        idle()
        if i == 0:
            land_z(2)
            land_z(6)
        idle()
        if i == 2:
            land_z(3)
            land_z(5)
            land_z(4)
        idle()
    for far in (0, 2, 3):
        for j in LINE:
            if far < 3 or j < 2:
                land_up(far, j)
            if far < 3 or j >= 2:
                land_down(far, j)
            idle()
    idle(len(pieces) - done[0])
    for n, key in enumerate(GROUP):
        slot = slot_of(*sources[key])
        send_to(group.at[slot], group.at[slot], s_group.at[n], r_group.at[n], members[key]).wait_recv()

    for k in range(NZ):
        for j in range(1, NY):
            zs, ys = lax.rem(z + k, NZ), lax.rem(y + NY - j, NY)
            send_to(upper.at[zs, ys], upper.at[zs, ys], s_uy.at[k, j - 1], r_uy.at[k, j - 1], up).wait_recv()

    rows = group[...].reshape(8 * 16, D + EXT)
    low_cols = plane[...].reshape(32 * 16, LOW)
    high_cols = upper[...].reshape(32 * 16, D - LOW + EXT)
    row_main, high_main = rows[:, :D], high_cols[:, : D - LOW]
    logit_mult = scalars_ref[1:2, 0:1]
    products = dot_t(row_main[:, :LOW], low_cols) + dot_t(row_main[:, LOW:], high_main)
    logits = logit_mult * products + scalars_ref[2:3, 0:1]
    pick = lax.broadcasted_iota(jnp.int32, (16, EXT), 0) * (EXT // 2)
    pick = jnp.where(pick == lax.broadcasted_iota(jnp.int32, (16, EXT), 1), 1.0, 0.0).astype(BF16)
    col_extra = dot_t(pick, high_cols[:, D - LOW :])
    total = jnp.sum(col_extra[1:2, :]) * (1.0 / 16.0)
    col_usable = col_extra[0:1, :]
    row_usable = rows[:, D : D + 1].astype(F32)
    shape = (8 * 16, 32 * 16)
    r = lax.broadcasted_iota(jnp.int32, shape, 0)
    q = lax.broadcasted_iota(jnp.int32, shape, 1)
    r_text = lax.rem(lax.div(r, 8), 2)
    q_text = lax.rem(lax.div(q, 8), 2)
    same = (lax.div(r, 16) == me) & (lax.div(q, 16) == z * NY + y) & (lax.rem(r, 8) == lax.rem(q, 8))
    used = (row_usable * col_usable > 0.5) & (r_text != q_text)
    sign = jnp.where(same, 1.0, -1.0)
    margin = -sign * logits
    coeff = scalars_ref[3:4, 0:1] / total
    dlogit = (jnp.where(used, -sign * jax.nn.sigmoid(margin), 0.0) * coeff).astype(BF16)
    grad = logit_mult * jnp.concatenate(
        [jnp.dot(dlogit, cols, preferred_element_type=F32) for cols in (low_cols, high_main)], axis=1
    )
    radial = jnp.sum(row_main.astype(F32) * grad, axis=1, keepdims=True)
    code = code_of(jnp.max(jnp.abs(grad), axis=1, keepdims=True))
    factor = jnp.exp2(TOP - code / CODE)
    digits = whole(grad * factor).astype(jnp.int16)
    radial = whole(radial * factor * (1.0 / 40.0))
    side = lax.broadcasted_iota(jnp.int32, (8 * 16, EXT), 1) < EXT // 2
    side = jnp.where(side, code.astype(jnp.int32), radial).astype(jnp.int16)
    for pair in range(4):
        for half in range(2):
            band = slice(pair * 32, pair * 32 + 32)
            parts[pair, half, :, :H] = digits[band, half * H : half * H + H]
            parts[pair, half, :, H:] = side[band]

    for n, (dx, dc) in enumerate(GROUP):
        tx, tc = lax.rem(x + dx, NX), lax.rem(c + dc, NC)
        src = parts.at[lax.div(tx, 2) * 2 + tc, lax.rem(tx, 2)]
        start(src, landed.at[me], s_part.at[n], r_part.at[n], members[(dx, dc)])

    soft = jnp.maximum(margin, 0.0) + jnp.log1p(jnp.exp(-jnp.abs(margin)))
    loss = jnp.sum(jnp.where(used & (r_text == 0), soft, 0.0), axis=1, keepdims=True)
    loss_group[0] = jnp.broadcast_to(jnp.sum(loss, axis=0, keepdims=True) / total, (8, 128))
    for n, key in enumerate(GROUP):
        start(loss_group.at[0], loss_group.at[n + 1], s_lg.at[n], r_lg.at[n], members[key])

    def opened(packed):
        wide = packed.astype(jnp.int32).astype(F32)
        back = jnp.exp2(wide[:, H : H + 1] / CODE - TOP)
        return wide[:, :H] * back, wide[:, H + EXT // 2 : H + EXT // 2 + 1] * (back * 40.0)

    sum_grad, sum_radial = opened(parts[pair_slot, lo])
    for n, key in enumerate(GROUP):
        slot = slot_of(*sources[key])
        send_to(landed.at[slot], landed.at[slot], s_part.at[n], r_part.at[n], members[key]).wait_recv()
        more_grad, more_radial = opened(landed[slot])
        sum_grad = sum_grad + more_grad
        sum_radial = sum_radial + more_radial
    gp = (sum_grad - unit_own[...] * sum_radial) / norm
    for i in range(16):
        row = (i // 8) * 16 + i % 8
        at = slice(64 * i, 64 * i + 64)
        image_gpre[at, :] = (gp[row : row + 1] / 64.0 * image_pre[at, :]).astype(BF16)
        at = slice(32 * i, 32 * i + 32)
        text_gpre[at, :] = (gp[row + 8 : row + 9] / 32.0 * text_pre[at, :]).astype(BF16)

    def compute(n):
        t = lax.rem(z + ORDER[n], NZ)
        image = jnp.dot(image_t[t], image_gpre[...], preferred_element_type=F32)
        text = jnp.dot(text_t[t], text_gpre[...], preferred_element_type=F32)
        terms[n] = jnp.where(c == 0, image, text)
        sib_out[n] = encode(jnp.where(c == 0, text, image), 16)
        start(sib_out.at[n], sib_in.at[n], s_sib.at[n], r_sib.at[n], twin)

    def chunk(n):
        send_to(sib_out.at[n], sib_in.at[n], s_sib.at[n], r_sib.at[n], twin).wait_recv()
        terms[n] += decode(sib_in[n], 16)

    def ring(step, n, h, out, inn, send_sem, recv_sem, way, early):
        value = terms[n, :, h * SUB : h * SUB + SUB]
        if step > 1 or (step == 1 and early):
            send_to(out.at[step - 1, h], inn.at[step - 1, h], send_sem.at[step - 1, h], recv_sem.at[step - 1, h], way).wait_recv()
            value = value + decode(inn[step - 1, h], 16)
        out[step, h] = encode(value, 16)
        start(out.at[step, h], inn.at[step, h], send_sem.at[step, h], recv_sem.at[step, h], way)

    def ring_step(step, n_up, n_down, begin=0, end=SUBS):
        ups, downs = list(range(UPS)), list(range(UPS, SUBS))
        if step > 0:
            ups, downs = downs + ups, ups + downs
        for i in range(begin, end):
            if i < len(ups):
                ring(step, n_up, ups[i], up_out, up_in, s_rup, r_rup, up, ups[i] < UPS)
            if i < len(downs):
                ring(step, n_down, downs[i], down_out, down_in, s_rdown, r_rdown, down, downs[i] >= UPS)

    def spread(q):
        values = []
        for n in range(4 * q, 4 * q + 4):
            values.append(terms[n, :, FAR:].reshape(2 * NY, OWN, REST))
        for i in range(2 * NY):
            wide_out[q, i] = encode(jnp.concatenate([value[i] for value in values], axis=0), 16)
        for n, (dxh, j) in enumerate(YX):
            src = wide_out.at[q, lax.rem(xh + dxh, 2) * NY + lax.rem(y + j, NY)]
            start(src, wide_in.at[q, n], s_wide.at[q, n], r_wide.at[q, n], near[(dxh, j)])

    def collect(q):
        value = decode(wide_out[q, xh * NY + y], 16)
        for n, key in enumerate(YX):
            send_to(wide_in.at[q, n], wide_in.at[q, n], s_wide.at[q, n], r_wide.at[q, n], near[key]).wait_recv()
            value = value + decode(wide_in[q, n], 16)
        for i in range(4):
            k = ORDER[4 * q + i]
            part = value[OWN * i : OWN * i + OWN]
            if k == 0:
                rest_own[...] = part
            else:
                line_out[k - 1] = encode(part, 8)
                start(line_out.at[k - 1], line_in.at[k - 1], s_line.at[k - 1], r_line.at[k - 1], z_peers[k - 1])

    old = copies[:]
    del copies[:]
    compute(0)
    compute(1)
    chunk(0)
    ring_step(0, 0, 0)
    compute(2)
    compute(3)
    for n in (1, 2):
        chunk(n)
    ring_step(1, 1, 2, 0, UPS)
    flush(old)
    chunk(3)
    spread(0)
    compute(4)
    compute(5)
    ring_step(1, 1, 2, UPS)
    compute(6)
    compute(7)
    for n in (4, 5, 6, 7):
        chunk(n)
    spread(1)
    for n, key in enumerate(GROUP):
        send_to(loss_group.at[0], loss_group.at[n + 1], s_lg.at[n], r_lg.at[n], members[key]).wait_recv()
    loss_y[0] = jnp.sum(loss_group[...], axis=0)
    for j in range(1, NY):
        start(loss_y.at[0], loss_y.at[j], s_ly.at[j - 1], r_ly.at[j - 1], y_peers[j - 1])
    ring_step(2, 3, 4)
    collect(0)
    for j in range(1, NY):
        send_to(loss_y.at[0], loss_y.at[j], s_ly.at[j - 1], r_ly.at[j - 1], y_peers[j - 1]).wait_recv()
    loss_z[0] = jnp.sum(loss_y[...], axis=0)
    for k in range(1, NZ):
        start(loss_z.at[0], loss_z.at[k], s_lz.at[k - 1], r_lz.at[k - 1], z_peers[k - 1])
    ring_step(3, 5, 6)
    collect(1)
    old = copies[:]
    del copies[:]
    for h in (0, 2, 1, 3):
        at = slice(h * SUB, h * SUB + SUB)
        value = terms[7, :, at]
        send_to(up_out.at[3, h], up_in.at[3, h], s_rup.at[3, h], r_rup.at[3, h], up).wait_recv()
        value = value + decode(up_in[3, h], 16)
        send_to(down_out.at[3, h], down_in.at[3, h], s_rdown.at[3, h], r_rdown.at[3, h], down).wait_recv()
        value = (value + decode(down_in[3, h], 16)).reshape(2 * NY, OWN, SUB)
        for i in range(2 * NY):
            near_out[i, :, at] = encode(value[i], 8)
    for n, (dxh, j) in enumerate(YX):
        src = near_out.at[lax.rem(xh + dxh, 2) * NY + lax.rem(y + j, NY)]
        start(src, near_in.at[n], s_near.at[n], r_near.at[n], near[(dxh, j)])
    flush(old)
    rest = rest_own[...]
    for k in range(1, NZ):
        send_to(line_in.at[k - 1], line_in.at[k - 1], s_line.at[k - 1], r_line.at[k - 1], z_peers[k - 1]).wait_recv()
        rest = rest + decode(line_in[k - 1], 8)
    final[c, :, FAR:] = rest
    for k in range(1, NZ):
        send_to(loss_z.at[0], loss_z.at[k], s_lz.at[k - 1], r_lz.at[k - 1], z_peers[k - 1]).wait_recv()
    loss_out_ref[...] = jnp.sum(loss_z[...], axis=0)
    result = decode(near_out[xh * NY + y], 8)
    for n, key in enumerate(YX):
        send_to(near_in.at[n], near_in.at[n], s_near.at[n], r_near.at[n], near[key]).wait_recv()
        result = result + decode(near_in[n], 8)
    final[c, :, :FAR] = result
    start(final.at[c], final.at[c], s_final, r_final, twin)
    send_to(final.at[1 - c], final.at[1 - c], s_final, r_final, twin).wait_recv()
    even = c == 0
    image_out_ref[...] = jnp.where(even, final[0, 0:12, :], final[0, 12:24, :])
    text_out_ref[...] = jnp.where(even, final[1, 0:12, :], final[1, 12:24, :])
    flush(copies)


def run_kernel(scalars, image, text, image_weight, text_weight):
    dma = pltpu.SemaphoreType.DMA
    vmem = pl.BlockSpec(memory_space=pltpu.VMEM)
    anywhere = pl.BlockSpec(memory_space=pltpu.HBM)
    image_rows, text_rows = image.shape[0], text.shape[0]
    ring = pltpu.VMEM((4, SUBS, ZROWS + 16, SUB), jnp.int16)
    tile = (8, 128)
    return pl.pallas_call(
        kernel,
        out_shape=(
            jax.ShapeDtypeStruct((12, H), F32),
            jax.ShapeDtypeStruct((12, H), F32),
            jax.ShapeDtypeStruct(tile, F32),
        ),
        in_specs=[vmem, anywhere, anywhere, anywhere, anywhere],
        out_specs=(vmem, vmem, vmem),
        scratch_shapes=[
            pltpu.VMEM((D, H), BF16),
            pltpu.VMEM((D, H), BF16),
            pltpu.VMEM((32, H), F32),
            pltpu.VMEM((2, 8, H + EXT), F32),
            pltpu.VMEM((2, 8, H + EXT), F32),
            pltpu.VMEM((4,) + tile, F32),
            pltpu.VMEM((NZ, NY, 16, LOW), BF16),
            pltpu.VMEM((NZ, NY, 16, D - LOW + EXT), BF16),
            pltpu.VMEM((8, 16, D + EXT), BF16),
            pltpu.VMEM((4, 2, 32, H + EXT), jnp.int16),
            pltpu.VMEM((8, 32, H + EXT), jnp.int16),
            pltpu.VMEM((32, H), F32),
            pltpu.VMEM((image_rows, D), BF16),
            pltpu.VMEM((text_rows, D), BF16),
            pltpu.VMEM((NZ, ZROWS, image_rows), BF16),
            pltpu.VMEM((NZ, ZROWS, text_rows), BF16),
            pltpu.VMEM((image_rows, H), F32),
            pltpu.VMEM((text_rows, H), F32),
            pltpu.VMEM((image_rows, H), BF16),
            pltpu.VMEM((text_rows, H), BF16),
            pltpu.VMEM((NZ, ZROWS, H), F32),
            pltpu.VMEM((NZ, ZROWS + 16, H), jnp.int16),
            pltpu.VMEM((NZ, ZROWS + 16, H), jnp.int16),
            ring,
            ring,
            ring,
            ring,
            pltpu.VMEM((2 * NY, 32, FAR), jnp.int16),
            pltpu.VMEM((7, 32, FAR), jnp.int16),
            pltpu.VMEM((2, 2 * NY, 112, REST), jnp.int16),
            pltpu.VMEM((2, 7, 112, REST), jnp.int16),
            pltpu.VMEM((7, 32, REST), jnp.int16),
            pltpu.VMEM((7, 32, REST), jnp.int16),
            pltpu.VMEM((OWN, REST), F32),
            pltpu.VMEM((2, OWN, H), F32),
            pltpu.VMEM((8,) + tile, F32),
            pltpu.VMEM((NY,) + tile, F32),
            pltpu.VMEM((NZ,) + tile, F32),
            dma((8,)),
        ]
        + [dma((2,))] * 2
        + [dma((3,))] * 2
        + [dma((7,))] * 2
        + [dma((3,))] * 2
        + [dma((4, 4))] * 4
        + [dma((7,))] * 2
        + [dma((NZ, 3))] * 2
        + [dma((7,))] * 2
        + [dma((8,))] * 2
        + [dma((4, SUBS))] * 4
        + [dma((7,))] * 2
        + [dma((2, 7))] * 2
        + [dma((7,))] * 2
        + [dma] * 2
        + [dma((7,))] * 2
        + [dma((3,))] * 2
        + [dma((7,))] * 2,
        compiler_params=pltpu.CompilerParams(
            collective_id=1, has_side_effects=True, vmem_limit_bytes=53 * 1024 * 1024
        ),
    )(scalars, image, text, image_weight, text_weight)


def body(
    image_tokens,
    text_tokens,
    image_weight,
    text_weight,
    logit_scale,
    logit_bias,
    loss_scale,
    valid_count,
):
    row = lax.broadcasted_iota(jnp.int32, (8, 128), 0)
    scalars = jnp.where(row == 0, valid_count[0].astype(F32), logit_scale[0])
    scalars = jnp.where(row == 2, logit_bias[0], jnp.where(row == 3, loss_scale[0], scalars))
    image_grad, text_grad, loss = run_kernel(
        scalars,
        image_tokens.reshape(-1, D),
        text_tokens.reshape(-1, D),
        image_weight,
        text_weight,
    )
    return (loss[0, 0], image_grad, text_grad)


def solution(mesh):
    placed = (
        P("dp", None, None),
        P("dp", None, None),
        P(None, "mp"),
        P(None, "mp"),
        P(),
        P(),
        P(),
        P("dp"),
    )
    return jax.shard_map(
        body,
        mesh=mesh,
        in_specs=placed,
        out_specs=(P(), P("dp", "mp"), P("dp", "mp")),
        check_vma=False,
    )
```

```python
import jax
import jax.numpy as jnp
from jax import lax
from jax.experimental import pallas as pl
from jax.experimental.pallas import tpu as pltpu
from jax.sharding import PartitionSpec as P

MESH = pl.DeviceIdType.MESH
F32 = jnp.float32
BF16 = jnp.bfloat16
NZ, NY, NX, NC = 8, 4, 4, 2
D = 1536
H = 768
EXT = 128
ZROWS = D // NZ
OWN = 24


def place():
    dp = lax.axis_index("dp")
    lo = lax.axis_index("mp")
    c = lax.rem(dp, 2)
    y = lax.rem(lax.div(dp, 2), 4)
    xh = lax.rem(lax.div(dp, 8), 2)
    z = lax.div(dp, 16)
    return z, y, xh * 2 + lo, c


def device_at(z, y, x, c):
    return (((z * 2 + lax.div(x, 2)) * 4 + y) * 2 + c, lax.rem(x, 2))


def slot_of(x, c):
    return (lax.div(x, 2) * 2 + c) * 2 + lax.rem(x, 2)


def send_to(src, dst, send_sem, recv_sem, device):
    return pltpu.make_async_remote_copy(
        src_ref=src,
        dst_ref=dst,
        send_sem=send_sem,
        recv_sem=recv_sem,
        device_id=device,
        device_id_type=MESH,
    )


def greet(devices):
    barrier = pltpu.get_barrier_semaphore()
    for device in devices:
        pl.semaphore_signal(barrier, inc=1, device_id=device, device_id_type=MESH)
    pl.semaphore_wait(barrier, len(devices))


GROUP = [(dx, dc) for dx in range(NX) for dc in range(NC) if (dx, dc) != (0, 0)]


def dot_t(a, b):
    return lax.dot_general(a, b, (((1,), (1,)), ((), ())), preferred_element_type=F32)


CODE = 256.0
TOP = 14.98
LEAST = 2.0**-100


def code_of(peak):
    return jnp.ceil(jnp.log2(jnp.maximum(peak, LEAST)) * CODE)


def whole(values):
    return jnp.round(values).astype(jnp.int32)


def encode(values, pad):
    code = code_of(jnp.max(jnp.abs(values), axis=0, keepdims=True))
    digits = whole(values * jnp.exp2(TOP - code / CODE))
    codes = jnp.broadcast_to(code.astype(jnp.int32), (pad, values.shape[1]))
    return jnp.concatenate([digits, codes], axis=0).astype(jnp.int16)


def decode(packed, pad):
    wide = packed.astype(jnp.int32).astype(F32)
    rows = packed.shape[0] - pad
    return wide[:rows] * jnp.exp2(wide[rows : rows + 1] / CODE - TOP)


def gelu(x):
    k = 0.7978845608028654
    return 0.5 * x * (1.0 + jnp.tanh(k * x * (1.0 + 0.044715 * (x * x))))


def slope_of(x):
    k = 0.7978845608028654
    x2 = x * x
    t = jnp.tanh(k * x * (1.0 + 0.044715 * x2))
    return 0.5 * (1.0 + t) + 0.5 * x * (1.0 - t * t) * (k * (1.0 + 3.0 * 0.044715 * x2))


YX = [(dxh, j) for dxh in range(2) for j in range(NY) if (dxh, j) != (0, 0)]
PAIRS = [(0, 1), (2, 0), (2, 1)]
LOW = 512
LINE = [0, 1, 3, 2]
ORDER = [4, 3, 5, 2, 6, 1, 7, 0]
SUBS = 4
UPS = 2
SUB = 128
FAR = SUBS * SUB
REST = H - FAR


def kernel(
    scalars_ref,
    image_ref,
    text_ref,
    image_weight_ref,
    text_weight_ref,
    image_out_ref,
    text_out_ref,
    loss_out_ref,
    image_weight,
    text_weight,
    pooled,
    half_out,
    half_in,
    counts,
    plane,
    upper,
    group,
    parts,
    landed,
    unit_own,
    image_tok,
    text_tok,
    image_t,
    text_t,
    image_pre,
    text_pre,
    image_gpre,
    text_gpre,
    terms,
    sib_out,
    sib_in,
    up_out,
    up_in,
    down_out,
    down_in,
    near_out,
    near_in,
    wide_out,
    wide_in,
    line_out,
    line_in,
    rest_own,
    final,
    loss_group,
    loss_y,
    loss_z,
    s_load,
    s_other,
    r_other,
    s_count,
    r_count,
    s_group,
    r_group,
    s_y,
    r_y,
    s_up,
    r_up,
    s_down,
    r_down,
    s_uz,
    r_uz,
    s_uy,
    r_uy,
    s_part,
    r_part,
    s_sib,
    r_sib,
    s_rup,
    r_rup,
    s_rdown,
    r_rdown,
    s_near,
    r_near,
    s_wide,
    r_wide,
    s_line,
    r_line,
    s_final,
    r_final,
    s_lg,
    r_lg,
    s_ly,
    r_ly,
    s_lz,
    r_lz,
):
    z, y, x, c = place()
    xh, lo = lax.div(x, 2), lax.rem(x, 2)
    me = slot_of(x, c)
    up = device_at(lax.rem(z + 1, NZ), y, x, c)
    down = device_at(lax.rem(z + NZ - 1, NZ), y, x, c)
    members = {(dx, dc): device_at(z, y, lax.rem(x + dx, NX), lax.rem(c + dc, NC)) for dx, dc in GROUP}
    sources = {(dx, dc): (lax.rem(x + NX - dx, NX), lax.rem(c + dc, NC)) for dx, dc in GROUP}
    near = {(dxh, j): device_at(z, lax.rem(y + j, NY), lax.rem(xh + dxh, 2) * 2 + lo, c) for dxh, j in YX}
    y_peers = [near[(0, j)] for j in range(1, NY)]
    z_peers = [device_at(lax.rem(z + k, NZ), y, x, c) for k in range(1, NZ)]
    partner = device_at(z, y, xh * 2 + 1 - lo, c)
    twin = members[(0, 1)]
    copies = []

    def flush(sent):
        for copy in sent:
            copy.wait_send()

    def start(*args):
        copy = send_to(*args)
        copy.start()
        copies.append(copy)

    loads = {}

    def fetch(name, src, dst):
        loads[name] = pltpu.make_async_copy(src, dst, s_load.at[len(loads)])
        loads[name].start()

    left, right = pl.ds(0, H // 2), pl.ds(H // 2, H // 2)
    fetch("t0", text_ref.at[pl.ds(0, 256)], text_tok.at[pl.ds(0, 256)])
    fetch("tw", text_weight_ref.at[:, left], text_weight.at[:, left])
    fetch("tx", text_weight_ref.at[:, right], text_weight.at[:, right])
    fetch("t1", text_ref.at[pl.ds(256, 256)], text_tok.at[pl.ds(256, 256)])
    fetch("iw", image_weight_ref, image_weight)
    for p in range(4):
        at = pl.ds(256 * p, 256)
        fetch("i%d" % p, image_ref.at[at], image_tok.at[at])
    peers = [members[key] for key in GROUP] + [near[key] for key in YX if key != (1, 0)] + z_peers
    barrier = pltpu.get_barrier_semaphore()
    for peer in peers:
        pl.semaphore_signal(barrier, inc=1, device_id=peer, device_id_type=MESH)

    columns = pl.ds(pl.multiple_of(lo * H, H), H)

    def forward(tok, weight, pre, p, begin=0, end=H):
        at, cols = slice(256 * p, 256 * p + 256), slice(begin, end)
        pre[at, cols] = jnp.dot(tok[at, :], weight[:, cols], preferred_element_type=F32)

    def pool(tok, pre, p, tokens, offset):
        for i in range(256 // tokens):
            at = slice(256 * p + tokens * i, 256 * p + tokens * i + tokens)
            hidden = tok[at, columns].astype(F32) + gelu(pre[at, :])
            sample = 256 // tokens * p + i
            row = (sample // 8) * 16 + offset + sample % 8
            pooled[row : row + 1, :] = jnp.sum(hidden, axis=0, keepdims=True) * (1.0 / tokens)

    first = lo == 0
    pair_slot = xh * 2 + c

    def swap(w):
        low, high = pooled[8 * w : 8 * w + 8, :], pooled[16 + 8 * w : 24 + 8 * w, :]
        ours = jnp.where(first, low, high)
        squares = jnp.sum(ours * ours, axis=1, keepdims=True)
        half_out[w, :, :H] = jnp.where(first, high, low)
        half_out[w, :, H:] = jnp.broadcast_to(squares, (8, EXT))
        start(half_out.at[w], half_in.at[w], s_other.at[w], r_other.at[w], partner)

    for name in ("t0", "tw"):
        loads[name].wait()
    forward(text_tok, text_weight, text_pre, 0, 0, H // 2)
    loads["tx"].wait()
    forward(text_tok, text_weight, text_pre, 0, H // 2, H)
    loads["t1"].wait()
    forward(text_tok, text_weight, text_pre, 1)
    pool(text_tok, text_pre, 0, 32, 8)
    for name in ("iw", "i0"):
        loads[name].wait()
    forward(image_tok, image_weight, image_pre, 0)
    pool(text_tok, text_pre, 1, 32, 8)
    pl.semaphore_wait(barrier, len(peers))
    swap(1)
    own_count = jnp.broadcast_to(scalars_ref[0:1, :], (8, 128))
    counts[pair_slot] = own_count
    for n, key in enumerate(PAIRS):
        start(counts.at[pair_slot], counts.at[pair_slot], s_count.at[n], r_count.at[n], members[key])
    for p in range(1, 4):
        loads["i%d" % p].wait()
        forward(image_tok, image_weight, image_pre, p)
        pool(image_tok, image_pre, p - 1, 64, 0)
    pool(image_tok, image_pre, 3, 64, 0)
    swap(0)
    mine = pooled[...]
    own_sq = jnp.sum(mine * mine, axis=1, keepdims=True)
    own_rows = jnp.where(first, mine[0:16], mine[16:32])
    own_rows_sq = jnp.where(first, own_sq[0:16], own_sq[16:32])
    rest_sq = jnp.where(first, own_sq[16:32], own_sq[0:16])
    for w in range(2):
        send_to(half_out.at[w], half_in.at[w], s_other.at[w], r_other.at[w], partner).wait_recv()
    arrived = half_in[...].reshape(16, H + EXT)
    theirs = arrived[:, :H]
    norm_own = jnp.sqrt(own_rows_sq + jnp.sum(theirs * theirs, axis=1, keepdims=True) + 1e-6)
    norm_rest = jnp.sqrt(rest_sq + arrived[:, H : H + 1] + 1e-6)
    norm = jnp.concatenate(
        [jnp.where(first, norm_own, norm_rest), jnp.where(first, norm_rest, norm_own)], axis=0
    )
    unit_own[...] = mine / norm
    unit_mine = own_rows / norm_own
    unit_theirs = theirs / norm_own
    low = jnp.where(first, unit_mine, unit_theirs)
    high = jnp.where(first, unit_theirs, unit_mine)
    for n, (dx, dc) in enumerate(PAIRS):
        slot = lax.rem(xh + dx // 2, 2) * 2 + lax.rem(c + dc, NC)
        send_to(counts.at[slot], counts.at[slot], s_count.at[n], r_count.at[n], members[(dx, dc)]).wait_recv()
    row_total = jnp.sum(counts[...], axis=0)[0:1, :]
    own_count = own_count[0:1, :]
    sample = lax.rem(lax.broadcasted_iota(jnp.int32, (16, EXT), 0), 8) + 8 * lo
    lane = lax.broadcasted_iota(jnp.int32, (16, EXT), 1)
    usable = jnp.where(sample.astype(F32) < own_count, 1.0, 0.0)
    extra = jnp.where(lane < EXT // 2, usable, jnp.broadcast_to(row_total, (16, EXT)))
    block = jnp.concatenate([low.astype(BF16), high.astype(BF16), extra.astype(BF16)], axis=1)
    plane[z, y] = block[:, :LOW]
    upper[z, y] = block[:, LOW:]
    group[me] = block

    def pass_up(far, j, zs, ys, hops):
        start(plane.at[zs, ys], plane.at[zs, ys], s_up.at[far, j], r_up.at[far, j], z_peers[hops - 1])

    def pass_down(far, j, zs, ys, hops):
        start(plane.at[zs, ys], plane.at[zs, ys], s_down.at[far, j], r_down.at[far, j], z_peers[NZ - hops - 1])

    def send_line(j, ys):
        for hops in (2, 1):
            pass_up(hops - 1, j, z, ys, hops)
            pass_down(hops - 1, j, z, ys, hops)

    def land_up(far, j):
        zs, ys = lax.rem(z + NZ - far - 1, NZ), lax.rem(y + NY - j, NY)
        send_to(plane.at[zs, ys], plane.at[zs, ys], s_up.at[far, j], r_up.at[far, j], up).wait_recv()
        if far == 1:
            if j < 2:
                pass_up(3, j, zs, ys, 2)
            pass_up(2, j, zs, ys, 1)

    def land_down(far, j):
        zs, ys = lax.rem(z + far + 1, NZ), lax.rem(y + NY - j, NY)
        send_to(plane.at[zs, ys], plane.at[zs, ys], s_down.at[far, j], r_down.at[far, j], down).wait_recv()
        if far == 1:
            if j >= 2:
                pass_down(3, j, zs, ys, 2)
            pass_down(2, j, zs, ys, 1)

    def pass_y(k):
        zs = lax.rem(z + k, NZ)
        for j in range(1, NY):
            start(upper.at[zs, y], upper.at[zs, y], s_uy.at[k, j - 1], r_uy.at[k, j - 1], y_peers[j - 1])

    def send_z(k, n, way):
        zs = lax.rem(z + k, NZ)
        start(upper.at[zs, y], upper.at[zs, y], s_uz.at[n], r_uz.at[n], way)

    def land_z(k):
        zs = lax.rem(z + k, NZ)
        send_to(upper.at[zs, y], upper.at[zs, y], s_uz.at[NZ - k - 1], r_uz.at[NZ - k - 1], up).wait_recv()
        if k < 3:
            send_z(k, NZ - k - 2, down)
        if k > 5:
            send_z(k, NZ - k, up)
        pass_y(k)

    for j in range(1, NY):
        start(plane.at[z, y], plane.at[z, y], s_y.at[j - 1], r_y.at[j - 1], y_peers[j - 1])
    send_line(0, y)
    send_z(0, 0, up)
    send_z(0, 6, down)
    send_z(0, 3, z_peers[3])
    pass_y(0)
    for n, key in enumerate(GROUP):
        start(group.at[me], group.at[me], s_group.at[n], r_group.at[n], members[key])

    def turn(tok, out, p):
        def work():
            flipped = tok[:, 384 * p : 384 * p + 384].T
            out[2 * p : 2 * p + 2] = flipped.reshape(2, ZROWS, tok.shape[0])

        return work

    def bend(pre, first_row, rows):
        def work():
            @pl.loop(0, rows // 16)
            def _(i):
                at = pl.ds(pl.multiple_of(first_row + i * 16, 16), 16)
                pre[at, :] = slope_of(pre[at, :])

        return work

    pieces = [turn(image_tok, image_t, p) for p in range(4)] + [turn(text_tok, text_t, p) for p in range(4)]
    pieces += [bend(image_pre, 128 * p, 128) for p in range(8)] + [bend(text_pre, 128 * p, 128) for p in range(4)]
    done = [0]

    def idle(amount=1):
        for piece in pieces[done[0] : done[0] + amount]:
            piece()
        done[0] += amount

    for j in LINE[1:]:
        ys = lax.rem(y + NY - j, NY)
        send_to(plane.at[z, ys], plane.at[z, ys], s_y.at[j - 1], r_y.at[j - 1], up).wait_recv()
        send_line(j, ys)
    land_z(1)
    land_z(7)
    idle()
    for i, j in enumerate(LINE):
        land_up(1, j)
        land_down(1, j)
        idle()
        if i == 0:
            land_z(2)
            land_z(6)
        idle()
        if i == 2:
            land_z(3)
            land_z(5)
            land_z(4)
        idle()
    for far in (0, 2, 3):
        for j in LINE:
            if far < 3 or j < 2:
                land_up(far, j)
            if far < 3 or j >= 2:
                land_down(far, j)
            idle()
    idle(len(pieces) - done[0])
    for n, key in enumerate(GROUP):
        slot = slot_of(*sources[key])
        send_to(group.at[slot], group.at[slot], s_group.at[n], r_group.at[n], members[key]).wait_recv()

    for k in range(NZ):
        for j in range(1, NY):
            zs, ys = lax.rem(z + k, NZ), lax.rem(y + NY - j, NY)
            send_to(upper.at[zs, ys], upper.at[zs, ys], s_uy.at[k, j - 1], r_uy.at[k, j - 1], up).wait_recv()

    rows = group[...].reshape(8 * 16, D + EXT)
    low_cols = plane[...].reshape(32 * 16, LOW)
    high_cols = upper[...].reshape(32 * 16, D - LOW + EXT)
    row_main, high_main = rows[:, :D], high_cols[:, : D - LOW]
    logit_mult = scalars_ref[1:2, 0:1]
    products = dot_t(row_main[:, :LOW], low_cols) + dot_t(row_main[:, LOW:], high_main)
    logits = logit_mult * products + scalars_ref[2:3, 0:1]
    pick = lax.broadcasted_iota(jnp.int32, (16, EXT), 0) * (EXT // 2)
    pick = jnp.where(pick == lax.broadcasted_iota(jnp.int32, (16, EXT), 1), 1.0, 0.0).astype(BF16)
    col_extra = dot_t(pick, high_cols[:, D - LOW :])
    total = jnp.sum(col_extra[1:2, :]) * (1.0 / 16.0)
    col_usable = col_extra[0:1, :]
    row_usable = rows[:, D : D + 1].astype(F32)
    shape = (8 * 16, 32 * 16)
    r = lax.broadcasted_iota(jnp.int32, shape, 0)
    q = lax.broadcasted_iota(jnp.int32, shape, 1)
    r_text = lax.rem(lax.div(r, 8), 2)
    q_text = lax.rem(lax.div(q, 8), 2)
    same = (lax.div(r, 16) == me) & (lax.div(q, 16) == z * NY + y) & (lax.rem(r, 8) == lax.rem(q, 8))
    used = (row_usable * col_usable > 0.5) & (r_text != q_text)
    sign = jnp.where(same, 1.0, -1.0)
    margin = -sign * logits
    coeff = scalars_ref[3:4, 0:1] / total
    dlogit = (jnp.where(used, -sign * jax.nn.sigmoid(margin), 0.0) * coeff).astype(BF16)
    grad = logit_mult * jnp.concatenate(
        [jnp.dot(dlogit, cols, preferred_element_type=F32) for cols in (low_cols, high_main)], axis=1
    )
    radial = jnp.sum(row_main.astype(F32) * grad, axis=1, keepdims=True)
    code = code_of(jnp.max(jnp.abs(grad), axis=1, keepdims=True))
    factor = jnp.exp2(TOP - code / CODE)
    digits = whole(grad * factor).astype(jnp.int16)
    radial = whole(radial * factor * (1.0 / 40.0))
    side = lax.broadcasted_iota(jnp.int32, (8 * 16, EXT), 1) < EXT // 2
    side = jnp.where(side, code.astype(jnp.int32), radial).astype(jnp.int16)
    for pair in range(4):
        for half in range(2):
            band = slice(pair * 32, pair * 32 + 32)
            parts[pair, half, :, :H] = digits[band, half * H : half * H + H]
            parts[pair, half, :, H:] = side[band]

    for n, (dx, dc) in enumerate(GROUP):
        tx, tc = lax.rem(x + dx, NX), lax.rem(c + dc, NC)
        src = parts.at[lax.div(tx, 2) * 2 + tc, lax.rem(tx, 2)]
        start(src, landed.at[me], s_part.at[n], r_part.at[n], members[(dx, dc)])

    soft = jnp.maximum(margin, 0.0) + jnp.log1p(jnp.exp(-jnp.abs(margin)))
    loss = jnp.sum(jnp.where(used & (r_text == 0), soft, 0.0), axis=1, keepdims=True)
    loss_group[0] = jnp.broadcast_to(jnp.sum(loss, axis=0, keepdims=True) / total, (8, 128))
    for n, key in enumerate(GROUP):
        start(loss_group.at[0], loss_group.at[n + 1], s_lg.at[n], r_lg.at[n], members[key])

    def opened(packed):
        wide = packed.astype(jnp.int32).astype(F32)
        back = jnp.exp2(wide[:, H : H + 1] / CODE - TOP)
        return wide[:, :H] * back, wide[:, H + EXT // 2 : H + EXT // 2 + 1] * (back * 40.0)

    sum_grad, sum_radial = opened(parts[pair_slot, lo])
    for n, key in enumerate(GROUP):
        slot = slot_of(*sources[key])
        send_to(landed.at[slot], landed.at[slot], s_part.at[n], r_part.at[n], members[key]).wait_recv()
        more_grad, more_radial = opened(landed[slot])
        sum_grad = sum_grad + more_grad
        sum_radial = sum_radial + more_radial
    gp = (sum_grad - unit_own[...] * sum_radial) / norm
    for i in range(16):
        row = (i // 8) * 16 + i % 8
        at = slice(64 * i, 64 * i + 64)
        image_gpre[at, :] = (gp[row : row + 1] / 64.0 * image_pre[at, :]).astype(BF16)
        at = slice(32 * i, 32 * i + 32)
        text_gpre[at, :] = (gp[row + 8 : row + 9] / 32.0 * text_pre[at, :]).astype(BF16)

    def compute(n):
        t = lax.rem(z + ORDER[n], NZ)
        image = jnp.dot(image_t[t], image_gpre[...], preferred_element_type=F32)
        text = jnp.dot(text_t[t], text_gpre[...], preferred_element_type=F32)
        terms[n] = jnp.where(c == 0, image, text)
        sib_out[n] = encode(jnp.where(c == 0, text, image), 16)
        start(sib_out.at[n], sib_in.at[n], s_sib.at[n], r_sib.at[n], twin)

    def chunk(n):
        send_to(sib_out.at[n], sib_in.at[n], s_sib.at[n], r_sib.at[n], twin).wait_recv()
        terms[n] += decode(sib_in[n], 16)

    def ring(step, n, h, out, inn, send_sem, recv_sem, way, early):
        value = terms[n, :, h * SUB : h * SUB + SUB]
        if step > 1 or (step == 1 and early):
            send_to(out.at[step - 1, h], inn.at[step - 1, h], send_sem.at[step - 1, h], recv_sem.at[step - 1, h], way).wait_recv()
            value = value + decode(inn[step - 1, h], 16)
        out[step, h] = encode(value, 16)
        start(out.at[step, h], inn.at[step, h], send_sem.at[step, h], recv_sem.at[step, h], way)

    def ring_step(step, n_up, n_down, begin=0, end=SUBS):
        ups, downs = list(range(UPS)), list(range(UPS, SUBS))
        if step > 0:
            ups, downs = downs + ups, ups + downs
        for i in range(begin, end):
            if i < len(ups):
                ring(step, n_up, ups[i], up_out, up_in, s_rup, r_rup, up, ups[i] < UPS)
            if i < len(downs):
                ring(step, n_down, downs[i], down_out, down_in, s_rdown, r_rdown, down, downs[i] >= UPS)

    def spread(q):
        values = []
        for n in range(4 * q, 4 * q + 4):
            values.append(terms[n, :, FAR:].reshape(2 * NY, OWN, REST))
        for i in range(2 * NY):
            wide_out[q, i] = encode(jnp.concatenate([value[i] for value in values], axis=0), 16)
        for n, (dxh, j) in enumerate(YX):
            src = wide_out.at[q, lax.rem(xh + dxh, 2) * NY + lax.rem(y + j, NY)]
            start(src, wide_in.at[q, n], s_wide.at[q, n], r_wide.at[q, n], near[(dxh, j)])

    def collect(q):
        value = decode(wide_out[q, xh * NY + y], 16)
        for n, key in enumerate(YX):
            send_to(wide_in.at[q, n], wide_in.at[q, n], s_wide.at[q, n], r_wide.at[q, n], near[key]).wait_recv()
            value = value + decode(wide_in[q, n], 16)
        for i in range(4):
            k = ORDER[4 * q + i]
            part = value[OWN * i : OWN * i + OWN]
            if k == 0:
                rest_own[...] = part
            else:
                line_out[k - 1] = encode(part, 8)
                start(line_out.at[k - 1], line_in.at[k - 1], s_line.at[k - 1], r_line.at[k - 1], z_peers[k - 1])

    old = copies[:]
    del copies[:]
    compute(0)
    compute(1)
    chunk(0)
    ring_step(0, 0, 0)
    compute(2)
    compute(3)
    for n in (1, 2):
        chunk(n)
    ring_step(1, 1, 2, 0, UPS)
    flush(old)
    chunk(3)
    spread(0)
    compute(4)
    compute(5)
    ring_step(1, 1, 2, UPS)
    compute(6)
    compute(7)
    for n in (4, 5, 6, 7):
        chunk(n)
    spread(1)
    for n, key in enumerate(GROUP):
        send_to(loss_group.at[0], loss_group.at[n + 1], s_lg.at[n], r_lg.at[n], members[key]).wait_recv()
    loss_y[0] = jnp.sum(loss_group[...], axis=0)
    for j in range(1, NY):
        start(loss_y.at[0], loss_y.at[j], s_ly.at[j - 1], r_ly.at[j - 1], y_peers[j - 1])
    ring_step(2, 3, 4)
    collect(0)
    for j in range(1, NY):
        send_to(loss_y.at[0], loss_y.at[j], s_ly.at[j - 1], r_ly.at[j - 1], y_peers[j - 1]).wait_recv()
    loss_z[0] = jnp.sum(loss_y[...], axis=0)
    for k in range(1, NZ):
        start(loss_z.at[0], loss_z.at[k], s_lz.at[k - 1], r_lz.at[k - 1], z_peers[k - 1])
    ring_step(3, 5, 6)
    collect(1)
    old = copies[:]
    del copies[:]
    for h in (0, 2, 1, 3):
        at = slice(h * SUB, h * SUB + SUB)
        value = terms[7, :, at]
        send_to(up_out.at[3, h], up_in.at[3, h], s_rup.at[3, h], r_rup.at[3, h], up).wait_recv()
        value = value + decode(up_in[3, h], 16)
        send_to(down_out.at[3, h], down_in.at[3, h], s_rdown.at[3, h], r_rdown.at[3, h], down).wait_recv()
        value = (value + decode(down_in[3, h], 16)).reshape(2 * NY, OWN, SUB)
        for i in range(2 * NY):
            near_out[i, :, at] = encode(value[i], 8)
    for n, (dxh, j) in enumerate(YX):
        src = near_out.at[lax.rem(xh + dxh, 2) * NY + lax.rem(y + j, NY)]
        start(src, near_in.at[n], s_near.at[n], r_near.at[n], near[(dxh, j)])
    flush(old)
    rest = rest_own[...]
    for k in range(1, NZ):
        send_to(line_in.at[k - 1], line_in.at[k - 1], s_line.at[k - 1], r_line.at[k - 1], z_peers[k - 1]).wait_recv()
        rest = rest + decode(line_in[k - 1], 8)
    final[c, :, FAR:] = rest
    for k in range(1, NZ):
        send_to(loss_z.at[0], loss_z.at[k], s_lz.at[k - 1], r_lz.at[k - 1], z_peers[k - 1]).wait_recv()
    loss_out_ref[...] = jnp.sum(loss_z[...], axis=0)
    result = decode(near_out[xh * NY + y], 8)
    for n, key in enumerate(YX):
        send_to(near_in.at[n], near_in.at[n], s_near.at[n], r_near.at[n], near[key]).wait_recv()
        result = result + decode(near_in[n], 8)
    final[c, :, :FAR] = result
    start(final.at[c], final.at[c], s_final, r_final, twin)
    send_to(final.at[1 - c], final.at[1 - c], s_final, r_final, twin).wait_recv()
    even = c == 0
    image_out_ref[...] = jnp.where(even, final[0, 0:12, :], final[0, 12:24, :])
    text_out_ref[...] = jnp.where(even, final[1, 0:12, :], final[1, 12:24, :])
    flush(copies)


def run_kernel(scalars, image, text, image_weight, text_weight):
    dma = pltpu.SemaphoreType.DMA
    vmem = pl.BlockSpec(memory_space=pltpu.VMEM)
    anywhere = pl.BlockSpec(memory_space=pltpu.HBM)
    image_rows, text_rows = image.shape[0], text.shape[0]
    ring = pltpu.VMEM((4, SUBS, ZROWS + 16, SUB), jnp.int16)
    tile = (8, 128)
    return pl.pallas_call(
        kernel,
        out_shape=(
            jax.ShapeDtypeStruct((12, H), F32),
            jax.ShapeDtypeStruct((12, H), F32),
            jax.ShapeDtypeStruct(tile, F32),
        ),
        in_specs=[vmem, anywhere, anywhere, anywhere, anywhere],
        out_specs=(vmem, vmem, vmem),
        scratch_shapes=[
            pltpu.VMEM((D, H), BF16),
            pltpu.VMEM((D, H), BF16),
            pltpu.VMEM((32, H), F32),
            pltpu.VMEM((2, 8, H + EXT), F32),
            pltpu.VMEM((2, 8, H + EXT), F32),
            pltpu.VMEM((4,) + tile, F32),
            pltpu.VMEM((NZ, NY, 16, LOW), BF16),
            pltpu.VMEM((NZ, NY, 16, D - LOW + EXT), BF16),
            pltpu.VMEM((8, 16, D + EXT), BF16),
            pltpu.VMEM((4, 2, 32, H + EXT), jnp.int16),
            pltpu.VMEM((8, 32, H + EXT), jnp.int16),
            pltpu.VMEM((32, H), F32),
            pltpu.VMEM((image_rows, D), BF16),
            pltpu.VMEM((text_rows, D), BF16),
            pltpu.VMEM((NZ, ZROWS, image_rows), BF16),
            pltpu.VMEM((NZ, ZROWS, text_rows), BF16),
            pltpu.VMEM((image_rows, H), F32),
            pltpu.VMEM((text_rows, H), F32),
            pltpu.VMEM((image_rows, H), BF16),
            pltpu.VMEM((text_rows, H), BF16),
            pltpu.VMEM((NZ, ZROWS, H), F32),
            pltpu.VMEM((NZ, ZROWS + 16, H), jnp.int16),
            pltpu.VMEM((NZ, ZROWS + 16, H), jnp.int16),
            ring,
            ring,
            ring,
            ring,
            pltpu.VMEM((2 * NY, 32, FAR), jnp.int16),
            pltpu.VMEM((7, 32, FAR), jnp.int16),
            pltpu.VMEM((2, 2 * NY, 112, REST), jnp.int16),
            pltpu.VMEM((2, 7, 112, REST), jnp.int16),
            pltpu.VMEM((7, 32, REST), jnp.int16),
            pltpu.VMEM((7, 32, REST), jnp.int16),
            pltpu.VMEM((OWN, REST), F32),
            pltpu.VMEM((2, OWN, H), F32),
            pltpu.VMEM((8,) + tile, F32),
            pltpu.VMEM((NY,) + tile, F32),
            pltpu.VMEM((NZ,) + tile, F32),
            dma((9,)),
        ]
        + [dma((2,))] * 2
        + [dma((3,))] * 2
        + [dma((7,))] * 2
        + [dma((3,))] * 2
        + [dma((4, 4))] * 4
        + [dma((7,))] * 2
        + [dma((NZ, 3))] * 2
        + [dma((7,))] * 2
        + [dma((8,))] * 2
        + [dma((4, SUBS))] * 4
        + [dma((7,))] * 2
        + [dma((2, 7))] * 2
        + [dma((7,))] * 2
        + [dma] * 2
        + [dma((7,))] * 2
        + [dma((3,))] * 2
        + [dma((7,))] * 2,
        compiler_params=pltpu.CompilerParams(
            collective_id=1, has_side_effects=True, vmem_limit_bytes=53 * 1024 * 1024
        ),
    )(scalars, image, text, image_weight, text_weight)


def body(
    image_tokens,
    text_tokens,
    image_weight,
    text_weight,
    logit_scale,
    logit_bias,
    loss_scale,
    valid_count,
):
    row = lax.broadcasted_iota(jnp.int32, (8, 128), 0)
    scalars = jnp.where(row == 0, valid_count[0].astype(F32), logit_scale[0])
    scalars = jnp.where(row == 2, logit_bias[0], jnp.where(row == 3, loss_scale[0], scalars))
    image_grad, text_grad, loss = run_kernel(
        scalars,
        image_tokens.reshape(-1, D),
        text_tokens.reshape(-1, D),
        image_weight,
        text_weight,
    )
    return (loss[0, 0], image_grad, text_grad)


def solution(mesh):
    placed = (
        P("dp", None, None),
        P("dp", None, None),
        P(None, "mp"),
        P(None, "mp"),
        P(),
        P(),
        P(),
        P("dp"),
    )
    return jax.shard_map(
        body,
        mesh=mesh,
        in_specs=placed,
        out_specs=(P(), P("dp", "mp"), P("dp", "mp")),
        check_vma=False,
    )
```
